512 devices in a mesh: face: 2 (over core), row: 16 (over y, z_lo), col: 16 (over z_hi, x).
Axes of the slice: x: 4, y: 4, z: 16 (z_hi: 4, z_lo: 4; z = z_hi * 4 + z_lo), core: 2. Of those that a mesh axis runs over, the one named last changes fastest.
Arguments:
- fields: bfloat16 [2, 256, 256, 128], P('face', 'row', 'col'), may hold values from -6 to 6
- conv_kernel: float32 [3, 3, 128], replicated, may hold values from -2 to 2
- conv_bias: float32 [128], replicated, may hold values from -3 to 3
- norm_gain: float32 [128], replicated, may hold values from 0.1 to 1.9
- norm_bias: float32 [128], replicated, may hold values from -3 to 3
- expand_weight: bfloat16 [128, 512], replicated, may hold values from -0.5 to 0.5
- expand_bias: float32 [512], replicated, may hold values from -3 to 3
- reduce_weight: bfloat16 [512, 128], replicated, may hold values from -0.25 to 0.25
- reduce_bias: float32 [128], replicated, may hold values from -3 to 3
- adjacency: int32 [2, 4, 3], replicated, may hold values from 0 to 3, as said below
- out_grad: bfloat16 [2, 256, 256, 128], P('face', 'row', 'col'), may hold values from -6 to 6
Outputs:
- block_out: bfloat16 [2, 256, 256, 128], P('face', 'row', 'col')
- in_grad: bfloat16 [2, 256, 256, 128], P('face', 'row', 'col')
- grad_kernel: float32 [3, 3, 128], replicated
- grad_conv_bias: float32 [128], replicated
- grad_norm_gain: float32 [128], replicated
- grad_norm_bias: float32 [128], replicated
- grad_expand_weight: float32 [128, 512], replicated
- grad_expand_bias: float32 [512], replicated
- grad_reduce_weight: float32 [512, 128], replicated
- grad_reduce_bias: float32 [128], replicated
The draws below stay inside these ranges and needn't reach their ends.
Inputs may be any that keep to these rules, and one draw needn't show every extreme that they name: adjacency[f, e] = (g, e2, r): edge e of face f (0 first row, 1 last row, 2 first column, 3 last column) is glued to edge e2 of the other face g, read in reverse order where r = 1; a row edge is always glued to a column edge and a column edge to a row edge; every edge is glued to exactly one edge, and the entry seen from that edge names it back with the same r.
All inputs are finite; a program needn't handle non-finite values.
Results may differ from the reference program's by a relative error of at most 0.007.
Values may be sent and summed in bfloat16 or wider, within the bound.
No kernel may reach another device: no remote copies, remote signals or barrier semaphores. Data moves between devices by JAX's collectives and lax.ppermute only.
A program may use at most 64 MiB of HBM per device.

```python
import math
import jax
import jax.numpy as jnp
from jax import lax

C = 128
HID = 512
NSIDE = 256
FACES = 2


def draw_adjacency(key, part):
    key = jax.random.fold_in(key, 7)
    swap_key, reversal_key = jax.random.split(key)
    flips = jax.random.randint(swap_key, (2,), 0, 2).astype(jnp.int32)
    first_flip = flips[0]
    second_flip = flips[1]
    shuffled = jnp.stack([2 + first_flip, 3 - first_flip, second_flip, 1 - second_flip]).astype(jnp.int32)
    reversal = jax.random.randint(reversal_key, (4,), 0, 2).astype(jnp.int32)
    edge_slots = jnp.arange(4, dtype=jnp.int32)
    inverse = jnp.zeros((4,), jnp.int32).at[shuffled].set(edge_slots)
    first_face = jnp.stack([jnp.ones((4,), jnp.int32), shuffled, reversal], axis=-1)
    second_face = jnp.stack([jnp.zeros((4,), jnp.int32), inverse, reversal[inverse]], axis=-1)
    glue_table = jnp.stack([first_face, second_face])
    return glue_table.reshape(FACES, 4, 3).astype(jnp.int32)


def block_scale(stream_key, extent, cuts, low, high):
    def one(position, blocks):
        steps = jax.random.uniform(jax.random.fold_in(jax.random.fold_in(stream_key, 6), position), (blocks,), jnp.float32, low / len(cuts), high / len(cuts))
        return jnp.repeat(jnp.exp(steps), extent[position] // blocks).reshape((-1,) + (1,) * (len(extent) - position - 1))

    gain = one(*cuts[0])
    for cut in cuts[1:]:
        gain = gain * one(*cut)
    return gain


def normal_values(key, shape, scale, limit, cuts=(), held_as=jnp.bfloat16):
    entries = jax.random.normal(key, shape, jnp.float32) * scale
    if len(cuts) > 0:
        entries = block_scale(key, shape, cuts, -0.22, 0.18) * entries
    return jnp.clip(entries, min=-limit, max=limit).astype(held_as)


def setup_inputs(seed: int = 0) -> dict:
    key_list = jax.random.split(jax.random.key(seed), 12)
    fields = normal_values(key_list[0], (FACES, NSIDE, NSIDE, C), 1.0, 6.0, ((0, 2), (1, 16), (2, 16)))
    conv_kernel = normal_values(key_list[1], (3, 3, C), 9 ** -0.5, 2.0, (), jnp.float32)
    conv_bias = normal_values(key_list[2], (C,), 0.5, 3.0, (), jnp.float32)
    norm_gain = jnp.clip(1.0 + 0.18 * jax.random.normal(key_list[3], (C,), jnp.float32), 0.1, 1.9)
    norm_bias = normal_values(key_list[4], (C,), 0.5, 3.0, (), jnp.float32)
    expand_weight = normal_values(key_list[5], (C, HID), C ** -0.5, 0.5)
    expand_bias = normal_values(key_list[6], (HID,), 0.5, 3.0, (), jnp.float32)
    reduce_weight = normal_values(key_list[7], (HID, C), HID ** -0.5, 0.25)
    reduce_bias = normal_values(key_list[8], (C,), 0.5, 3.0, (), jnp.float32)
    adjacency = draw_adjacency(jax.random.fold_in(key_list[11], 71), 0)
    out_grad = normal_values(key_list[10], (FACES, NSIDE, NSIDE, C), 1.0, 6.0, ((0, 2), (1, 16), (2, 16)))
    return dict(fields=fields, conv_kernel=conv_kernel, conv_bias=conv_bias, norm_gain=norm_gain, norm_bias=norm_bias, expand_weight=expand_weight, expand_bias=expand_bias, reduce_weight=reduce_weight, reduce_bias=reduce_bias, adjacency=adjacency, out_grad=out_grad)


GELU_SCALE = math.sqrt(2.0 / math.pi)
NORM_EPS = 1e-06

def gelu_pair(preact):
    cubic_term = preact + 0.044715 * preact * preact * preact
    tangent = jnp.tanh(GELU_SCALE * cubic_term)
    gelu_value = 0.5 * preact * (1.0 + tangent)
    gelu_slope = 0.5 * (1.0 + tangent) + 0.5 * preact * (1.0 - tangent * tangent) * GELU_SCALE * (1.0 + 3.0 * 0.044715 * preact * preact)
    return (gelu_value, gelu_slope)

def cell_block(mixed_cells, resid_cells, grad_cells, norm_gain, norm_bias, expand_weight, expand_bias, reduce_weight, reduce_bias):
    center = mixed_cells - lax.optimization_barrier(jnp.mean(mixed_cells, axis=-1, keepdims=True))
    inv_std = lax.rsqrt(lax.optimization_barrier(jnp.mean(center * center, axis=-1, keepdims=True)) + NORM_EPS)
    normalized = center * inv_std
    normed = (normalized * norm_gain + norm_bias).astype(jnp.bfloat16)
    preact = jnp.dot(normed, expand_weight, preferred_element_type=jnp.float32) + expand_bias
    gelu_value, gelu_slope = gelu_pair(preact)
    hidden = gelu_value.astype(jnp.bfloat16)
    block_out = (resid_cells.astype(jnp.float32) + jnp.dot(hidden, reduce_weight, preferred_element_type=jnp.float32) + reduce_bias).astype(jnp.bfloat16)
    grad_hidden = lax.dot_general(grad_cells, reduce_weight, (((1,), (1,)), ((), ())), preferred_element_type=jnp.float32)
    grad_preact = (grad_hidden * gelu_slope).astype(jnp.bfloat16)
    grad_normed = lax.dot_general(grad_preact, expand_weight, (((1,), (1,)), ((), ())), preferred_element_type=jnp.float32)
    scaled = grad_normed * norm_gain
    grad_mixed = inv_std * (scaled - lax.optimization_barrier(jnp.mean(scaled, axis=-1, keepdims=True)) - normalized * lax.optimization_barrier(jnp.mean(scaled * normalized, axis=-1, keepdims=True)))
    cell_sums = (lax.optimization_barrier(jnp.sum(grad_mixed, axis=0)), lax.optimization_barrier(jnp.sum(grad_normed * normalized, axis=0)), lax.optimization_barrier(jnp.sum(grad_normed, axis=0)), lax.dot_general(normed, grad_preact, (((0,), (0,)), ((), ())), preferred_element_type=jnp.float32), lax.optimization_barrier(jnp.sum(grad_preact.astype(jnp.float32), axis=0)), lax.dot_general(hidden, grad_cells, (((0,), (0,)), ((), ())), preferred_element_type=jnp.float32), lax.optimization_barrier(jnp.sum(grad_cells.astype(jnp.float32), axis=0)))
    return (block_out, grad_mixed, cell_sums)

def conv_rows(padded, conv_kernel, conv_bias, row_count, col_count):
    running_sum = jnp.zeros((row_count, col_count, padded.shape[2]), jnp.float32) + conv_bias
    for shift_row in range(3):
        for shift_col in range(3):
            window_cells = padded[shift_row:shift_row + row_count, shift_col:shift_col + col_count].astype(jnp.float32)
            running_sum = running_sum + conv_kernel[shift_row, shift_col] * window_cells
    return running_sum

def kernel_grad(padded, grad_mixed, row_count, col_count):
    kernel_rows = []
    for shift_row in range(3):
        kernel_cols = []
        for shift_col in range(3):
            window_cells = padded[shift_row:shift_row + row_count, shift_col:shift_col + col_count].astype(jnp.float32)
            kernel_cols.append(lax.optimization_barrier(jnp.sum(grad_mixed * window_cells, axis=(0, 1))))
        kernel_rows.append(jnp.stack(kernel_cols))
    return jnp.stack(kernel_rows)

def conv_back(grad_mixed, conv_kernel):
    row_count, col_count, channels = grad_mixed.shape
    running_sum = jnp.zeros((row_count + 2, col_count + 2, channels), jnp.float32)
    for shift_row in range(3):
        for shift_col in range(3):
            placed = jnp.pad(conv_kernel[shift_row, shift_col] * grad_mixed, ((shift_row, 2 - shift_row), (shift_col, 2 - shift_col), (0, 0)))
            running_sum = running_sum + placed
    return running_sum

def read_edges(edge_lines, adjacency, face_slot, row_offset, col_offset, first_pos, count_pos):
    line_count = edge_lines.shape[2]
    flat_lines = edge_lines.reshape(edge_lines.shape[0] * 4, line_count, edge_lines.shape[3])
    steps_along = jnp.arange(count_pos, dtype=jnp.int32) + first_pos
    result = []
    for border in range(4):
        entry_row = adjacency[face_slot, border]
        offset = col_offset if border < 2 else row_offset
        positions = steps_along + offset
        source = lax.dynamic_index_in_dim(flat_lines, entry_row[0] * 4 + entry_row[1], 0, keepdims=False)
        line_index = jnp.where(entry_row[2] == 1, line_count - 1 - positions, positions)
        inside = (positions >= 0) & (positions < line_count)
        picked = jnp.take(source, jnp.clip(line_index, 0, line_count - 1), axis=0)
        result.append(jnp.where(inside[:, None], picked, jnp.zeros_like(picked)))
    return result

def collect_edges(fields):
    return jnp.stack([fields[:, 0], fields[:, -1], fields[:, :, 0], fields[:, :, -1]], axis=1)

def reference(fields, conv_kernel, conv_bias, norm_gain, norm_bias, expand_weight, expand_bias, reduce_weight, reduce_bias, adjacency, out_grad):
    band_rows = 16
    line_x = collect_edges(fields)
    running = (jnp.zeros((3, 3, C), jnp.float32), jnp.zeros((C,), jnp.float32), jnp.zeros((C,), jnp.float32), jnp.zeros((C,), jnp.float32), jnp.zeros((C, HID), jnp.float32), jnp.zeros((HID,), jnp.float32), jnp.zeros((HID, C), jnp.float32), jnp.zeros((C,), jnp.float32))
    outputs = []
    base_grads = []
    rim_rows = []
    row_starts = jnp.arange(0, NSIDE, band_rows, dtype=jnp.int32)
    for face_slot in range(FACES):
        rim_cells = read_edges(line_x, adjacency, face_slot, 0, 0, -1, NSIDE + 2)
        padded = jnp.pad(fields[face_slot], ((1, 1), (1, 1), (0, 0)))
        padded = padded.at[0].set(rim_cells[0]).at[NSIDE + 1].set(rim_cells[1])
        padded = padded.at[:, 0].set(rim_cells[2]).at[:, NSIDE + 1].set(rim_cells[3])
        face_field = fields[face_slot]
        face_grad = out_grad[face_slot]

        def band_step(totals, row_start):
            window_rows = lax.dynamic_slice_in_dim(padded, row_start, band_rows + 2, 0)
            mixed_rows = conv_rows(window_rows, conv_kernel, conv_bias, band_rows, NSIDE)
            resid_rows = lax.dynamic_slice_in_dim(face_field, row_start, band_rows, 0)
            grad_rows = lax.dynamic_slice_in_dim(face_grad, row_start, band_rows, 0)
            block_out, grad_mixed, cell_sums = cell_block(mixed_rows.reshape(-1, C), resid_rows.reshape(-1, C), grad_rows.reshape(-1, C), norm_gain, norm_bias, expand_weight, expand_bias, reduce_weight, reduce_bias)
            grad_mixed = grad_mixed.reshape(band_rows, NSIDE, C)
            kernel_sum = kernel_grad(window_rows, grad_mixed, band_rows, NSIDE)
            band_terms = (kernel_sum,) + cell_sums
            updated = tuple((running_term + new_term for running_term, new_term in zip(totals, band_terms)))
            return (updated, (block_out.reshape(band_rows, NSIDE, C), grad_mixed))
        running, (out_bands, grad_bands) = lax.scan(band_step, running, row_starts)
        outputs.append(out_bands.reshape(NSIDE, NSIDE, C))
        grad_padded = conv_back(grad_bands.reshape(NSIDE, NSIDE, C), conv_kernel)
        base_grads.append(face_grad.astype(jnp.float32) + grad_padded[1:NSIDE + 1, 1:NSIDE + 1])
        rim_rows.append(jnp.stack([grad_padded[0, 1:NSIDE + 1], grad_padded[NSIDE + 1, 1:NSIDE + 1], grad_padded[1:NSIDE + 1, 0], grad_padded[1:NSIDE + 1, NSIDE + 1]]).astype(jnp.bfloat16))
    rim_grad = jnp.stack(rim_rows)
    in_grads = []
    for face_slot in range(FACES):
        partner_adds = read_edges(rim_grad, adjacency, face_slot, 0, 0, 0, NSIDE)
        base_grad = base_grads[face_slot]
        base_grad = base_grad.at[0].add(partner_adds[0].astype(jnp.float32))
        base_grad = base_grad.at[NSIDE - 1].add(partner_adds[1].astype(jnp.float32))
        base_grad = base_grad.at[:, 0].add(partner_adds[2].astype(jnp.float32))
        base_grad = base_grad.at[:, NSIDE - 1].add(partner_adds[3].astype(jnp.float32))
        in_grads.append(base_grad.astype(jnp.bfloat16))
    grad_totals = tuple((running_term / NSIDE for running_term in running))
    return (jnp.stack(outputs), jnp.stack(in_grads), grad_totals[0], grad_totals[1], grad_totals[2], grad_totals[3], grad_totals[4], grad_totals[5], grad_totals[6], grad_totals[7])
```

```python
import math

import jax
import jax.numpy as jnp
from jax import lax
from jax.sharding import PartitionSpec as P

GELU_SCALE = math.sqrt(2.0 / math.pi)
NORM_EPS = 1e-06
BF = jnp.bfloat16
F32 = jnp.float32


def gelu_pair(preact):
    cubic_term = preact + 0.044715 * preact * preact * preact
    tangent = jnp.tanh(GELU_SCALE * cubic_term)
    gelu_value = 0.5 * preact * (1.0 + tangent)
    gelu_slope = 0.5 * (1.0 + tangent) + 0.5 * preact * (1.0 - tangent * tangent) * GELU_SCALE * (
        1.0 + 3.0 * 0.044715 * preact * preact
    )
    return (gelu_value, gelu_slope)


def cell_block(
    mixed_cells,
    resid_cells,
    grad_cells,
    norm_gain,
    norm_bias,
    expand_weight,
    expand_bias,
    reduce_weight,
    reduce_bias,
):
    center = mixed_cells - jnp.mean(mixed_cells, axis=-1, keepdims=True)
    inv_std = lax.rsqrt(jnp.mean(center * center, axis=-1, keepdims=True) + NORM_EPS)
    normalized = center * inv_std
    normed = (normalized * norm_gain + norm_bias).astype(BF)
    preact = jnp.dot(normed, expand_weight, preferred_element_type=F32) + expand_bias
    gelu_value, gelu_slope = gelu_pair(preact)
    hidden = gelu_value.astype(BF)
    block_out = (
        resid_cells.astype(F32)
        + jnp.dot(hidden, reduce_weight, preferred_element_type=F32)
        + reduce_bias
    ).astype(BF)
    grad_hidden = lax.dot_general(
        grad_cells, reduce_weight, (((1,), (1,)), ((), ())), preferred_element_type=F32
    )
    grad_preact = (grad_hidden * gelu_slope).astype(BF)
    grad_normed = lax.dot_general(
        grad_preact, expand_weight, (((1,), (1,)), ((), ())), preferred_element_type=F32
    )
    scaled = grad_normed * norm_gain
    grad_mixed = inv_std * (
        scaled
        - jnp.mean(scaled, axis=-1, keepdims=True)
        - normalized * jnp.mean(scaled * normalized, axis=-1, keepdims=True)
    )
    cell_sums = (
        jnp.sum(grad_mixed, axis=0),
        jnp.sum(grad_normed * normalized, axis=0),
        jnp.sum(grad_normed, axis=0),
        lax.dot_general(normed, grad_preact, (((0,), (0,)), ((), ())), preferred_element_type=F32),
        jnp.sum(grad_preact.astype(F32), axis=0),
        lax.dot_general(hidden, grad_cells, (((0,), (0,)), ((), ())), preferred_element_type=F32),
        jnp.sum(grad_cells.astype(F32), axis=0),
    )
    return (block_out, grad_mixed, cell_sums)


def conv_rows(padded, conv_kernel, conv_bias, row_count, col_count):
    running_sum = jnp.zeros((row_count, col_count, padded.shape[2]), F32) + conv_bias
    for shift_row in range(3):
        for shift_col in range(3):
            window_cells = padded[
                shift_row : shift_row + row_count, shift_col : shift_col + col_count
            ].astype(F32)
            running_sum = running_sum + conv_kernel[shift_row, shift_col] * window_cells
    return running_sum


def kernel_grad(padded, grad_mixed, row_count, col_count):
    taps = []
    for shift_row in range(3):
        for shift_col in range(3):
            window_cells = padded[
                shift_row : shift_row + row_count, shift_col : shift_col + col_count
            ].astype(F32)
            taps.append(jnp.sum(grad_mixed * window_cells, axis=(0, 1)))
    return jnp.stack(taps)


def conv_back(grad_mixed, conv_kernel):
    row_count, col_count, channels = grad_mixed.shape
    running_sum = jnp.zeros((row_count + 2, col_count + 2, channels), F32)
    for shift_row in range(3):
        for shift_col in range(3):
            placed = jnp.pad(
                conv_kernel[shift_row, shift_col] * grad_mixed,
                ((shift_row, 2 - shift_row), (shift_col, 2 - shift_col), (0, 0)),
            )
            running_sum = running_sum + placed
    return running_sum


def pick(wanted, held, cells):
    chosen = (wanted[:, None] == held[None, :]).astype(BF)
    return jnp.dot(chosen, cells, preferred_element_type=F32).astype(BF)


def swap(slots, axes):
    return lax.all_to_all(slots, axes, 0, 0)


def at(slots, index):
    return lax.dynamic_index_in_dim(slots, index, 0, keepdims=False)


def on_device(
    fields,
    conv_kernel,
    conv_bias,
    norm_gain,
    norm_bias,
    expand_weight,
    expand_bias,
    reduce_weight,
    reduce_bias,
    adjacency,
    out_grad,
):
    tile = fields[0]
    cells = tile.shape[0]
    channels = tile.shape[2]
    hid = expand_weight.shape[1]
    side = lax.axis_size("row")
    width = side * cells
    lanes = ("face", "row")
    f = lax.axis_index("face")
    r = lax.axis_index("row")
    c = lax.axis_index("col")
    last = side - 1
    base = f * side
    other = (1 - f) * side
    up, down = base + jnp.maximum(r - 1, 0), base + jnp.minimum(r + 1, last)
    west_of, east_of = jnp.maximum(c - 1, 0), jnp.minimum(c + 1, last)

    slot = jnp.arange(2 * side)
    first = jnp.where(slot // side == f, slot % side < r, r == 0)[:, None, None]
    column = jnp.arange(side)
    adjacent = (jnp.abs(column - c) == 1)[:, None, None]
    lower = (column < c)[:, None, None]
    at_first, at_last = (column == 0)[:, None, None], (column == last)[:, None, None]
    edge_col = (c == 0) | (c == last)

    row_entry = jnp.where(r == 0, adjacency[f, 0], adjacency[f, 1])
    row_source = jnp.where(row_entry[1] == 2, 0, last)
    west_entry, east_entry = adjacency[f, 2], adjacency[f, 3]

    def turned(position, entry):
        return jnp.where(entry[2] == 1, width - 1 - position, position)

    def column_parts(halo_low, halo_high, row_windows, west_window, east_window):
        near = jnp.where(adjacent, jnp.where(lower, halo_low, halo_high), row_windows)
        far = jnp.where(at_first, west_window, jnp.where(at_last, east_window, row_windows))
        return near, far

    wide = jnp.arange(cells + 2) - 1
    thin = jnp.arange(cells)

    sent = jnp.concatenate(
        [
            jnp.where(first, tile[0], tile[cells - 1]),
            jnp.broadcast_to(
                jnp.where(c == 0, tile[:, 0], tile[:, cells - 1]), (2 * side, cells, channels)
            ),
        ],
        axis=1,
    )
    got = swap(sent, lanes)
    north, south = at(got, up)[:cells], at(got, down)[:cells]
    line = lax.dynamic_slice_in_dim(got, other, side, 0)[:, cells:].reshape(width, channels)
    ends = (at(got, other)[:cells], at(got, other + last)[:cells])

    row_wanted = turned((column[:, None] * cells + wide[None, :]).reshape(-1), row_entry)
    row_windows = pick(row_wanted, jnp.arange(width), line).reshape(side, cells + 2, channels)
    side_windows = []
    for entry in (west_entry, east_entry):
        strip = jnp.where(entry[1] == 0, ends[0], ends[1])
        side_windows.append(pick(turned(r * cells + wide, entry), c * cells + thin, strip))
    near, far = column_parts(
        jnp.concatenate([north[:1], tile[:, 0], south[:1]]),
        jnp.concatenate([north[cells - 1 :], tile[:, cells - 1], south[cells - 1 :]]),
        row_windows,
        side_windows[0],
        side_windows[1],
    )
    rim = cells + 2
    got = swap(jnp.concatenate([near, far], axis=1), "col")
    rim_col = jnp.sum(got[:, rim:].astype(F32), axis=0).astype(BF)
    from_source = at(got, row_source)
    rim_row = jnp.where(edge_col, from_source[:rim], from_source[rim:])
    west = jnp.where(c == 0, rim_col, at(got, west_of)[:rim])
    east = jnp.where(c == last, rim_col, at(got, east_of)[:rim])
    top = jnp.where(r == 0, rim_row, jnp.concatenate([west[:1], north, east[:1]]))
    bottom = jnp.where(r == last, rim_row, jnp.concatenate([west[rim - 1 :], south, east[rim - 1 :]]))
    padded = jnp.concatenate(
        [
            top[None],
            jnp.concatenate([west[1:-1, None], tile, east[1:-1, None]], axis=1),
            bottom[None],
        ]
    )

    mixed = conv_rows(padded, conv_kernel, conv_bias, cells, cells)
    block_out, grad_mixed, cell_sums = cell_block(
        mixed.reshape(cells * cells, channels),
        tile.reshape(cells * cells, channels),
        out_grad[0].reshape(cells * cells, channels),
        norm_gain,
        norm_bias,
        expand_weight,
        expand_bias,
        reduce_weight,
        reduce_bias,
    )
    grad_mixed = grad_mixed.reshape(cells, cells, channels)
    bias_sum, gain_sum, shift_sum, expand_sum, expand_bias_sum, reduce_sum, reduce_bias_sum = (
        cell_sums
    )
    blocks = hid // channels
    weight_sums = jnp.concatenate(
        [expand_sum[:, k * channels : (k + 1) * channels] for k in range(blocks)] + [reduce_sum]
    )
    small_sums = jnp.concatenate(
        [
            kernel_grad(padded, grad_mixed, cells, cells),
            bias_sum[None],
            gain_sum[None],
            shift_sum[None],
            expand_bias_sum.reshape(blocks, channels),
            reduce_bias_sum[None],
        ]
    )
    small_count = small_sums.shape[0]
    few = -(-small_count // (2 * side))
    small_sums = jnp.pad(small_sums, ((0, 2 * side * few - small_count), (0, 0)))
    many = weight_sums.shape[0] // (2 * side)
    sums = many + 2 * few

    def packed(weights, small):
        high = small.astype(BF)
        low = (small - high.astype(F32)).astype(BF)
        return jnp.concatenate([weights.astype(BF), high, low], axis=-2)

    def unpacked(part):
        small = part[..., many : many + few, :].astype(F32) + part[..., many + few : sums, :].astype(F32)
        return part[..., :many, :].astype(F32), small

    grad_padded = conv_back(grad_mixed, conv_kernel)
    rims = grad_padded.astype(BF)
    sent = jnp.concatenate(
        [
            packed(
                weight_sums.reshape(2 * side, many, channels),
                small_sums.reshape(2 * side, few, channels),
            ),
            jnp.where(first, rims[0], rims[rim - 1]),
            jnp.broadcast_to(
                jnp.where(c == 0, rims[:, 0], rims[:, rim - 1]), (2 * side, rim, channels)
            ),
        ],
        axis=1,
    )
    got = swap(sent, lanes)
    weights, small = unpacked(got)
    weights, small = jnp.sum(weights, axis=0), jnp.sum(small, axis=0)
    north = jnp.where(r == 0, 0, at(got, up)[sums : sums + rim].astype(F32))
    south = jnp.where(r == last, 0, at(got, down)[sums : sums + rim].astype(F32))
    line = lax.dynamic_slice_in_dim(got, other, side, 0)[:, sums + rim :].reshape(side * rim, channels)
    ends = (at(got, other)[sums : sums + rim], at(got, other + last)[sums : sums + rim])

    row_wanted = turned(jnp.arange(width), row_entry)
    held = (column[:, None] * cells + wide[None, :]).reshape(-1)
    row_windows = pick(row_wanted, held, line).reshape(side, cells, channels)
    side_windows = []
    for entry in (west_entry, east_entry):
        strip = jnp.where(entry[1] == 0, ends[0], ends[1])
        side_windows.append(pick(turned(r * cells + thin, entry), c * cells + wide, strip))

    def folded(col):
        whole = grad_padded[1:-1, col]
        return jnp.concatenate(
            [whole[:1] + north[col][None], whole[1:-1], whole[-1:] + south[col][None]]
        ).astype(BF)

    near, far = column_parts(
        folded(0), folded(rim - 1), row_windows, side_windows[0], side_windows[1]
    )
    sent = jnp.concatenate(
        [jnp.broadcast_to(packed(weights, small), (side, sums, channels)), near, far], axis=1
    )
    got = swap(sent, "col")
    weights, small = unpacked(got)
    weights, small = jnp.sum(weights, axis=0) / width, jnp.sum(small, axis=0) / width
    spread = swap(jnp.broadcast_to(packed(weights, small), (2 * side, sums, channels)), lanes)

    near, far = got[:, sums : sums + cells], got[:, sums + cells :]
    rim_col = jnp.sum(far.astype(F32), axis=0)
    rim_row = jnp.where(edge_col, at(near, row_source), at(far, row_source)).astype(F32)
    west = jnp.where(c == 0, rim_col, at(near, west_of).astype(F32))
    east = jnp.where(c == last, rim_col, at(near, east_of).astype(F32))
    north = jnp.where(r == 0, rim_row, north[1:-1])
    south = jnp.where(r == last, rim_row, south[1:-1])
    in_grad = out_grad[0].astype(F32) + grad_padded[1:-1, 1:-1]
    in_grad = in_grad + jnp.pad(north[None], ((0, cells - 1), (0, 0), (0, 0)))
    in_grad = in_grad + jnp.pad(south[None], ((cells - 1, 0), (0, 0), (0, 0)))
    in_grad = in_grad + jnp.pad(west[:, None], ((0, 0), (0, cells - 1), (0, 0)))
    in_grad = in_grad + jnp.pad(east[:, None], ((0, 0), (cells - 1, 0), (0, 0)))

    weights, small = unpacked(spread)
    weights = weights.reshape(-1, channels)
    small = small.reshape(-1, channels)
    return (
        block_out.reshape(1, cells, cells, channels),
        in_grad.astype(BF)[None],
        small[:9].reshape(3, 3, channels),
        small[9],
        small[10],
        small[11],
        jnp.concatenate([weights[k * channels : (k + 1) * channels] for k in range(blocks)], axis=1),
        small[12 : 12 + blocks].reshape(hid),
        weights[hid:],
        small[12 + blocks],
    )


def solution(mesh):
    tiles = P("face", "row", "col", None)
    in_specs = (tiles,) + (P(),) * 9 + (tiles,)
    out_specs = (tiles, tiles) + (P(),) * 8
    return jax.shard_map(
        on_device, mesh=mesh, in_specs=in_specs, out_specs=out_specs, check_vma=False
    )
```

```python
import math

import jax
import jax.numpy as jnp
from jax import lax
from jax.experimental import pallas as pl
from jax.experimental.pallas import tpu as pltpu
from jax.sharding import PartitionSpec as P

GELU_SCALE = math.sqrt(2.0 / math.pi)
NORM_EPS = 1e-06
BF = jnp.bfloat16
F32 = jnp.float32


def gelu_pair(preact):
    cubic_term = preact + 0.044715 * preact * preact * preact
    tangent = jnp.tanh(GELU_SCALE * cubic_term)
    gelu_value = 0.5 * preact * (1.0 + tangent)
    gelu_slope = 0.5 * (1.0 + tangent) + 0.5 * preact * (1.0 - tangent * tangent) * GELU_SCALE * (
        1.0 + 3.0 * 0.044715 * preact * preact
    )
    return (gelu_value, gelu_slope)


def block_kernel(
    plan_ref,
    padded_ref,
    tile_ref,
    grad_ref,
    tap_ref,
    conv_bias_ref,
    gain_ref,
    shift_ref,
    expand_ref,
    expand_bias_ref,
    reduce_ref,
    reduce_bias_ref,
    out_ref,
    sent_ref,
    base_ref,
    cols_ref,
    wide_ref,
):
    rows, columns, channels = tile_ref.shape
    count = rows * columns
    rim = rows + 2
    hid = expand_ref.shape[1]
    slots, _, _ = sent_ref.shape
    side = slots // 2
    padded = padded_ref[...].astype(F32)
    shifted = [padded[:, b : b + columns] for b in range(3)]

    mixed = jnp.zeros((rows, columns, channels), F32) + conv_bias_ref[...].reshape(1, 1, channels)
    for a in range(3):
        for b in range(3):
            mixed = mixed + tap_ref[3 * a + b].reshape(1, 1, channels) * shifted[b][a : a + rows]
    mixed = mixed.reshape(count, channels)
    center = mixed - jnp.mean(mixed, axis=-1, keepdims=True)
    inv_std = lax.rsqrt(jnp.mean(center * center, axis=-1, keepdims=True) + NORM_EPS)
    normalized = center * inv_std
    normed = (normalized * gain_ref[...] + shift_ref[...]).astype(BF)
    preact = jnp.dot(normed, expand_ref[...], preferred_element_type=F32) + expand_bias_ref[...]
    gelu_value, gelu_slope = gelu_pair(preact)
    hidden = gelu_value.astype(BF)
    grad_cells = grad_ref[...].reshape(count, channels)
    grad_hidden = lax.dot_general(
        grad_cells, reduce_ref[...], (((1,), (1,)), ((), ())), preferred_element_type=F32
    )
    grad_preact = (grad_hidden * gelu_slope).astype(BF)
    grad_normed = lax.dot_general(
        grad_preact, expand_ref[...], (((1,), (1,)), ((), ())), preferred_element_type=F32
    )
    scaled = grad_normed * gain_ref[...]
    grad_mixed = inv_std * (
        scaled
        - jnp.mean(scaled, axis=-1, keepdims=True)
        - normalized * jnp.mean(scaled * normalized, axis=-1, keepdims=True)
    )
    out = tile_ref[...].reshape(count, channels).astype(F32)
    out = out + jnp.dot(hidden, reduce_ref[...], preferred_element_type=F32) + reduce_bias_ref[...]
    out_ref[...] = out.astype(BF).reshape(rows, columns, channels)

    def total(cells):
        return jnp.sum(cells, axis=0, keepdims=True)

    square = grad_mixed.reshape(rows, columns, channels)
    small = [
        total((square * shifted[b][a : a + rows]).reshape(count, channels))
        for a in range(3)
        for b in range(3)
    ]
    small += [total(grad_mixed), total(grad_normed * normalized), total(grad_normed)]
    preact_total = total(grad_preact.astype(F32))
    small += [preact_total[:, k : k + channels] for k in range(0, hid, channels)]
    small += [total(grad_cells.astype(F32))]

    across = (((0,), (0,)), ((), ()))
    expand_sum = lax.dot_general(normed, grad_preact, across, preferred_element_type=F32).astype(BF)
    reduce_sum = lax.dot_general(hidden, grad_cells, across, preferred_element_type=F32).astype(BF)
    many = 2 * hid // slots
    for k in range(0, hid, channels):
        for j in range(0, channels, many):
            sent_ref[(k + j) // many, 0:many] = expand_sum[j : j + many, k : k + channels]
    for k in range(0, hid, many):
        sent_ref[(hid + k) // many, 0:many] = reduce_sum[k : k + many]

    wide_ref[...] = jnp.zeros(wide_ref.shape, F32)
    for b in range(3):
        parts = [tap_ref[3 * a + b].reshape(1, 1, channels) * square for a in range(3)]
        wide_ref[0, b : b + columns] += parts[0][0]
        wide_ref[1, b : b + columns] += parts[0][1] + parts[1][0]
        wide_ref[2:rows, b : b + columns] += (
            parts[0][2:] + parts[1][1 : rows - 1] + parts[2][: rows - 2]
        )
        wide_ref[rows, b : b + columns] += parts[1][rows - 1] + parts[2][rows - 2]
        wide_ref[rows + 1, b : b + columns] += parts[2][rows - 1]
    base_ref[...] = grad_ref[...].astype(F32) + wide_ref[1 : rows + 1, 1 : columns + 1]
    west = jnp.concatenate([wide_ref[k, 0:1] for k in range(rim)])
    east = jnp.concatenate([wide_ref[k, rim - 1 : rim] for k in range(rim)])
    cols_ref[0] = west[1 : rim - 1]
    cols_ref[1] = east[1 : rim - 1]
    north = wide_ref[0, 0:rim]
    south = wide_ref[rim - 1, 0:rim]

    face, row, col = plan_ref[0], plan_ref[1], plan_ref[2]
    few = -(-len(small) // slots)
    extra = sent_ref.shape[1] - many - 2 * rows
    side_strip = jnp.where(col == 0, west, east)
    side_cells = side_strip[1 : rim - 1].astype(BF)
    place = lax.broadcasted_iota(jnp.int32, (extra, channels), 0)
    near = many + rows
    for slot in range(slots):
        first = jnp.where(face == slot // side, slot % side < row, row == 0)
        strip = jnp.where(first, north, south)
        sent_ref[slot, many:near] = strip[1 : rim - 1].astype(BF)
        sent_ref[slot, near : near + rows] = side_cells
        ends = [strip[0:1], strip[rim - 1 : rim], side_strip[0:1], side_strip[rim - 1 : rim]]
        values = ends
        for k in range(few * slot, min(few * slot + few, len(small))):
            high = small[k].astype(BF).astype(F32)
            values = values + [high, small[k] - high]
        block = jnp.zeros((extra, channels), F32)
        for k, value in enumerate(values):
            block = jnp.where(place == k, value, block)
        sent_ref[slot, near + rows : near + rows + extra] = block.astype(BF)


def block_on_tile(plan, padded, tile, grad, taps, *params):
    rows, columns, channels = tile.shape
    slots, depth = params[-2:]
    return pl.pallas_call(
        block_kernel,
        out_shape=(
            jax.ShapeDtypeStruct(tile.shape, BF),
            jax.ShapeDtypeStruct((slots, depth, channels), BF),
            jax.ShapeDtypeStruct(tile.shape, F32),
            jax.ShapeDtypeStruct((2, rows, channels), F32),
        ),
        in_specs=[pl.BlockSpec(memory_space=pltpu.SMEM)]
        + [pl.BlockSpec(memory_space=pltpu.VMEM)] * 11,
        out_specs=(pl.BlockSpec(memory_space=pltpu.VMEM),) * 4,
        scratch_shapes=[pltpu.VMEM((rows + 2, columns + 8, channels), F32)],
        compiler_params=pltpu.CompilerParams(vmem_limit_bytes=24 * 1024 * 1024),
        name="block",
    )(plan, padded, tile, grad, taps, *params[:-2])


def finish_kernel(got_ref, *out_refs):
    tap_ref, bias_ref, gain_ref, shift_ref, expand_ref, expand_bias_ref, reduce_ref, reduce_bias_ref = (
        out_refs
    )
    slots, depth, channels = got_ref.shape
    hid = reduce_ref.shape[0]
    many = 2 * hid // slots
    for k in range(0, hid, channels):
        for j in range(0, channels, many):
            expand_ref[j : j + many, k : k + channels] = got_ref[(k + j) // many, 0:many].astype(F32)
    for k in range(0, hid, many):
        reduce_ref[k : k + many] = got_ref[(hid + k) // many, 0:many].astype(F32)
    blocks = hid // channels
    few = -(-(13 + blocks) // slots)
    small = []
    for slot in range(slots):
        rest = got_ref[slot, many:depth].astype(F32)
        small += [rest[2 * k : 2 * k + 1] + rest[2 * k + 1 : 2 * k + 2] for k in range(few)]
    for k in range(9):
        tap_ref[k : k + 1] = small[k]
    bias_ref[...] = small[9]
    gain_ref[...] = small[10]
    shift_ref[...] = small[11]
    for k in range(blocks):
        expand_bias_ref[:, k * channels : (k + 1) * channels] = small[12 + k]
    reduce_bias_ref[...] = small[12 + blocks]


def finish(got, hid):
    channels = got.shape[2]
    shapes = [(9, channels)] + [(1, channels)] * 3
    shapes += [(channels, hid), (1, hid), (hid, channels), (1, channels)]
    return pl.pallas_call(
        finish_kernel,
        out_shape=tuple(jax.ShapeDtypeStruct(shape, F32) for shape in shapes),
        in_specs=[pl.BlockSpec(memory_space=pltpu.VMEM)],
        out_specs=(pl.BlockSpec(memory_space=pltpu.VMEM),) * len(shapes),
        compiler_params=pltpu.CompilerParams(vmem_limit_bytes=16 * 1024 * 1024),
        name="finish",
    )(got)


def pick(wanted, held, cells):
    chosen = (wanted[:, None] == held[None, :]).astype(BF)
    return jnp.dot(chosen, cells, preferred_element_type=F32).astype(BF)


def swap(slots, axes):
    return lax.all_to_all(slots, axes, 0, 0)


def at(slots, index):
    return lax.dynamic_index_in_dim(slots, index, 0, keepdims=False)


def on_device(
    fields,
    conv_kernel,
    conv_bias,
    norm_gain,
    norm_bias,
    expand_weight,
    expand_bias,
    reduce_weight,
    reduce_bias,
    adjacency,
    out_grad,
):
    tile = fields[0]
    cells = tile.shape[0]
    channels = tile.shape[2]
    hid = expand_weight.shape[1]
    side = lax.axis_size("row")
    width = side * cells
    lanes = ("face", "row")
    f = lax.axis_index("face")
    r = lax.axis_index("row")
    c = lax.axis_index("col")
    last = side - 1
    base = f * side
    other = (1 - f) * side
    up, down = base + jnp.maximum(r - 1, 0), base + jnp.minimum(r + 1, last)
    west_of, east_of = jnp.maximum(c - 1, 0), jnp.minimum(c + 1, last)

    slot = jnp.arange(2 * side)
    first = jnp.where(slot // side == f, slot % side < r, r == 0)[:, None, None]
    column = jnp.arange(side)
    adjacent = (jnp.abs(column - c) == 1)[:, None, None]
    lower = (column < c)[:, None, None]
    at_first, at_last = (column == 0)[:, None, None], (column == last)[:, None, None]
    edge_col = (c == 0) | (c == last)

    row_entry = jnp.where(r == 0, adjacency[f, 0], adjacency[f, 1])
    row_source = jnp.where(row_entry[1] == 2, 0, last)
    west_entry, east_entry = adjacency[f, 2], adjacency[f, 3]

    def turned(position, entry):
        return jnp.where(entry[2] == 1, width - 1 - position, position)

    def column_parts(halo_low, halo_high, row_windows, west_window, east_window):
        near = jnp.where(adjacent, jnp.where(lower, halo_low, halo_high), row_windows)
        far = jnp.where(at_first, west_window, jnp.where(at_last, east_window, row_windows))
        return near, far

    wide = jnp.arange(cells + 2) - 1
    thin = jnp.arange(cells)

    sent = jnp.concatenate(
        [
            jnp.where(first, tile[0], tile[cells - 1]),
            jnp.broadcast_to(
                jnp.where(c == 0, tile[:, 0], tile[:, cells - 1]), (2 * side, cells, channels)
            ),
        ],
        axis=1,
    )
    got = swap(sent, lanes)
    north, south = at(got, up)[:cells], at(got, down)[:cells]
    line = lax.dynamic_slice_in_dim(got, other, side, 0)[:, cells:].reshape(width, channels)
    ends = (at(got, other)[:cells], at(got, other + last)[:cells])

    row_wanted = turned((column[:, None] * cells + wide[None, :]).reshape(-1), row_entry)
    row_windows = pick(row_wanted, jnp.arange(width), line).reshape(side, cells + 2, channels)
    side_windows = []
    for entry in (west_entry, east_entry):
        strip = jnp.where(entry[1] == 0, ends[0], ends[1])
        side_windows.append(pick(turned(r * cells + wide, entry), c * cells + thin, strip))
    near, far = column_parts(
        jnp.concatenate([north[:1], tile[:, 0], south[:1]]),
        jnp.concatenate([north[cells - 1 :], tile[:, cells - 1], south[cells - 1 :]]),
        row_windows,
        side_windows[0],
        side_windows[1],
    )
    rim = cells + 2
    got = swap(jnp.concatenate([near, far], axis=1), "col")
    rim_col = jnp.sum(got[:, rim:].astype(F32), axis=0).astype(BF)
    from_source = at(got, row_source)
    rim_row = jnp.where(edge_col, from_source[:rim], from_source[rim:])
    west = jnp.where(c == 0, rim_col, at(got, west_of)[:rim])
    east = jnp.where(c == last, rim_col, at(got, east_of)[:rim])
    top = jnp.where(r == 0, rim_row, jnp.concatenate([west[:1], north, east[:1]]))
    bottom = jnp.where(r == last, rim_row, jnp.concatenate([west[rim - 1 :], south, east[rim - 1 :]]))
    padded = jnp.concatenate(
        [
            top[None],
            jnp.concatenate([west[1:-1, None], tile, east[1:-1, None]], axis=1),
            bottom[None],
        ]
    )

    small_count = 13 + hid // channels
    many = 2 * hid // (2 * side)
    few = -(-small_count // (2 * side))
    extra = -(-(2 * few + 4) // 8) * 8
    block_out, sent, base_grad, edge_cols = block_on_tile(
        jnp.stack([f, r, c]).astype(jnp.int32),
        padded,
        tile,
        out_grad[0],
        conv_kernel.reshape(9, channels),
        conv_bias.reshape(1, channels),
        norm_gain.reshape(1, channels),
        norm_bias.reshape(1, channels),
        expand_weight,
        expand_bias.reshape(1, hid),
        reduce_weight,
        reduce_bias.reshape(1, channels),
        2 * side,
        many + 2 * cells + extra,
    )
    got = swap(sent, lanes)
    near_at, far_at, rest_at = many, many + cells, many + 2 * cells

    def packed(small):
        high = small.astype(BF)
        low = (small - high.astype(F32)).astype(BF)
        pairs = jnp.stack([high, low], axis=-2).reshape(2 * few, channels)
        return jnp.pad(pairs, ((0, 8 * (-(-few // 4)) - 2 * few), (0, 0)))

    def small_total(rest):
        pairs = jnp.sum(rest.astype(F32), axis=0).reshape(few, 2, channels)
        return pairs[:, 0] + pairs[:, 1]

    weights = jnp.sum(got[:, :many].astype(F32), axis=0)
    small = small_total(got[:, rest_at + 4 : rest_at + 4 + 2 * few])

    def strip(part, main, spare):
        return jnp.concatenate(
            [
                part[..., rest_at + spare : rest_at + spare + 1, :],
                part[..., main : main + cells, :],
                part[..., rest_at + spare + 1 : rest_at + spare + 2, :],
            ],
            axis=-2,
        )

    north = jnp.where(r == 0, 0, strip(at(got, up), near_at, 0).astype(F32))
    south = jnp.where(r == last, 0, strip(at(got, down), near_at, 0).astype(F32))
    line = strip(lax.dynamic_slice_in_dim(got, other, side, 0), far_at, 2).reshape(
        side * rim, channels
    )
    ends = (strip(at(got, other), near_at, 0), strip(at(got, other + last), near_at, 0))

    row_wanted = turned(jnp.arange(width), row_entry)
    held = (column[:, None] * cells + wide[None, :]).reshape(-1)
    row_windows = pick(row_wanted, held, line).reshape(side, cells, channels)
    side_windows = []
    for entry in (west_entry, east_entry):
        strip = jnp.where(entry[1] == 0, ends[0], ends[1])
        side_windows.append(pick(turned(r * cells + thin, entry), c * cells + wide, strip))

    def folded(end, col):
        whole = edge_cols[end]
        return jnp.concatenate(
            [whole[:1] + north[col][None], whole[1:-1], whole[-1:] + south[col][None]]
        ).astype(BF)

    near, far = column_parts(
        folded(0, 0), folded(1, rim - 1), row_windows, side_windows[0], side_windows[1]
    )
    rest = packed(small)
    sent = jnp.concatenate(
        [
            jnp.broadcast_to(weights.astype(BF), (side, many, channels)),
            near,
            far,
            jnp.broadcast_to(rest, (side,) + rest.shape),
        ],
        axis=1,
    )
    got = swap(sent, "col")
    weights = jnp.sum(got[:, :many].astype(F32), axis=0) / width
    small = small_total(got[:, rest_at : rest_at + 2 * few]) / width
    share = jnp.concatenate([weights.astype(BF), packed(small)])
    spread = swap(jnp.broadcast_to(share, (2 * side,) + share.shape), lanes)

    near, far = got[:, near_at:far_at], got[:, far_at:rest_at]
    rim_col = jnp.sum(far.astype(F32), axis=0)
    rim_row = jnp.where(edge_col, at(near, row_source), at(far, row_source)).astype(F32)
    west = jnp.where(c == 0, rim_col, at(near, west_of).astype(F32))
    east = jnp.where(c == last, rim_col, at(near, east_of).astype(F32))
    north = jnp.where(r == 0, rim_row, north[1:-1])
    south = jnp.where(r == last, rim_row, south[1:-1])
    in_grad = base_grad
    in_grad = in_grad + jnp.pad(north[None], ((0, cells - 1), (0, 0), (0, 0)))
    in_grad = in_grad + jnp.pad(south[None], ((cells - 1, 0), (0, 0), (0, 0)))
    in_grad = in_grad + jnp.pad(west[:, None], ((0, 0), (0, cells - 1), (0, 0)))
    in_grad = in_grad + jnp.pad(east[:, None], ((0, 0), (cells - 1, 0), (0, 0)))

    taps, bias, gain, shift, expand, expand_vector, reduce, reduce_vector = finish(spread, hid)
    return (
        block_out[None],
        in_grad.astype(BF)[None],
        taps.reshape(3, 3, channels),
        bias.reshape(channels),
        gain.reshape(channels),
        shift.reshape(channels),
        expand,
        expand_vector.reshape(hid),
        reduce,
        reduce_vector.reshape(channels),
    )


def solution(mesh):
    tiles = P("face", "row", "col", None)
    in_specs = (tiles,) + (P(),) * 9 + (tiles,)
    out_specs = (tiles, tiles) + (P(),) * 8
    return jax.shard_map(
        on_device, mesh=mesh, in_specs=in_specs, out_specs=out_specs, check_vma=False
    )
```

```python
import math

import jax
import jax.numpy as jnp
from jax import lax
from jax.experimental import pallas as pl
from jax.experimental.pallas import tpu as pltpu
from jax.sharding import PartitionSpec as P

GELU_SCALE = math.sqrt(2.0 / math.pi)
NORM_EPS = 1e-06
BF = jnp.bfloat16
F32 = jnp.float32


def gelu_pair(preact):
    cubic_term = preact + 0.044715 * preact * preact * preact
    tangent = jnp.tanh(GELU_SCALE * cubic_term)
    gelu_value = 0.5 * preact * (1.0 + tangent)
    gelu_slope = 0.5 * (1.0 + tangent) + 0.5 * preact * (1.0 - tangent * tangent) * GELU_SCALE * (
        1.0 + 3.0 * 0.044715 * preact * preact
    )
    return (gelu_value, gelu_slope)


def block_kernel(
    plan_ref,
    padded_ref,
    tile_ref,
    grad_ref,
    tap_ref,
    conv_bias_ref,
    gain_ref,
    shift_ref,
    expand_ref,
    expand_bias_ref,
    reduce_ref,
    reduce_bias_ref,
    out_ref,
    sent_ref,
    base_ref,
    wide_ref,
):
    rows, columns, channels = tile_ref.shape
    count = rows * columns
    rim = rows + 2
    hid = expand_ref.shape[1]
    slots, _, _ = sent_ref.shape
    side = slots // 2
    padded = padded_ref[...].astype(F32)
    shifted = [padded[:, b : b + columns] for b in range(3)]

    mixed = jnp.zeros((rows, columns, channels), F32) + conv_bias_ref[...].reshape(1, 1, channels)
    for a in range(3):
        for b in range(3):
            mixed = mixed + tap_ref[3 * a + b].reshape(1, 1, channels) * shifted[b][a : a + rows]
    mixed = mixed.reshape(count, channels)
    center = mixed - jnp.mean(mixed, axis=-1, keepdims=True)
    inv_std = lax.rsqrt(jnp.mean(center * center, axis=-1, keepdims=True) + NORM_EPS)
    normalized = center * inv_std
    normed = (normalized * gain_ref[...] + shift_ref[...]).astype(BF)
    preact = jnp.dot(normed, expand_ref[...], preferred_element_type=F32) + expand_bias_ref[...]
    gelu_value, gelu_slope = gelu_pair(preact)
    hidden = gelu_value.astype(BF)
    grad_cells = grad_ref[...].reshape(count, channels)
    grad_hidden = lax.dot_general(
        grad_cells, reduce_ref[...], (((1,), (1,)), ((), ())), preferred_element_type=F32
    )
    grad_preact = (grad_hidden * gelu_slope).astype(BF)
    grad_normed = lax.dot_general(
        grad_preact, expand_ref[...], (((1,), (1,)), ((), ())), preferred_element_type=F32
    )
    scaled = grad_normed * gain_ref[...]
    grad_mixed = inv_std * (
        scaled
        - jnp.mean(scaled, axis=-1, keepdims=True)
        - normalized * jnp.mean(scaled * normalized, axis=-1, keepdims=True)
    )
    out = tile_ref[...].reshape(count, channels).astype(F32)
    out = out + jnp.dot(hidden, reduce_ref[...], preferred_element_type=F32) + reduce_bias_ref[...]
    out_ref[...] = out.astype(BF).reshape(rows, columns, channels)

    def total(cells):
        return jnp.sum(cells, axis=0, keepdims=True)

    square = grad_mixed.reshape(rows, columns, channels)
    small = [
        total((square * shifted[b][a : a + rows]).reshape(count, channels))
        for a in range(3)
        for b in range(3)
    ]
    small += [total(grad_mixed), total(grad_normed * normalized), total(grad_normed)]
    preact_total = total(grad_preact.astype(F32))
    small += [preact_total[:, k : k + channels] for k in range(0, hid, channels)]
    small += [total(grad_cells.astype(F32))]

    across = (((0,), (0,)), ((), ()))
    expand_sum = lax.dot_general(normed, grad_preact, across, preferred_element_type=F32).astype(BF)
    reduce_sum = lax.dot_general(hidden, grad_cells, across, preferred_element_type=F32).astype(BF)
    many = 2 * hid // slots
    for k in range(0, hid, channels):
        for j in range(0, channels, many):
            sent_ref[(k + j) // many, 0:many] = expand_sum[j : j + many, k : k + channels]
    for k in range(0, hid, many):
        sent_ref[(hid + k) // many, 0:many] = reduce_sum[k : k + many]

    wide_ref[...] = jnp.zeros(wide_ref.shape, F32)
    for b in range(3):
        parts = [tap_ref[3 * a + b].reshape(1, 1, channels) * square for a in range(3)]
        wide_ref[0, b : b + columns] += parts[0][0]
        wide_ref[1, b : b + columns] += parts[0][1] + parts[1][0]
        wide_ref[2:rows, b : b + columns] += (
            parts[0][2:] + parts[1][1 : rows - 1] + parts[2][: rows - 2]
        )
        wide_ref[rows, b : b + columns] += parts[1][rows - 1] + parts[2][rows - 2]
        wide_ref[rows + 1, b : b + columns] += parts[2][rows - 1]
    base_ref[...] = grad_ref[...].astype(F32) + wide_ref[1 : rows + 1, 1 : columns + 1]
    west = jnp.concatenate([wide_ref[k, 0:1] for k in range(rim)])
    east = jnp.concatenate([wide_ref[k, rim - 1 : rim] for k in range(rim)])
    north = wide_ref[0, 0:rim]
    south = wide_ref[rim - 1, 0:rim]

    face, row, col = plan_ref[0], plan_ref[1], plan_ref[2]
    cut = math.isqrt(side)
    here_y, here_x = row // cut, col % cut
    few = -(-len(small) // slots)
    extra = sent_ref.shape[1] - many - 2 * rows
    place = lax.broadcasted_iota(jnp.int32, (extra, channels), 0)
    near = many + rows
    edge_row = jnp.where(row == 0, north, south)
    edge_col = jnp.where(col == 0, west, east)
    for slot in range(slots):
        same = face == slot // side
        y, x = slot % side // cut, slot % cut
        level = jnp.where(
            x == (here_x + cut - 1) % cut, west, jnp.where(x == (here_x + 1) % cut, east, north)
        )
        inner = jnp.where(y < here_y, north, jnp.where(y > here_y, south, level))
        strip = jnp.where(same, inner, edge_row)
        side_strip = jnp.where(same, south, edge_col)
        sent_ref[slot, many:near] = strip[1 : rim - 1].astype(BF)
        sent_ref[slot, near : near + rows] = side_strip[1 : rim - 1].astype(BF)
        ends = [strip[0:1], strip[rim - 1 : rim], side_strip[0:1], side_strip[rim - 1 : rim]]
        values = ends
        for k in range(few * slot, min(few * slot + few, len(small))):
            high = small[k].astype(BF).astype(F32)
            values = values + [high, small[k] - high]
        block = jnp.zeros((extra, channels), F32)
        for k, value in enumerate(values):
            block = jnp.where(place == k, value, block)
        sent_ref[slot, near + rows : near + rows + extra] = block.astype(BF)


def block_on_tile(plan, padded, tile, grad, taps, *params):
    rows, columns, channels = tile.shape
    slots, depth = params[-2:]
    return pl.pallas_call(
        block_kernel,
        out_shape=(
            jax.ShapeDtypeStruct(tile.shape, BF),
            jax.ShapeDtypeStruct((slots, depth, channels), BF),
            jax.ShapeDtypeStruct(tile.shape, F32),
        ),
        in_specs=[pl.BlockSpec(memory_space=pltpu.SMEM)]
        + [pl.BlockSpec(memory_space=pltpu.VMEM)] * 11,
        out_specs=(pl.BlockSpec(memory_space=pltpu.VMEM),) * 3,
        scratch_shapes=[pltpu.VMEM((rows + 2, columns + 8, channels), F32)],
        compiler_params=pltpu.CompilerParams(vmem_limit_bytes=24 * 1024 * 1024),
        name="block",
    )(plan, padded, tile, grad, taps, *params[:-2])


def finish_kernel(got_ref, *out_refs):
    tap_ref, bias_ref, gain_ref, shift_ref, expand_ref, expand_bias_ref, reduce_ref, reduce_bias_ref = (
        out_refs
    )
    slots, depth, channels = got_ref.shape
    hid = reduce_ref.shape[0]
    many = 2 * hid // slots
    for k in range(0, hid, channels):
        for j in range(0, channels, many):
            expand_ref[j : j + many, k : k + channels] = got_ref[(k + j) // many, 0:many].astype(F32)
    for k in range(0, hid, many):
        reduce_ref[k : k + many] = got_ref[(hid + k) // many, 0:many].astype(F32)
    blocks = hid // channels
    few = -(-(13 + blocks) // slots)
    small = []
    for slot in range(slots):
        rest = got_ref[slot, many:depth].astype(F32)
        small += [rest[2 * k : 2 * k + 1] + rest[2 * k + 1 : 2 * k + 2] for k in range(few)]
    for k in range(9):
        tap_ref[k : k + 1] = small[k]
    bias_ref[...] = small[9]
    gain_ref[...] = small[10]
    shift_ref[...] = small[11]
    for k in range(blocks):
        expand_bias_ref[:, k * channels : (k + 1) * channels] = small[12 + k]
    reduce_bias_ref[...] = small[12 + blocks]


def finish(got, hid):
    channels = got.shape[2]
    shapes = [(9, channels)] + [(1, channels)] * 3
    shapes += [(channels, hid), (1, hid), (hid, channels), (1, channels)]
    return pl.pallas_call(
        finish_kernel,
        out_shape=tuple(jax.ShapeDtypeStruct(shape, F32) for shape in shapes),
        in_specs=[pl.BlockSpec(memory_space=pltpu.VMEM)],
        out_specs=(pl.BlockSpec(memory_space=pltpu.VMEM),) * len(shapes),
        compiler_params=pltpu.CompilerParams(vmem_limit_bytes=16 * 1024 * 1024),
        name="finish",
    )(got)


def swap(slots, groups):
    return lax.all_to_all(slots, ("face", "row", "col"), 0, 0, axis_index_groups=groups)


def at(slots, index):
    return lax.dynamic_index_in_dim(slots, index, 0, keepdims=False)


def plane_and_line_groups(side):
    cut = math.isqrt(side)
    steps = range(cut)

    def device(f, y, x, high, low):
        return (f * side + y * cut + low) * side + high * cut + x

    planes = [
        [device(f, y, x, high, low) for f in range(2) for y in steps for x in steps]
        for high in steps
        for low in steps
    ]
    lines = [
        [device(f, y, x, high, low) for high in steps for low in steps]
        for f in range(2)
        for y in steps
        for x in steps
    ]
    return planes, lines


def frame_sources(adjacency, f, y, x, sender, target, side, cells, stride, rims):
    cut = math.isqrt(side)
    last = side - 1
    width = side * cells
    high, low = sender // cut, sender % cut
    row, col = y * cut + target % cut, target // cut * cut + x
    step = jnp.arange(cells + 2, dtype=jnp.int32) - 1
    high, low, row, col = (jnp.asarray(v)[..., None] for v in (high, low, row, col))

    def held(face, tile_row, tile_col, part, cell, valid, virtual):
        valid = valid & (tile_row % cut == low) & (tile_col // cut == high)
        slot = face * side + tile_row // cut * cut + tile_col % cut
        index = slot * stride + part * cells + cell
        if rims:
            end = slot * stride + 2 * cells + 2 * part + jnp.where(cell == 0, 0, 1)
            index = jnp.where(virtual, end, index)
        return jnp.where(valid, index, -1)

    virtual = (step < 0) | (step >= cells)

    def glued(edge, along, on_rows):
        entry = adjacency[f, edge]
        position = along * cells + step
        turned = jnp.where(entry[2] == 1, width - 1 - position, position)
        valid = (position >= 0) & (position < width)
        tile, cell = turned // cells, turned % cells
        if on_rows:
            end = jnp.where(entry[1] == 2, 0, last)
            return held(1 - f, tile, end, 1, cell, valid, virtual)
        end = jnp.where(entry[1] == 0, 0, last)
        return held(1 - f, end, tile, 0, cell, valid, virtual)

    def beside(next_row, far_cell, own_part):
        position = col * cells + step
        valid = (position >= 0) & (position < width)
        tile, cell = position // cells, position % cells
        level = next_row // cut == y
        own = level & ~virtual
        part = jnp.where(own, own_part, 0)
        cell = jnp.where(level & virtual, far_cell, cell)
        return held(f, next_row, tile, part, cell, valid, virtual)

    top = jnp.where(row == 0, glued(0, col, True), beside(row - 1, cells - 1, 1))
    bottom = jnp.where(row == last, glued(1, col, True), beside(row + 1, 0, 0))
    west = jnp.where(
        col == 0, glued(2, row, False), held(f, row, col - 1, 0, step, ~virtual, virtual)
    )
    east = jnp.where(
        col == last, glued(3, row, False), held(f, row, col + 1, 0, step, ~virtual, virtual)
    )
    west = jnp.where(x == 0, west, -1)
    east = jnp.where(x == cut - 1, east, -1)
    return [top, bottom, west, east]


def two_sides(sources):
    need = [jnp.any(source >= 0, axis=-1) for source in sources]
    near = jnp.where(need[0], 0, jnp.where(need[1], 1, jnp.where(need[2], 2, 3)))
    after_one = jnp.where(need[2], 2, 3)
    far = jnp.where(
        need[0], jnp.where(need[1], 1, after_one), jnp.where(need[1], after_one, jnp.where(need[2], 3, 2))
    )
    return near, far


def slot_order(near, far):
    return jnp.concatenate(
        [
            near[..., 1:-1],
            far[..., 1:-1],
            near[..., :1],
            near[..., -1:],
            far[..., :1],
            far[..., -1:],
            jnp.full(near.shape[:-1] + (4,), -1, jnp.int32),
        ],
        axis=-1,
    )


def picked(wanted, held):
    chosen = (wanted.reshape(-1, 1) == jnp.arange(held.shape[0], dtype=jnp.int32)).astype(BF)
    cells = jnp.dot(chosen, held, preferred_element_type=F32).astype(BF)
    return cells.reshape(wanted.shape + held.shape[1:])


def on_device(
    fields,
    conv_kernel,
    conv_bias,
    norm_gain,
    norm_bias,
    expand_weight,
    expand_bias,
    reduce_weight,
    reduce_bias,
    adjacency,
    out_grad,
):
    tile = fields[0]
    cells = tile.shape[0]
    channels = tile.shape[2]
    hid = expand_weight.shape[1]
    side = lax.axis_size("row")
    width = side * cells
    rim = cells + 2
    cut = math.isqrt(side)
    f = lax.axis_index("face")
    r = lax.axis_index("row")
    c = lax.axis_index("col")
    y, x = r // cut, c % cut
    place = c // cut * cut + r % cut
    planes, lines = plane_and_line_groups(side)
    line_slots = jnp.arange(side, dtype=jnp.int32)

    def wanted(stride, rims):
        sources = frame_sources(
            adjacency, f, y, x, place, line_slots, side, cells, stride, rims
        )
        near, far = two_sides(sources)

        def chosen(which):
            which = which[:, None]
            return jnp.where(
                which == 0,
                sources[0],
                jnp.where(which == 1, sources[1], jnp.where(which == 2, sources[2], sources[3])),
            )

        return slot_order(chosen(near), chosen(far))

    near, far = two_sides(
        frame_sources(adjacency, f, y, x, line_slots, place, side, cells, 2 * cells, False)
    )
    step = jnp.arange(rim, dtype=jnp.int32)
    arrival = slot_order(near[:, None] * rim + step, far[:, None] * rim + step)
    frame_rows = jnp.arange(4 * rim, dtype=jnp.int32)[:, None]
    gather_frame = (frame_rows == arrival.reshape(1, -1)).astype(BF)

    def frame_of(strips):
        flat = strips.reshape(-1, channels)
        return jnp.dot(gather_frame, flat, preferred_element_type=F32).reshape(4, rim, channels)

    def direct(strips, frame):
        base = f * side + y * cut
        west = at(strips, base + jnp.maximum(x - 1, 0)).astype(F32)
        east = at(strips, base + jnp.minimum(x + 1, cut - 1)).astype(F32)
        return jnp.where(x == 0, frame[2], west), jnp.where(x == cut - 1, frame[3], east)

    slot = jnp.arange(2 * side, dtype=jnp.int32)[:, None, None]
    same, slot_y, slot_x = slot // side == f, slot % side // cut, slot % cut
    top_row, bottom_row = tile[0], tile[cells - 1]
    first_col, last_col = tile[:, 0], tile[:, cells - 1]
    upper = jnp.where(same, slot_y <= y, r == 0)
    level = same & (slot_y == y)
    near_strip = jnp.where(
        level & (slot_x == (x + cut - 1) % cut),
        first_col,
        jnp.where(
            level & (slot_x == (x + 1) % cut), last_col, jnp.where(upper, top_row, bottom_row)
        ),
    )
    far_strip = jnp.where(same, bottom_row, jnp.where(c == 0, first_col, last_col))
    got = swap(jnp.concatenate([near_strip, far_strip], axis=1), planes)
    passed = picked(wanted(2 * cells, False), got.reshape(-1, channels))
    frame = frame_of(swap(passed, lines))
    west, east = direct(got[:, :cells], frame[:, 1:-1])
    ends = frame[2:, ::rim - 1]
    top = jnp.concatenate(
        [frame[0, :1] + ends[0, :1], frame[0, 1:-1], frame[0, -1:] + ends[1, :1]]
    ).astype(BF)
    bottom = jnp.concatenate(
        [frame[1, :1] + ends[0, 1:], frame[1, 1:-1], frame[1, -1:] + ends[1, 1:]]
    ).astype(BF)
    padded = jnp.concatenate(
        [
            top[None],
            jnp.concatenate([west.astype(BF)[:, None], tile, east.astype(BF)[:, None]], axis=1),
            bottom[None],
        ]
    )

    small_count = 13 + hid // channels
    many = 2 * hid // (2 * side)
    few = -(-small_count // (2 * side))
    extra = 8
    assert 2 * few <= 4
    block_out, sent, base_grad = block_on_tile(
        jnp.stack([f, r, c]).astype(jnp.int32),
        padded,
        tile,
        out_grad[0],
        conv_kernel.reshape(9, channels),
        conv_bias.reshape(1, channels),
        norm_gain.reshape(1, channels),
        norm_bias.reshape(1, channels),
        expand_weight,
        expand_bias.reshape(1, hid),
        reduce_weight,
        reduce_bias.reshape(1, channels),
        2 * side,
        many + 2 * cells + extra,
    )
    got = swap(sent, planes)

    def pairs(small):
        high = small.astype(BF)
        low = (small - high.astype(F32)).astype(BF)
        return jnp.stack([high, low], axis=-2).reshape(2 * few, channels)

    def small_total(rest):
        sums = jnp.sum(rest.astype(F32), axis=0).reshape(few, 2, channels)
        return sums[:, 0] + sums[:, 1]

    spare = many + 2 * cells + 4
    weights = jnp.sum(got[:, :many].astype(F32), axis=0)
    small = small_total(got[:, spare : spare + 2 * few])
    strips = got[:, many:]
    passed = picked(wanted(2 * cells + extra, True), strips.reshape(-1, channels))
    tail = jnp.pad(pairs(small), ((0, 4 - 2 * few), (0, 0)))
    sent = jnp.concatenate(
        [
            jnp.broadcast_to(weights.astype(BF), (side, many, channels)),
            passed[:, : 2 * cells],
            jnp.concatenate(
                [passed[:, 2 * cells : 2 * cells + 4], jnp.broadcast_to(tail, (side, 4, channels))],
                axis=1,
            ),
        ],
        axis=1,
    )
    got = swap(sent, lines)
    weights = jnp.sum(got[:, :many].astype(F32), axis=0) / width
    small = small_total(got[:, spare : spare + 2 * few]) / width
    share = jnp.concatenate(
        [weights.astype(BF), jnp.pad(pairs(small), ((0, 8 - 2 * few), (0, 0)))]
    )
    spread = swap(jnp.broadcast_to(share, (2 * side,) + share.shape), planes)

    frame = frame_of(got[:, many:])
    folded = frame[:, 1:-1]
    folded = folded.at[:, 0].add(frame[:, 0]).at[:, -1].add(frame[:, -1])
    west, east = direct(strips[:, :cells], folded)
    in_grad = base_grad
    in_grad = in_grad + jnp.pad(folded[:1], ((0, cells - 1), (0, 0), (0, 0)))
    in_grad = in_grad + jnp.pad(folded[1:2], ((cells - 1, 0), (0, 0), (0, 0)))
    in_grad = in_grad + jnp.pad(west[:, None], ((0, 0), (0, cells - 1), (0, 0)))
    in_grad = in_grad + jnp.pad(east[:, None], ((0, 0), (cells - 1, 0), (0, 0)))

    taps, bias, gain, shift, expand, expand_vector, reduce, reduce_vector = finish(spread, hid)
    return (
        block_out[None],
        in_grad.astype(BF)[None],
        taps.reshape(3, 3, channels),
        bias.reshape(channels),
        gain.reshape(channels),
        shift.reshape(channels),
        expand,
        expand_vector.reshape(hid),
        reduce,
        reduce_vector.reshape(channels),
    )


def solution(mesh):
    tiles = P("face", "row", "col", None)
    in_specs = (tiles,) + (P(),) * 9 + (tiles,)
    out_specs = (tiles, tiles) + (P(),) * 8
    return jax.shard_map(
        on_device, mesh=mesh, in_specs=in_specs, out_specs=out_specs, check_vma=False
    )
```

```python
import functools
import math

import jax
import jax.numpy as jnp
from jax import lax
from jax.experimental import pallas as pl
from jax.experimental.pallas import tpu as pltpu
from jax.sharding import PartitionSpec as P

GELU_SCALE = math.sqrt(2.0 / math.pi)
NORM_EPS = 1e-06
BF = jnp.bfloat16
F32 = jnp.float32


def gelu_pair(preact):
    cubic_term = preact + 0.044715 * preact * preact * preact
    tangent = jnp.tanh(GELU_SCALE * cubic_term)
    gelu_value = 0.5 * preact * (1.0 + tangent)
    gelu_slope = 0.5 * (1.0 + tangent) + 0.5 * preact * (1.0 - tangent * tangent) * GELU_SCALE * (
        1.0 + 3.0 * 0.044715 * preact * preact
    )
    return (gelu_value, gelu_slope)


def slot_strips(face, row, col, slot, side, north, south, west, east):
    cut = math.isqrt(side)
    here_y, here_x = row // cut, col % cut
    same = face == slot // side
    y, x = slot % side // cut, slot % cut
    level = jnp.where(
        x == (here_x + cut - 1) % cut, west, jnp.where(x == (here_x + 1) % cut, east, north)
    )
    inner = jnp.where(y < here_y, north, jnp.where(y > here_y, south, level))
    near = jnp.where(same, inner, jnp.where(row == 0, north, south))
    far = jnp.where(same, south, jnp.where(col == 0, west, east))
    return near, far


def edges_kernel(place_ref, tile_ref, sent_ref):
    slots, depth, _ = sent_ref.shape
    rows = depth // 2
    tile = tile_ref[...].astype(F32)
    north, south = tile[0], tile[rows - 1]
    west = jnp.concatenate([tile[k, 0:1] for k in range(rows)])
    east = jnp.concatenate([tile[k, rows - 1 : rows] for k in range(rows)])
    for slot in range(slots):
        near, far = slot_strips(
            place_ref[0], place_ref[1], place_ref[2], slot, slots // 2, north, south, west, east
        )
        sent_ref[slot, 0:rows] = near.astype(BF)
        sent_ref[slot, rows:depth] = far.astype(BF)


def edges_of(place, tile, slots):
    rows, _, channels = tile.shape
    return pl.pallas_call(
        edges_kernel,
        out_shape=jax.ShapeDtypeStruct((slots, 2 * rows, channels), BF),
        in_specs=[
            pl.BlockSpec(memory_space=pltpu.SMEM),
            pl.BlockSpec(memory_space=pltpu.VMEM),
        ],
        out_specs=pl.BlockSpec(memory_space=pltpu.VMEM),
        compiler_params=pltpu.CompilerParams(vmem_limit_bytes=8 * 1024 * 1024),
        name="edges",
    )(place, tile)


def block_kernel(
    plan_ref,
    padded_ref,
    tile_ref,
    grad_ref,
    tap_ref,
    conv_bias_ref,
    gain_ref,
    shift_ref,
    expand_ref,
    expand_bias_ref,
    reduce_ref,
    reduce_bias_ref,
    out_ref,
    sent_ref,
    base_ref,
    wide_ref,
):
    rows, columns, channels = tile_ref.shape
    count = rows * columns
    rim = rows + 2
    hid = expand_ref.shape[1]
    slots, _, _ = sent_ref.shape
    side = slots // 2
    padded = padded_ref[...].astype(F32)
    shifted = [padded[:, b : b + columns] for b in range(3)]

    mixed = jnp.zeros((rows, columns, channels), F32) + conv_bias_ref[...].reshape(1, 1, channels)
    for a in range(3):
        for b in range(3):
            mixed = mixed + tap_ref[3 * a + b].reshape(1, 1, channels) * shifted[b][a : a + rows]
    mixed = mixed.reshape(count, channels)
    center = mixed - jnp.mean(mixed, axis=-1, keepdims=True)
    inv_std = lax.rsqrt(jnp.mean(center * center, axis=-1, keepdims=True) + NORM_EPS)
    normalized = center * inv_std
    normed = (normalized * gain_ref[...] + shift_ref[...]).astype(BF)
    preact = jnp.dot(normed, expand_ref[...], preferred_element_type=F32) + expand_bias_ref[...]
    gelu_value, gelu_slope = gelu_pair(preact)
    hidden = gelu_value.astype(BF)
    grad_cells = grad_ref[...].reshape(count, channels)
    grad_hidden = lax.dot_general(
        grad_cells, reduce_ref[...], (((1,), (1,)), ((), ())), preferred_element_type=F32
    )
    grad_preact = (grad_hidden * gelu_slope).astype(BF)
    grad_normed = lax.dot_general(
        grad_preact, expand_ref[...], (((1,), (1,)), ((), ())), preferred_element_type=F32
    )
    scaled = grad_normed * gain_ref[...]
    grad_mixed = inv_std * (
        scaled
        - jnp.mean(scaled, axis=-1, keepdims=True)
        - normalized * jnp.mean(scaled * normalized, axis=-1, keepdims=True)
    )
    out = tile_ref[...].reshape(count, channels).astype(F32)
    out = out + jnp.dot(hidden, reduce_ref[...], preferred_element_type=F32) + reduce_bias_ref[...]
    out_ref[...] = out.astype(BF).reshape(rows, columns, channels)

    def total(cells):
        return jnp.sum(cells, axis=0, keepdims=True)

    square = grad_mixed.reshape(rows, columns, channels)
    small = [
        total((square * shifted[b][a : a + rows]).reshape(count, channels))
        for a in range(3)
        for b in range(3)
    ]
    small += [total(grad_mixed), total(grad_normed * normalized), total(grad_normed)]
    preact_total = total(grad_preact.astype(F32))
    small += [preact_total[:, k : k + channels] for k in range(0, hid, channels)]
    small += [total(grad_cells.astype(F32))]

    across = (((0,), (0,)), ((), ()))
    expand_sum = lax.dot_general(normed, grad_preact, across, preferred_element_type=F32).astype(BF)
    reduce_sum = lax.dot_general(hidden, grad_cells, across, preferred_element_type=F32).astype(BF)
    many = 2 * hid // slots
    for k in range(0, hid, channels):
        for j in range(0, channels, many):
            sent_ref[(k + j) // many, 0:many] = expand_sum[j : j + many, k : k + channels]
    for k in range(0, hid, many):
        sent_ref[(hid + k) // many, 0:many] = reduce_sum[k : k + many]

    wide_ref[...] = jnp.zeros(wide_ref.shape, F32)
    for b in range(3):
        parts = [tap_ref[3 * a + b].reshape(1, 1, channels) * square for a in range(3)]
        wide_ref[0, b : b + columns] += parts[0][0]
        wide_ref[1, b : b + columns] += parts[0][1] + parts[1][0]
        wide_ref[2:rows, b : b + columns] += (
            parts[0][2:] + parts[1][1 : rows - 1] + parts[2][: rows - 2]
        )
        wide_ref[rows, b : b + columns] += parts[1][rows - 1] + parts[2][rows - 2]
        wide_ref[rows + 1, b : b + columns] += parts[2][rows - 1]
    base_ref[...] = grad_ref[...].astype(F32) + wide_ref[1 : rows + 1, 1 : columns + 1]
    west = jnp.concatenate([wide_ref[k, 0:1] for k in range(rim)])
    east = jnp.concatenate([wide_ref[k, rim - 1 : rim] for k in range(rim)])
    north = wide_ref[0, 0:rim]
    south = wide_ref[rim - 1, 0:rim]

    face, row, col = plan_ref[0], plan_ref[1], plan_ref[2]
    few = -(-len(small) // slots)
    extra = sent_ref.shape[1] - many - 2 * rows
    place = lax.broadcasted_iota(jnp.int32, (extra, channels), 0)
    near = many + rows
    for slot in range(slots):
        strip, side_strip = slot_strips(face, row, col, slot, side, north, south, west, east)
        sent_ref[slot, many:near] = strip[1 : rim - 1].astype(BF)
        sent_ref[slot, near : near + rows] = side_strip[1 : rim - 1].astype(BF)
        ends = [strip[0:1], strip[rim - 1 : rim], side_strip[0:1], side_strip[rim - 1 : rim]]
        values = ends
        for k in range(few * slot, min(few * slot + few, len(small))):
            high = small[k].astype(BF).astype(F32)
            values = values + [high, small[k] - high]
        block = jnp.zeros((extra, channels), F32)
        for k, value in enumerate(values):
            block = jnp.where(place == k, value, block)
        sent_ref[slot, near + rows : near + rows + extra] = block.astype(BF)


def block_on_tile(plan, padded, tile, grad, taps, *params):
    rows, columns, channels = tile.shape
    slots, depth = params[-2:]
    return pl.pallas_call(
        block_kernel,
        out_shape=(
            jax.ShapeDtypeStruct(tile.shape, BF),
            jax.ShapeDtypeStruct((slots, depth, channels), BF),
            jax.ShapeDtypeStruct(tile.shape, F32),
        ),
        in_specs=[pl.BlockSpec(memory_space=pltpu.SMEM)]
        + [pl.BlockSpec(memory_space=pltpu.VMEM)] * 11,
        out_specs=(pl.BlockSpec(memory_space=pltpu.VMEM),) * 3,
        scratch_shapes=[pltpu.VMEM((rows + 2, columns + 8, channels), F32)],
        compiler_params=pltpu.CompilerParams(vmem_limit_bytes=24 * 1024 * 1024),
        name="block",
    )(plan, padded, tile, grad, taps, *params[:-2])


def share_kernel(scale, few, got_ref, share_ref):
    slots, depth, channels = share_ref.shape
    many = depth - 8
    spare = got_ref.shape[1] - 4
    weights = jnp.zeros((many, channels), F32)
    rest = jnp.zeros((4, channels), F32)
    for k in range(got_ref.shape[0]):
        weights = weights + got_ref[k, 0:many].astype(F32)
        rest = rest + got_ref[k, spare - 4 : spare + 4].astype(F32)[4:8]
    weights = (weights * scale).astype(BF)
    place = lax.broadcasted_iota(jnp.int32, (8, channels), 0)
    block = jnp.zeros((8, channels), F32)
    for k in range(few):
        small = (rest[2 * k : 2 * k + 1] + rest[2 * k + 1 : 2 * k + 2]) * scale
        high = small.astype(BF).astype(F32)
        block = jnp.where(place == 2 * k, high, jnp.where(place == 2 * k + 1, small - high, block))
    block = block.astype(BF)
    for slot in range(slots):
        share_ref[slot, 0:many] = weights
        share_ref[slot, many:depth] = block


def share_of(got, slots, many, few, scale):
    channels = got.shape[2]
    return pl.pallas_call(
        functools.partial(share_kernel, scale, few),
        out_shape=jax.ShapeDtypeStruct((slots, many + 8, channels), BF),
        in_specs=[pl.BlockSpec(memory_space=pltpu.VMEM)],
        out_specs=pl.BlockSpec(memory_space=pltpu.VMEM),
        compiler_params=pltpu.CompilerParams(vmem_limit_bytes=8 * 1024 * 1024),
        name="share",
    )(got)


def finish_kernel(got_ref, *out_refs):
    tap_ref, bias_ref, gain_ref, shift_ref, expand_ref, expand_bias_ref, reduce_ref, reduce_bias_ref = (
        out_refs
    )
    slots, depth, channels = got_ref.shape
    hid = reduce_ref.shape[0]
    many = 2 * hid // slots
    for k in range(0, hid, channels):
        for j in range(0, channels, many):
            expand_ref[j : j + many, k : k + channels] = got_ref[(k + j) // many, 0:many].astype(F32)
    for k in range(0, hid, many):
        reduce_ref[k : k + many] = got_ref[(hid + k) // many, 0:many].astype(F32)
    blocks = hid // channels
    few = -(-(13 + blocks) // slots)
    small = []
    for slot in range(slots):
        rest = got_ref[slot, many:depth].astype(F32)
        small += [rest[2 * k : 2 * k + 1] + rest[2 * k + 1 : 2 * k + 2] for k in range(few)]
    for k in range(9):
        tap_ref[k // 3, k % 3 : k % 3 + 1] = small[k]
    bias_ref[...] = small[9]
    gain_ref[...] = small[10]
    shift_ref[...] = small[11]
    for k in range(blocks):
        expand_bias_ref[:, k * channels : (k + 1) * channels] = small[12 + k]
    reduce_bias_ref[...] = small[12 + blocks]


def finish(got, hid):
    channels = got.shape[2]
    shapes = [(3, 3, channels)] + [(1, channels)] * 3
    shapes += [(channels, hid), (1, hid), (hid, channels), (1, channels)]
    return pl.pallas_call(
        finish_kernel,
        out_shape=tuple(jax.ShapeDtypeStruct(shape, F32) for shape in shapes),
        in_specs=[pl.BlockSpec(memory_space=pltpu.VMEM)],
        out_specs=(pl.BlockSpec(memory_space=pltpu.VMEM),) * len(shapes),
        compiler_params=pltpu.CompilerParams(vmem_limit_bytes=16 * 1024 * 1024),
        name="finish",
    )(got)


def swap(slots, groups):
    return lax.all_to_all(slots, ("face", "row", "col"), 0, 0, axis_index_groups=groups)


def at(slots, index):
    return lax.dynamic_index_in_dim(slots, index, 0, keepdims=False)


def plane_and_line_groups(side):
    cut = math.isqrt(side)
    steps = range(cut)

    def device(f, y, x, high, low):
        return (f * side + y * cut + low) * side + high * cut + x

    planes = [
        [device(f, y, x, high, low) for f in range(2) for y in steps for x in steps]
        for high in steps
        for low in steps
    ]
    lines = [
        [device(f, y, x, high, low) for high in steps for low in steps]
        for f in range(2)
        for y in steps
        for x in steps
    ]
    return planes, lines


def frame_sources(entries, f, y, x, sender, target, step, side, cells):
    cut = math.isqrt(side)
    last, width, low_bits, cell_bits = side - 1, side * cells, cut - 1, cells - 1
    shift, cell_shift = low_bits.bit_length(), cell_bits.bit_length()
    high, low = sender >> shift, sender & low_bits
    row, col = y * cut + (target & low_bits), (target >> shift) * cut + x
    virtual = (step < 0) | (step >= cells)

    def held(face, tile_row, tile_col, part, cell, valid):
        valid = valid & ((tile_row & low_bits) == low) & ((tile_col >> shift) == high)
        slot = face * side + ((tile_row >> shift) << shift) + (tile_col & low_bits)
        inner = part * cells + cell
        end = 2 * cells + 2 * part + jnp.where(cell == 0, 0, 1)
        inner_index = slot * (2 * cells) + inner
        end_index = slot * (2 * cells + 8) + jnp.where(virtual, end, inner)
        return jnp.where(valid, inner_index, -1), jnp.where(valid, end_index, -1)

    def glued(edge, along, on_rows):
        other_edge, reverse = entries[edge]
        position = along * cells + step
        turned = jnp.where(reverse == 1, width - 1 - position, position)
        valid = (position >= 0) & (position < width)
        tile, cell = turned >> cell_shift, turned & cell_bits
        if on_rows:
            end = jnp.where(other_edge == 2, 0, last)
            return held(1 - f, tile, end, 1, cell, valid)
        end = jnp.where(other_edge == 0, 0, last)
        return held(1 - f, end, tile, 0, cell, valid)

    def beside(next_row, far_cell, own_part):
        position = col * cells + step
        valid = (position >= 0) & (position < width)
        tile, cell = position >> cell_shift, position & cell_bits
        level = (next_row >> shift) == y
        part = jnp.where(level & (step >= 0) & (step < cells), own_part, 0)
        cell = jnp.where(level & virtual, far_cell, cell)
        return held(f, next_row, tile, part, cell, valid)

    def either(condition, first, second):
        return tuple(jnp.where(condition, p, q) for p, q in zip(first, second))

    inner = (step >= 0) & (step < cells)
    nothing = (-1, -1)
    top = either(row == 0, glued(0, col, True), beside(row - 1, cells - 1, 1))
    bottom = either(row == last, glued(1, col, True), beside(row + 1, 0, 0))
    west = either(col == 0, glued(2, row, False), held(f, row, col - 1, 0, step, inner))
    east = either(col == last, glued(3, row, False), held(f, row, col + 1, 0, step, inner))
    return [top, bottom, either(x == 0, west, nothing), either(x == cut - 1, east, nothing)]


def two_sides(sources):
    need = [jnp.max(source[1].astype(F32), axis=-1, keepdims=True) >= 0.0 for source in sources]
    near = jnp.where(need[0], 0, jnp.where(need[1], 1, jnp.where(need[2], 2, 3)))
    after_one = jnp.where(need[2], 2, 3)
    far = jnp.where(
        need[0], jnp.where(need[1], 1, after_one), jnp.where(need[1], after_one, jnp.where(need[2], 3, 2))
    )
    return near, far


def plan_arrays(entries, f, r, c, side, cells):
    cut = math.isqrt(side)
    y, x = r // cut, c % cut
    here = c // cut * cut + r % cut
    others = lax.broadcasted_iota(jnp.int32, (side, 128), 0)
    lane = lax.broadcasted_iota(jnp.int32, (side, 128), 1)
    main = lane < 2 * cells
    step = jnp.where(main, lane & (cells - 1), jnp.where((lane & 1) == 0, -1, cells))
    second = jnp.where(main, lane - cells, lane - 2 * cells - 2) >= 0
    used = lane < 2 * cells + 4
    sources = frame_sources(entries, f, y, x, here, others, step, side, cells)
    near, far = two_sides(sources)
    which = jnp.where(second, far, near)
    passed = []
    for form in range(2):
        index = jnp.where(
            which == 0,
            sources[0][form],
            jnp.where(
                which == 1, sources[1][form], jnp.where(which == 2, sources[2][form], sources[3][form])
            ),
        )
        passed.append(jnp.where(used, index, -1))
    sources = frame_sources(entries, f, y, x, others, here, step, side, cells)
    near, far = two_sides(sources)
    which = jnp.where(second, far, near)
    return passed[0], passed[1], jnp.where(used, which * (cells + 2) + step + 1, -1)


def plan_kernel(side, cells, place_ref, adjacency_ref, plan_ref):
    f = place_ref[0]
    entries = [
        (adjacency_ref[f * 12 + 3 * edge + 1], adjacency_ref[f * 12 + 3 * edge + 2])
        for edge in range(4)
    ]
    arrays = plan_arrays(entries, f, place_ref[1], place_ref[2], side, cells)
    for k, array in enumerate(arrays):
        plan_ref[k] = array


def plan_of(place, adjacency, side, cells):
    return pl.pallas_call(
        functools.partial(plan_kernel, side, cells),
        out_shape=jax.ShapeDtypeStruct((3, side, 128), jnp.int32),
        in_specs=[pl.BlockSpec(memory_space=pltpu.SMEM)] * 2,
        out_specs=pl.BlockSpec(memory_space=pltpu.VMEM),
        compiler_params=pltpu.CompilerParams(vmem_limit_bytes=4 * 1024 * 1024),
        name="plan",
    )(place, adjacency.reshape(-1))


def picked(wanted, held):
    chosen = (wanted.reshape(-1, 1) == jnp.arange(held.shape[0], dtype=jnp.int32)).astype(BF)
    cells = jnp.dot(chosen, held, preferred_element_type=F32).astype(BF)
    return cells.reshape(wanted.shape + held.shape[1:])


def on_device(
    fields,
    conv_kernel,
    conv_bias,
    norm_gain,
    norm_bias,
    expand_weight,
    expand_bias,
    reduce_weight,
    reduce_bias,
    adjacency,
    out_grad,
):
    tile = fields[0]
    cells = tile.shape[0]
    channels = tile.shape[2]
    hid = expand_weight.shape[1]
    side = lax.axis_size("row")
    width = side * cells
    rim = cells + 2
    cut = math.isqrt(side)
    f = lax.axis_index("face")
    r = lax.axis_index("row")
    c = lax.axis_index("col")
    y, x = r // cut, c % cut
    planes, lines = plane_and_line_groups(side)
    place = jnp.stack([f, r, c]).astype(jnp.int32)
    few = -(-(13 + hid // channels) // (2 * side))
    extra = 8
    assert 2 * few <= 4 and cells & (cells - 1) == 0 and cut & (cut - 1) == 0

    plan = plan_of(place, adjacency, side, cells)
    inner_wanted = plan[0, :, : 2 * cells + 4]
    end_wanted = plan[1, :, : 2 * cells + extra]
    frame_rows = jnp.arange(4 * rim, dtype=jnp.int32)[:, None]

    def frame_of(strips):
        depth = strips.shape[1]
        arrival = plan[2, :, :depth].reshape(1, -1)
        flat = strips.reshape(-1, channels)
        gather_frame = (frame_rows == arrival).astype(BF)
        return jnp.dot(gather_frame, flat, preferred_element_type=F32).reshape(4, rim, channels)

    def direct(strips, frame):
        base = f * side + y * cut
        west = at(strips, base + jnp.maximum(x - 1, 0)).astype(F32)
        east = at(strips, base + jnp.minimum(x + 1, cut - 1)).astype(F32)
        return jnp.where(x == 0, frame[2], west), jnp.where(x == cut - 1, frame[3], east)

    got = swap(edges_of(place, tile, 2 * side), planes)
    passed = picked(inner_wanted, got.reshape(-1, channels))
    passed = swap(passed.reshape(side, -1, 4, channels), lines)
    frame = frame_of(passed.reshape(side, 2 * cells + 4, channels))
    west, east = direct(got[:, :cells], frame[:, 1:-1])
    ends = frame[2:, ::rim - 1]
    top = jnp.concatenate(
        [frame[0, :1] + ends[0, :1], frame[0, 1:-1], frame[0, -1:] + ends[1, :1]]
    ).astype(BF)
    bottom = jnp.concatenate(
        [frame[1, :1] + ends[0, 1:], frame[1, 1:-1], frame[1, -1:] + ends[1, 1:]]
    ).astype(BF)
    padded = jnp.concatenate(
        [
            top[None],
            jnp.concatenate([west.astype(BF)[:, None], tile, east.astype(BF)[:, None]], axis=1),
            bottom[None],
        ]
    )

    many = 2 * hid // (2 * side)
    block_out, sent, base_grad = block_on_tile(
        place,
        padded,
        tile,
        out_grad[0],
        conv_kernel.reshape(9, channels),
        conv_bias.reshape(1, channels),
        norm_gain.reshape(1, channels),
        norm_bias.reshape(1, channels),
        expand_weight,
        expand_bias.reshape(1, hid),
        reduce_weight,
        reduce_bias.reshape(1, channels),
        2 * side,
        many + 2 * cells + extra,
    )
    got = swap(sent, planes)

    def pairs(small):
        high = small.astype(BF)
        low = (small - high.astype(F32)).astype(BF)
        return jnp.stack([high, low], axis=-2).reshape(2 * few, channels)

    def small_total(rest):
        sums = jnp.sum(rest.astype(F32), axis=0).reshape(few, 2, channels)
        return sums[:, 0] + sums[:, 1]

    spare = many + 2 * cells + 4
    weights = jnp.sum(got[:, :many].astype(F32), axis=0)
    small = small_total(got[:, spare : spare + 2 * few])
    strips = got[:, many:]
    passed = picked(end_wanted, strips.reshape(-1, channels))
    tail = jnp.pad(pairs(small), ((0, 4 - 2 * few), (0, 0)))
    sent = jnp.concatenate(
        [
            jnp.broadcast_to(weights.astype(BF), (side, many, channels)),
            passed[:, : 2 * cells],
            jnp.concatenate(
                [passed[:, 2 * cells : 2 * cells + 4], jnp.broadcast_to(tail, (side, 4, channels))],
                axis=1,
            ),
        ],
        axis=1,
    )
    got = swap(sent, lines)
    spread = swap(share_of(got, 2 * side, many, few, 1.0 / width), planes)

    frame = frame_of(got[:, many:])
    folded = frame[:, 1:-1]
    folded = folded.at[:, 0].add(frame[:, 0]).at[:, -1].add(frame[:, -1])
    west, east = direct(strips[:, :cells], folded)
    in_grad = base_grad
    in_grad = in_grad + jnp.pad(folded[:1], ((0, cells - 1), (0, 0), (0, 0)))
    in_grad = in_grad + jnp.pad(folded[1:2], ((cells - 1, 0), (0, 0), (0, 0)))
    in_grad = in_grad + jnp.pad(west[:, None], ((0, 0), (0, cells - 1), (0, 0)))
    in_grad = in_grad + jnp.pad(east[:, None], ((0, 0), (cells - 1, 0), (0, 0)))

    taps, bias, gain, shift, expand, expand_vector, reduce, reduce_vector = finish(spread, hid)
    return (
        block_out[None],
        in_grad.astype(BF)[None],
        taps,
        bias.reshape(channels),
        gain.reshape(channels),
        shift.reshape(channels),
        expand,
        expand_vector.reshape(hid),
        reduce,
        reduce_vector.reshape(channels),
    )


def solution(mesh):
    tiles = P("face", "row", "col", None)
    in_specs = (tiles,) + (P(),) * 9 + (tiles,)
    out_specs = (tiles, tiles) + (P(),) * 8
    return jax.shard_map(
        on_device, mesh=mesh, in_specs=in_specs, out_specs=out_specs, check_vma=False
    )
```

```python
import functools
import math

import jax
import jax.numpy as jnp
from jax import lax
from jax.experimental import pallas as pl
from jax.experimental.pallas import tpu as pltpu
from jax.sharding import PartitionSpec as P

GELU_SCALE = math.sqrt(2.0 / math.pi)
NORM_EPS = 1e-06
BF = jnp.bfloat16
F32 = jnp.float32


def gelu_pair(preact):
    cubic_term = preact + 0.044715 * preact * preact * preact
    tangent = jnp.tanh(GELU_SCALE * cubic_term)
    gelu_value = 0.5 * preact * (1.0 + tangent)
    gelu_slope = 0.5 * (1.0 + tangent) + 0.5 * preact * (1.0 - tangent * tangent) * GELU_SCALE * (
        1.0 + 3.0 * 0.044715 * preact * preact
    )
    return (gelu_value, gelu_slope)


def slot_strips(face, row, col, slot, side, north, south, west, east):
    cut = math.isqrt(side)
    here_y, here_x = row // cut, col % cut
    same = face == slot // side
    y, x = slot % side // cut, slot % cut
    level = jnp.where(
        x == (here_x + cut - 1) % cut, west, jnp.where(x == (here_x + 1) % cut, east, north)
    )
    inner = jnp.where(y < here_y, north, jnp.where(y > here_y, south, level))
    near = jnp.where(same, inner, jnp.where(row == 0, north, south))
    far = jnp.where(same, south, jnp.where(col == 0, west, east))
    return near, far


def edges_kernel(place_ref, tile_ref, sent_ref):
    slots, depth, _ = sent_ref.shape
    rows = depth // 2
    tile = tile_ref[...].astype(F32)
    north, south = tile[0], tile[rows - 1]
    west = jnp.concatenate([tile[k, 0:1] for k in range(rows)])
    east = jnp.concatenate([tile[k, rows - 1 : rows] for k in range(rows)])
    for slot in range(slots):
        near, far = slot_strips(
            place_ref[0], place_ref[1], place_ref[2], slot, slots // 2, north, south, west, east
        )
        sent_ref[slot, 0:rows] = near.astype(BF)
        sent_ref[slot, rows:depth] = far.astype(BF)


def edges_of(place, tile, slots):
    rows, _, channels = tile.shape
    return pl.pallas_call(
        edges_kernel,
        out_shape=jax.ShapeDtypeStruct((slots, 2 * rows, channels), BF),
        in_specs=[
            pl.BlockSpec(memory_space=pltpu.SMEM),
            pl.BlockSpec(memory_space=pltpu.VMEM),
        ],
        out_specs=pl.BlockSpec(memory_space=pltpu.VMEM),
        compiler_params=pltpu.CompilerParams(vmem_limit_bytes=8 * 1024 * 1024),
        name="edges",
    )(place, tile)


def block_kernel(
    plan_ref,
    padded_ref,
    grad_ref,
    grad_hidden_ref,
    tap_ref,
    conv_bias_ref,
    gain_ref,
    shift_ref,
    expand_ref,
    expand_bias_ref,
    hidden_ref,
    sent_ref,
    base_ref,
    wide_ref,
):
    rows, columns, channels = grad_ref.shape
    count = rows * columns
    rim = rows + 2
    hid = expand_ref.shape[1]
    slots, _, _ = sent_ref.shape
    side = slots // 2
    padded = padded_ref[...].astype(F32)
    shifted = [padded[:, b : b + columns] for b in range(3)]

    mixed = jnp.zeros((rows, columns, channels), F32) + conv_bias_ref[...].reshape(1, 1, channels)
    for a in range(3):
        for b in range(3):
            mixed = mixed + tap_ref[3 * a + b].reshape(1, 1, channels) * shifted[b][a : a + rows]
    mixed = mixed.reshape(count, channels)
    center = mixed - jnp.mean(mixed, axis=-1, keepdims=True)
    inv_std = lax.rsqrt(jnp.mean(center * center, axis=-1, keepdims=True) + NORM_EPS)
    normalized = center * inv_std
    normed = (normalized * gain_ref[...] + shift_ref[...]).astype(BF)
    preact = jnp.dot(normed, expand_ref[...], preferred_element_type=F32) + expand_bias_ref[...]
    gelu_value, gelu_slope = gelu_pair(preact)
    hidden = gelu_value.astype(BF)
    hidden_ref[...] = hidden
    grad_cells = grad_ref[...].reshape(count, channels)
    grad_preact = (grad_hidden_ref[...] * gelu_slope).astype(BF)
    grad_normed = lax.dot_general(
        grad_preact, expand_ref[...], (((1,), (1,)), ((), ())), preferred_element_type=F32
    )
    scaled = grad_normed * gain_ref[...]
    grad_mixed = inv_std * (
        scaled
        - jnp.mean(scaled, axis=-1, keepdims=True)
        - normalized * jnp.mean(scaled * normalized, axis=-1, keepdims=True)
    )

    def total(cells):
        return jnp.sum(cells, axis=0, keepdims=True)

    square = grad_mixed.reshape(rows, columns, channels)
    small = [
        total((square * shifted[b][a : a + rows]).reshape(count, channels))
        for a in range(3)
        for b in range(3)
    ]
    small += [total(grad_mixed), total(grad_normed * normalized), total(grad_normed)]
    preact_total = total(grad_preact.astype(F32))
    small += [preact_total[:, k : k + channels] for k in range(0, hid, channels)]
    small += [total(grad_cells.astype(F32))]

    across = (((0,), (0,)), ((), ()))
    expand_sum = lax.dot_general(normed, grad_preact, across, preferred_element_type=F32).astype(BF)
    reduce_sum = lax.dot_general(hidden, grad_cells, across, preferred_element_type=F32).astype(BF)
    many = 2 * hid // slots
    for k in range(0, hid, channels):
        for j in range(0, channels, many):
            sent_ref[(k + j) // many, 0:many] = expand_sum[j : j + many, k : k + channels]
    for k in range(0, hid, many):
        sent_ref[(hid + k) // many, 0:many] = reduce_sum[k : k + many]

    wide_ref[...] = jnp.zeros(wide_ref.shape, F32)
    for b in range(3):
        parts = [tap_ref[3 * a + b].reshape(1, 1, channels) * square for a in range(3)]
        wide_ref[0, b : b + columns] += parts[0][0]
        wide_ref[1, b : b + columns] += parts[0][1] + parts[1][0]
        wide_ref[2:rows, b : b + columns] += (
            parts[0][2:] + parts[1][1 : rows - 1] + parts[2][: rows - 2]
        )
        wide_ref[rows, b : b + columns] += parts[1][rows - 1] + parts[2][rows - 2]
        wide_ref[rows + 1, b : b + columns] += parts[2][rows - 1]
    base_ref[...] = grad_ref[...].astype(F32) + wide_ref[1 : rows + 1, 1 : columns + 1]
    west = jnp.concatenate([wide_ref[k, 0:1] for k in range(rim)])
    east = jnp.concatenate([wide_ref[k, rim - 1 : rim] for k in range(rim)])
    north = wide_ref[0, 0:rim]
    south = wide_ref[rim - 1, 0:rim]

    face, row, col = plan_ref[0], plan_ref[1], plan_ref[2]
    few = -(-len(small) // slots)
    extra = sent_ref.shape[1] - many - 2 * rows
    place = lax.broadcasted_iota(jnp.int32, (extra, channels), 0)
    near = many + rows
    for slot in range(slots):
        strip, side_strip = slot_strips(face, row, col, slot, side, north, south, west, east)
        sent_ref[slot, many:near] = strip[1 : rim - 1].astype(BF)
        sent_ref[slot, near : near + rows] = side_strip[1 : rim - 1].astype(BF)
        ends = [strip[0:1], strip[rim - 1 : rim], side_strip[0:1], side_strip[rim - 1 : rim]]
        values = ends
        for k in range(few * slot, min(few * slot + few, len(small))):
            high = small[k].astype(BF).astype(F32)
            values = values + [high, small[k] - high]
        block = jnp.zeros((extra, channels), F32)
        for k, value in enumerate(values):
            block = jnp.where(place == k, value, block)
        sent_ref[slot, near + rows : near + rows + extra] = block.astype(BF)


def block_on_tile(place, padded, grad, grad_hidden, *params):
    rows, columns, channels = grad.shape
    slots, depth = params[-2:]
    return pl.pallas_call(
        block_kernel,
        out_shape=(
            jax.ShapeDtypeStruct(grad_hidden.shape, BF),
            jax.ShapeDtypeStruct((slots, depth, channels), BF),
            jax.ShapeDtypeStruct(grad.shape, F32),
        ),
        in_specs=[pl.BlockSpec(memory_space=pltpu.SMEM)]
        + [pl.BlockSpec(memory_space=pltpu.VMEM)] * 9,
        out_specs=(pl.BlockSpec(memory_space=pltpu.VMEM),) * 3,
        scratch_shapes=[pltpu.VMEM((rows + 2, columns + 8, channels), F32)],
        compiler_params=pltpu.CompilerParams(vmem_limit_bytes=24 * 1024 * 1024),
        name="block",
    )(place, padded, grad, grad_hidden, *params[:-2])


def share_kernel(scale, few, many, got_ref, share_ref):
    total, channels = share_ref.shape
    spare = got_ref.shape[1] - 4
    weights = jnp.zeros((many, channels), F32)
    rest = jnp.zeros((4, channels), F32)
    for k in range(got_ref.shape[0]):
        weights = weights + got_ref[k, 0:many].astype(F32)
        rest = rest + got_ref[k, spare - 4 : spare + 4].astype(F32)[4:8]
    parts = [weights * scale]
    for k in range(few):
        small = (rest[2 * k : 2 * k + 1] + rest[2 * k + 1 : 2 * k + 2]) * scale
        high = small.astype(BF).astype(F32)
        parts += [high, small - high]
    block = jnp.concatenate(parts * 8).astype(BF)
    depth = block.shape[0]
    for k in range(0, total, depth):
        share_ref[k : k + depth] = block


def share_of(got, slots, many, few, scale):
    channels = got.shape[2]
    return pl.pallas_call(
        functools.partial(share_kernel, scale, few, many),
        out_shape=jax.ShapeDtypeStruct((slots * (many + 2 * few), channels), BF),
        in_specs=[pl.BlockSpec(memory_space=pltpu.VMEM)],
        out_specs=pl.BlockSpec(memory_space=pltpu.VMEM),
        compiler_params=pltpu.CompilerParams(vmem_limit_bytes=8 * 1024 * 1024),
        name="share",
    )(got)


def finish_kernel(many, few, got_ref, *out_refs):
    tap_ref, bias_ref, gain_ref, shift_ref, expand_ref, expand_bias_ref, reduce_ref, reduce_bias_ref = (
        out_refs
    )
    total, channels = got_ref.shape
    hid = reduce_ref.shape[0]
    depth = many + 2 * few
    small = []
    for start in range(0, total, 8 * depth):
        block = got_ref[start : start + 8 * depth].astype(F32)
        for k in range(8):
            slot = start // depth + k
            part = block[k * depth : (k + 1) * depth]
            row = slot * many
            if row < hid:
                lane, row = row // channels * channels, row % channels
                expand_ref[row : row + many, lane : lane + channels] = part[:many]
            else:
                reduce_ref[row - hid : row - hid + many] = part[:many]
            if slot % 2 == 0:
                rest = part[many:]
                small += [rest[2 * k : 2 * k + 1] + rest[2 * k + 1 : 2 * k + 2] for k in range(few)]
    blocks = hid // channels
    for k in range(9):
        tap_ref[k // 3, k % 3 : k % 3 + 1] = small[k]
    bias_ref[...] = small[9]
    gain_ref[...] = small[10]
    shift_ref[...] = small[11]
    for k in range(blocks):
        expand_bias_ref[:, k * channels : (k + 1) * channels] = small[12 + k]
    reduce_bias_ref[...] = small[12 + blocks]


def finish(got, hid, many, few):
    channels = got.shape[1]
    shapes = [(3, 3, channels)] + [(1, channels)] * 3
    shapes += [(channels, hid), (1, hid), (hid, channels), (1, channels)]
    return pl.pallas_call(
        functools.partial(finish_kernel, many, few),
        out_shape=tuple(jax.ShapeDtypeStruct(shape, F32) for shape in shapes),
        in_specs=[pl.BlockSpec(memory_space=pltpu.VMEM)],
        out_specs=(pl.BlockSpec(memory_space=pltpu.VMEM),) * len(shapes),
        compiler_params=pltpu.CompilerParams(vmem_limit_bytes=16 * 1024 * 1024),
        name="finish",
    )(got)


def swap(slots, groups):
    return lax.all_to_all(slots, ("face", "row", "col"), 0, 0, axis_index_groups=groups)


def at(slots, index):
    return lax.dynamic_index_in_dim(slots, index, 0, keepdims=False)


def device_groups(side):
    cut = math.isqrt(side)
    steps = range(cut)

    def device(f, y, x, high, low):
        return (f * side + y * cut + low) * side + high * cut + x

    planes = [
        [device(f, y, x, high, low) for f in range(2) for y in steps for x in steps]
        for high in steps
        for low in steps
    ]
    lines = [
        [device(f, y, x, high, low) for high in steps for low in steps]
        for f in range(2)
        for y in steps
        for x in steps
    ]
    doubles = [
        [device(f, y, x, high, low + k) for f in range(2) for y in steps for x in steps for k in range(2)]
        for high in steps
        for low in range(0, cut, 2)
    ]
    return planes, lines, doubles


def frame_sources(entries, f, y, x, sender, target, step, side, cells):
    cut = math.isqrt(side)
    last, width, low_bits, cell_bits = side - 1, side * cells, cut - 1, cells - 1
    shift, cell_shift = low_bits.bit_length(), cell_bits.bit_length()
    high, low = sender >> shift, sender & low_bits
    row, col = y * cut + (target & low_bits), (target >> shift) * cut + x
    virtual = (step < 0) | (step >= cells)

    def held(face, tile_row, tile_col, part, cell, valid):
        valid = valid & ((tile_row & low_bits) == low) & ((tile_col >> shift) == high)
        slot = face * side + ((tile_row >> shift) << shift) + (tile_col & low_bits)
        inner = part * cells + cell
        end = 2 * cells + 2 * part + jnp.where(cell == 0, 0, 1)
        inner_index = slot * (2 * cells) + inner
        end_index = slot * (2 * cells + 8) + jnp.where(virtual, end, inner)
        return jnp.where(valid, inner_index, -1), jnp.where(valid, end_index, -1)

    def glued(edge, along, on_rows):
        other_edge, reverse = entries[edge]
        position = along * cells + step
        turned = jnp.where(reverse == 1, width - 1 - position, position)
        valid = (position >= 0) & (position < width)
        tile, cell = turned >> cell_shift, turned & cell_bits
        if on_rows:
            end = jnp.where(other_edge == 2, 0, last)
            return held(1 - f, tile, end, 1, cell, valid)
        end = jnp.where(other_edge == 0, 0, last)
        return held(1 - f, end, tile, 0, cell, valid)

    def beside(next_row, far_cell, own_part):
        position = col * cells + step
        valid = (position >= 0) & (position < width)
        tile, cell = position >> cell_shift, position & cell_bits
        level = (next_row >> shift) == y
        part = jnp.where(level & (step >= 0) & (step < cells), own_part, 0)
        cell = jnp.where(level & virtual, far_cell, cell)
        return held(f, next_row, tile, part, cell, valid)

    def either(condition, first, second):
        return tuple(jnp.where(condition, p, q) for p, q in zip(first, second))

    inner = (step >= 0) & (step < cells)
    nothing = (-1, -1)
    top = either(row == 0, glued(0, col, True), beside(row - 1, cells - 1, 1))
    bottom = either(row == last, glued(1, col, True), beside(row + 1, 0, 0))
    west = either(col == 0, glued(2, row, False), held(f, row, col - 1, 0, step, inner))
    east = either(col == last, glued(3, row, False), held(f, row, col + 1, 0, step, inner))
    return [top, bottom, either(x == 0, west, nothing), either(x == cut - 1, east, nothing)]


def two_sides(sources):
    need = [jnp.max(source[1].astype(F32), axis=-1, keepdims=True) >= 0.0 for source in sources]
    near = jnp.where(need[0], 0, jnp.where(need[1], 1, jnp.where(need[2], 2, 3)))
    after_one = jnp.where(need[2], 2, 3)
    far = jnp.where(
        need[0], jnp.where(need[1], 1, after_one), jnp.where(need[1], after_one, jnp.where(need[2], 3, 2))
    )
    return near, far


def plan_arrays(entries, f, r, c, side, cells):
    cut = math.isqrt(side)
    y, x = r // cut, c % cut
    here = c // cut * cut + r % cut
    others = lax.broadcasted_iota(jnp.int32, (side, 128), 0)
    lane = lax.broadcasted_iota(jnp.int32, (side, 128), 1)
    main = lane < 2 * cells
    step = jnp.where(main, lane & (cells - 1), jnp.where((lane & 1) == 0, -1, cells))
    second = jnp.where(main, lane - cells, lane - 2 * cells - 2) >= 0
    used = lane < 2 * cells + 4
    sources = frame_sources(entries, f, y, x, here, others, step, side, cells)
    near, far = two_sides(sources)
    which = jnp.where(second, far, near)
    passed = []
    for form in range(2):
        index = jnp.where(
            which == 0,
            sources[0][form],
            jnp.where(
                which == 1, sources[1][form], jnp.where(which == 2, sources[2][form], sources[3][form])
            ),
        )
        passed.append(jnp.where(used, index, -1))
    sources = frame_sources(entries, f, y, x, others, here, step, side, cells)
    near, far = two_sides(sources)
    which = jnp.where(second, far, near)
    return passed[0], passed[1], jnp.where(used, which * (cells + 2) + step + 1, -1)


def plan_kernel(side, cells, place_ref, adjacency_ref, plan_ref):
    f = place_ref[0]
    entries = [
        (adjacency_ref[f * 12 + 3 * edge + 1], adjacency_ref[f * 12 + 3 * edge + 2])
        for edge in range(4)
    ]
    arrays = plan_arrays(entries, f, place_ref[1], place_ref[2], side, cells)
    for k, array in enumerate(arrays):
        plan_ref[k] = array


def plan_of(place, adjacency, side, cells):
    return pl.pallas_call(
        functools.partial(plan_kernel, side, cells),
        out_shape=jax.ShapeDtypeStruct((3, side, 128), jnp.int32),
        in_specs=[pl.BlockSpec(memory_space=pltpu.SMEM)] * 2,
        out_specs=pl.BlockSpec(memory_space=pltpu.VMEM),
        compiler_params=pltpu.CompilerParams(vmem_limit_bytes=4 * 1024 * 1024),
        name="plan",
    )(place, adjacency.reshape(-1))


def picked(wanted, held):
    chosen = (wanted.reshape(-1, 1) == jnp.arange(held.shape[0], dtype=jnp.int32)).astype(BF)
    cells = jnp.dot(chosen, held, preferred_element_type=F32).astype(BF)
    return cells.reshape(wanted.shape + held.shape[1:])


def on_device(
    fields,
    conv_kernel,
    conv_bias,
    norm_gain,
    norm_bias,
    expand_weight,
    expand_bias,
    reduce_weight,
    reduce_bias,
    adjacency,
    out_grad,
):
    tile = fields[0]
    cells = tile.shape[0]
    channels = tile.shape[2]
    hid = expand_weight.shape[1]
    side = lax.axis_size("row")
    width = side * cells
    rim = cells + 2
    cut = math.isqrt(side)
    f = lax.axis_index("face")
    r = lax.axis_index("row")
    c = lax.axis_index("col")
    y, x = r // cut, c % cut
    planes, lines, doubles = device_groups(side)
    place = jnp.stack([f, r, c]).astype(jnp.int32)
    few = -(-(13 + hid // channels) // (2 * side))
    extra = 8
    assert 2 * few <= 4 and cells & (cells - 1) == 0 and cut & (cut - 1) == 0

    plan = plan_of(place, adjacency, side, cells)
    inner_wanted = plan[0, :, : 2 * cells + 4]
    end_wanted = plan[1, :, : 2 * cells + extra]
    frame_rows = jnp.arange(4 * rim, dtype=jnp.int32)[:, None]

    def frame_of(strips):
        depth = strips.shape[1]
        arrival = plan[2, :, :depth].reshape(1, -1)
        flat = strips.reshape(-1, channels)
        gather_frame = (frame_rows == arrival).astype(BF)
        return jnp.dot(gather_frame, flat, preferred_element_type=F32).reshape(4, rim, channels)

    def direct(strips, frame):
        base = f * side + y * cut
        west = at(strips, base + jnp.maximum(x - 1, 0)).astype(F32)
        east = at(strips, base + jnp.minimum(x + 1, cut - 1)).astype(F32)
        return jnp.where(x == 0, frame[2], west), jnp.where(x == cut - 1, frame[3], east)

    got = swap(edges_of(place, tile, 2 * side), planes)
    passed = picked(inner_wanted, got.reshape(-1, channels))
    passed = swap(passed.reshape(side, -1, 4, channels), lines)
    frame = frame_of(passed.reshape(side, 2 * cells + 4, channels))
    west, east = direct(got[:, :cells], frame[:, 1:-1])
    ends = frame[2:, ::rim - 1]
    top = jnp.concatenate(
        [frame[0, :1] + ends[0, :1], frame[0, 1:-1], frame[0, -1:] + ends[1, :1]]
    ).astype(BF)
    bottom = jnp.concatenate(
        [frame[1, :1] + ends[0, 1:], frame[1, 1:-1], frame[1, -1:] + ends[1, 1:]]
    ).astype(BF)
    padded = jnp.concatenate(
        [
            top[None],
            jnp.concatenate([west.astype(BF)[:, None], tile, east.astype(BF)[:, None]], axis=1),
            bottom[None],
        ]
    )

    many = 2 * hid // (2 * side)
    grad_cells = out_grad[0].reshape(cells * cells, channels)
    grad_hidden = lax.dot_general(
        grad_cells, reduce_weight, (((1,), (1,)), ((), ())), preferred_element_type=F32
    )
    hidden, sent, base_grad = block_on_tile(
        place,
        padded,
        out_grad[0],
        grad_hidden,
        conv_kernel.reshape(9, channels),
        conv_bias.reshape(1, channels),
        norm_gain.reshape(1, channels),
        norm_bias.reshape(1, channels),
        expand_weight,
        expand_bias.reshape(1, hid),
        2 * side,
        many + 2 * cells + extra,
    )
    block_out = (
        tile.reshape(cells * cells, channels).astype(F32)
        + jnp.dot(hidden, reduce_weight, preferred_element_type=F32)
        + reduce_bias
    ).astype(BF)
    got = swap(sent, planes)

    def pairs(small):
        high = small.astype(BF)
        low = (small - high.astype(F32)).astype(BF)
        return jnp.stack([high, low], axis=-2).reshape(2 * few, channels)

    def small_total(rest):
        sums = jnp.sum(rest.astype(F32), axis=0).reshape(few, 2, channels)
        return sums[:, 0] + sums[:, 1]

    half = many // 2
    spare = many + 2 * cells + 4
    weights = jnp.sum(got[:, :many].astype(F32), axis=0)
    small = small_total(got[:, spare : spare + 2 * few])
    strips = got[:, many:]
    passed = picked(end_wanted, strips.reshape(-1, channels))
    tail = jnp.pad(pairs(small), ((0, 4 - 2 * few), (0, 0)))
    sent = jnp.concatenate(
        [
            jnp.tile(weights.astype(BF).reshape(2, half, channels), (side // 2, 1, 1)),
            passed[:, : 2 * cells],
            jnp.concatenate(
                [passed[:, 2 * cells : 2 * cells + 4], jnp.broadcast_to(tail, (side, 4, channels))],
                axis=1,
            ),
        ],
        axis=1,
    )
    got = swap(sent, lines)
    share = share_of(got, 4 * side, half, few, 1.0 / width)
    spread = swap(share.reshape(4 * side, -1, 2, channels), doubles).reshape(share.shape)

    frame = frame_of(got[:, half:])
    folded = frame[:, 1:-1]
    folded = folded.at[:, 0].add(frame[:, 0]).at[:, -1].add(frame[:, -1])
    west, east = direct(strips[:, :cells], folded)
    in_grad = base_grad
    in_grad = in_grad + jnp.pad(folded[:1], ((0, cells - 1), (0, 0), (0, 0)))
    in_grad = in_grad + jnp.pad(folded[1:2], ((cells - 1, 0), (0, 0), (0, 0)))
    in_grad = in_grad + jnp.pad(west[:, None], ((0, 0), (0, cells - 1), (0, 0)))
    in_grad = in_grad + jnp.pad(east[:, None], ((0, 0), (cells - 1, 0), (0, 0)))

    taps, bias, gain, shift, expand, expand_vector, reduce, reduce_vector = finish(spread, hid, half, few)
    return (
        block_out.reshape(1, cells, cells, channels),
        in_grad.astype(BF)[None],
        taps,
        bias.reshape(channels),
        gain.reshape(channels),
        shift.reshape(channels),
        expand,
        expand_vector.reshape(hid),
        reduce,
        reduce_vector.reshape(channels),
    )


def solution(mesh):
    tiles = P("face", "row", "col", None)
    in_specs = (tiles,) + (P(),) * 9 + (tiles,)
    out_specs = (tiles, tiles) + (P(),) * 8
    return jax.shard_map(
        on_device, mesh=mesh, in_specs=in_specs, out_specs=out_specs, check_vma=False
    )
```

```python
import functools
import math

import jax
import jax.numpy as jnp
from jax import lax
from jax.experimental import pallas as pl
from jax.experimental.pallas import tpu as pltpu
from jax.sharding import PartitionSpec as P

GELU_SCALE = math.sqrt(2.0 / math.pi)
NORM_EPS = 1e-06
BF = jnp.bfloat16
F32 = jnp.float32


def gelu_pair(preact):
    cubic_term = preact + 0.044715 * preact * preact * preact
    tangent = jnp.tanh(GELU_SCALE * cubic_term)
    gelu_value = 0.5 * preact * (1.0 + tangent)
    gelu_slope = 0.5 * (1.0 + tangent) + 0.5 * preact * (1.0 - tangent * tangent) * GELU_SCALE * (
        1.0 + 3.0 * 0.044715 * preact * preact
    )
    return (gelu_value, gelu_slope)


def slot_strips(face, row, col, slot, side, north, south, west, east):
    cut = math.isqrt(side)
    here_y, here_x = row // cut, col % cut
    same = face == slot // side
    y, x = slot % side // cut, slot % cut
    level = jnp.where(
        x == (here_x + cut - 1) % cut, west, jnp.where(x == (here_x + 1) % cut, east, north)
    )
    inner = jnp.where(y < here_y, north, jnp.where(y > here_y, south, level))
    near = jnp.where(same, inner, jnp.where(row == 0, north, south))
    far = jnp.where(same, south, jnp.where(col == 0, west, east))
    return near, far


def edges_kernel(place_ref, tile_ref, sent_ref):
    slots, depth, _ = sent_ref.shape
    rows = depth // 2
    tile = tile_ref[...].astype(F32)
    north, south = tile[0], tile[rows - 1]
    west = jnp.concatenate([tile[k, 0:1] for k in range(rows)])
    east = jnp.concatenate([tile[k, rows - 1 : rows] for k in range(rows)])
    for slot in range(slots):
        near, far = slot_strips(
            place_ref[0], place_ref[1], place_ref[2], slot, slots // 2, north, south, west, east
        )
        sent_ref[slot, 0:rows] = near.astype(BF)
        sent_ref[slot, rows:depth] = far.astype(BF)


def edges_of(place, tile, slots):
    rows, _, channels = tile.shape
    return pl.pallas_call(
        edges_kernel,
        out_shape=jax.ShapeDtypeStruct((slots, 2 * rows, channels), BF),
        in_specs=[
            pl.BlockSpec(memory_space=pltpu.SMEM),
            pl.BlockSpec(memory_space=pltpu.VMEM),
        ],
        out_specs=pl.BlockSpec(memory_space=pltpu.VMEM),
        compiler_params=pltpu.CompilerParams(vmem_limit_bytes=8 * 1024 * 1024),
        name="edges",
    )(place, tile)


def block_kernel(
    plan_ref,
    padded_ref,
    grad_ref,
    grad_hidden_ref,
    tap_ref,
    conv_bias_ref,
    gain_ref,
    shift_ref,
    expand_ref,
    expand_bias_ref,
    hidden_ref,
    sent_ref,
    base_ref,
    wide_ref,
):
    rows, columns, channels = grad_ref.shape
    count = rows * columns
    rim = rows + 2
    hid = expand_ref.shape[1]
    slots, _, _ = sent_ref.shape
    side = slots // 2
    padded = padded_ref[...].astype(F32)
    shifted = [padded[:, b : b + columns] for b in range(3)]

    mixed = jnp.zeros((rows, columns, channels), F32) + conv_bias_ref[...].reshape(1, 1, channels)
    for a in range(3):
        for b in range(3):
            mixed = mixed + tap_ref[3 * a + b].reshape(1, 1, channels) * shifted[b][a : a + rows]
    mixed = mixed.reshape(count, channels)
    center = mixed - jnp.mean(mixed, axis=-1, keepdims=True)
    inv_std = lax.rsqrt(jnp.mean(center * center, axis=-1, keepdims=True) + NORM_EPS)
    normalized = center * inv_std
    normed = (normalized * gain_ref[...] + shift_ref[...]).astype(BF)
    preact = jnp.dot(normed, expand_ref[...], preferred_element_type=F32) + expand_bias_ref[...]
    gelu_value, gelu_slope = gelu_pair(preact)
    hidden = gelu_value.astype(BF)
    hidden_ref[...] = hidden
    grad_cells = grad_ref[...].reshape(count, channels)
    grad_preact = (grad_hidden_ref[...] * gelu_slope).astype(BF)
    grad_normed = lax.dot_general(
        grad_preact, expand_ref[...], (((1,), (1,)), ((), ())), preferred_element_type=F32
    )
    scaled = grad_normed * gain_ref[...]
    grad_mixed = inv_std * (
        scaled
        - jnp.mean(scaled, axis=-1, keepdims=True)
        - normalized * jnp.mean(scaled * normalized, axis=-1, keepdims=True)
    )

    def total(cells):
        return jnp.sum(cells, axis=0, keepdims=True)

    square = grad_mixed.reshape(rows, columns, channels)
    small = [
        total((square * shifted[b][a : a + rows]).reshape(count, channels))
        for a in range(3)
        for b in range(3)
    ]
    small += [total(grad_mixed), total(grad_normed * normalized), total(grad_normed)]
    preact_total = total(grad_preact.astype(F32))
    small += [preact_total[:, k : k + channels] for k in range(0, hid, channels)]
    small += [total(grad_cells.astype(F32))]

    across = (((0,), (0,)), ((), ()))
    expand_sum = lax.dot_general(normed, grad_preact, across, preferred_element_type=F32).astype(BF)
    reduce_sum = lax.dot_general(hidden, grad_cells, across, preferred_element_type=F32).astype(BF)
    many = 2 * hid // slots
    for k in range(0, hid, channels):
        for j in range(0, channels, many):
            sent_ref[(k + j) // many, 0:many] = expand_sum[j : j + many, k : k + channels]
    for k in range(0, hid, many):
        sent_ref[(hid + k) // many, 0:many] = reduce_sum[k : k + many]

    wide_ref[...] = jnp.zeros(wide_ref.shape, F32)
    for b in range(3):
        parts = [tap_ref[3 * a + b].reshape(1, 1, channels) * square for a in range(3)]
        wide_ref[0, b : b + columns] += parts[0][0]
        wide_ref[1, b : b + columns] += parts[0][1] + parts[1][0]
        wide_ref[2:rows, b : b + columns] += (
            parts[0][2:] + parts[1][1 : rows - 1] + parts[2][: rows - 2]
        )
        wide_ref[rows, b : b + columns] += parts[1][rows - 1] + parts[2][rows - 2]
        wide_ref[rows + 1, b : b + columns] += parts[2][rows - 1]
    base_ref[...] = grad_ref[...].astype(F32) + wide_ref[1 : rows + 1, 1 : columns + 1]
    west = jnp.concatenate([wide_ref[k, 0:1] for k in range(rim)])
    east = jnp.concatenate([wide_ref[k, rim - 1 : rim] for k in range(rim)])
    north = wide_ref[0, 0:rim]
    south = wide_ref[rim - 1, 0:rim]

    face, row, col = plan_ref[0], plan_ref[1], plan_ref[2]
    few = -(-len(small) // slots)
    extra = sent_ref.shape[1] - many - 2 * rows
    place = lax.broadcasted_iota(jnp.int32, (extra, channels), 0)
    near = many + rows
    for slot in range(slots):
        strip, side_strip = slot_strips(face, row, col, slot, side, north, south, west, east)
        sent_ref[slot, many:near] = strip[1 : rim - 1].astype(BF)
        sent_ref[slot, near : near + rows] = side_strip[1 : rim - 1].astype(BF)
        ends = [strip[0:1], strip[rim - 1 : rim], side_strip[0:1], side_strip[rim - 1 : rim]]
        values = ends
        for k in range(few * slot, min(few * slot + few, len(small))):
            high = small[k].astype(BF).astype(F32)
            values = values + [high, small[k] - high]
        block = jnp.zeros((extra, channels), F32)
        for k, value in enumerate(values):
            block = jnp.where(place == k, value, block)
        sent_ref[slot, near + rows : near + rows + extra] = block.astype(BF)


def block_on_tile(place, padded, grad, grad_hidden, *params):
    rows, columns, channels = grad.shape
    slots, depth = params[-2:]
    return pl.pallas_call(
        block_kernel,
        out_shape=(
            jax.ShapeDtypeStruct(grad_hidden.shape, BF),
            jax.ShapeDtypeStruct((slots, depth, channels), BF),
            jax.ShapeDtypeStruct(grad.shape, F32),
        ),
        in_specs=[pl.BlockSpec(memory_space=pltpu.SMEM)]
        + [pl.BlockSpec(memory_space=pltpu.VMEM)] * 9,
        out_specs=(pl.BlockSpec(memory_space=pltpu.VMEM),) * 3,
        scratch_shapes=[pltpu.VMEM((rows + 2, columns + 8, channels), F32)],
        compiler_params=pltpu.CompilerParams(vmem_limit_bytes=24 * 1024 * 1024),
        name="block",
    )(place, padded, grad, grad_hidden, *params[:-2])


def share_kernel(scale, few, many, got_ref, share_ref):
    total, channels = share_ref.shape
    spare = got_ref.shape[1] - 4
    weights = jnp.zeros((many, channels), F32)
    rest = jnp.zeros((4, channels), F32)
    for k in range(got_ref.shape[0]):
        weights = weights + got_ref[k, 0:many].astype(F32)
        rest = rest + got_ref[k, spare - 4 : spare + 4].astype(F32)[4:8]
    parts = [weights * scale]
    for k in range(few):
        small = (rest[2 * k : 2 * k + 1] + rest[2 * k + 1 : 2 * k + 2]) * scale
        high = small.astype(BF).astype(F32)
        parts += [high, small - high]
    block = jnp.concatenate(parts * 8).astype(BF)
    depth = block.shape[0]
    for k in range(0, total, depth):
        share_ref[k : k + depth] = block


def share_of(got, slots, many, few, scale):
    channels = got.shape[2]
    return pl.pallas_call(
        functools.partial(share_kernel, scale, few, many),
        out_shape=jax.ShapeDtypeStruct((slots * (many + 2 * few), channels), BF),
        in_specs=[pl.BlockSpec(memory_space=pltpu.VMEM)],
        out_specs=pl.BlockSpec(memory_space=pltpu.VMEM),
        compiler_params=pltpu.CompilerParams(vmem_limit_bytes=8 * 1024 * 1024),
        name="share",
    )(got)


def finish_kernel(many, few, got_ref, *out_refs):
    tap_ref, bias_ref, gain_ref, shift_ref, expand_ref, expand_bias_ref, reduce_ref, reduce_bias_ref = (
        out_refs
    )
    total, channels = got_ref.shape
    hid = reduce_ref.shape[0]
    depth = many + 2 * few
    small = []
    for start in range(0, total, 8 * depth):
        block = got_ref[start : start + 8 * depth].astype(F32)
        for k in range(8):
            slot = start // depth + k
            part = block[k * depth : (k + 1) * depth]
            row = slot * many
            if row < hid:
                lane, row = row // channels * channels, row % channels
                expand_ref[row : row + many, lane : lane + channels] = part[:many]
            else:
                reduce_ref[row - hid : row - hid + many] = part[:many]
            rest = part[many:]
            small += [rest[2 * k : 2 * k + 1] + rest[2 * k + 1 : 2 * k + 2] for k in range(few)]
    blocks = hid // channels
    for k in range(9):
        tap_ref[k // 3, k % 3 : k % 3 + 1] = small[k]
    bias_ref[...] = small[9]
    gain_ref[...] = small[10]
    shift_ref[...] = small[11]
    for k in range(blocks):
        expand_bias_ref[:, k * channels : (k + 1) * channels] = small[12 + k]
    reduce_bias_ref[...] = small[12 + blocks]


def finish(got, hid, many, few):
    channels = got.shape[1]
    shapes = [(3, 3, channels)] + [(1, channels)] * 3
    shapes += [(channels, hid), (1, hid), (hid, channels), (1, channels)]
    return pl.pallas_call(
        functools.partial(finish_kernel, many, few),
        out_shape=tuple(jax.ShapeDtypeStruct(shape, F32) for shape in shapes),
        in_specs=[pl.BlockSpec(memory_space=pltpu.VMEM)],
        out_specs=(pl.BlockSpec(memory_space=pltpu.VMEM),) * len(shapes),
        compiler_params=pltpu.CompilerParams(vmem_limit_bytes=16 * 1024 * 1024),
        name="finish",
    )(got)


def swap(slots, groups):
    return lax.all_to_all(slots, ("face", "row", "col"), 0, 0, axis_index_groups=groups)


def at(slots, index):
    return lax.dynamic_index_in_dim(slots, index, 0, keepdims=False)


def device_groups(side):
    cut = math.isqrt(side)
    steps = range(cut)

    def device(f, y, x, high, low):
        return (f * side + y * cut + low) * side + high * cut + x

    planes = [
        [device(f, y, x, high, low) for f in range(2) for y in steps for x in steps]
        for high in steps
        for low in steps
    ]
    lines = [
        [device(f, y, x, high, low) for high in steps for low in steps]
        for f in range(2)
        for y in steps
        for x in steps
    ]
    return planes, lines


def frame_sources(entries, f, y, x, sender, target, step, side, cells):
    cut = math.isqrt(side)
    last, width, low_bits, cell_bits = side - 1, side * cells, cut - 1, cells - 1
    shift, cell_shift = low_bits.bit_length(), cell_bits.bit_length()
    high, low = sender >> shift, sender & low_bits
    row, col = y * cut + (target & low_bits), (target >> shift) * cut + x
    virtual = (step < 0) | (step >= cells)

    def held(face, tile_row, tile_col, part, cell, valid):
        valid = valid & ((tile_row & low_bits) == low) & ((tile_col >> shift) == high)
        slot = face * side + ((tile_row >> shift) << shift) + (tile_col & low_bits)
        inner = part * cells + cell
        end = 2 * cells + 2 * part + jnp.where(cell == 0, 0, 1)
        inner_index = slot * (2 * cells) + inner
        end_index = slot * (2 * cells + 8) + jnp.where(virtual, end, inner)
        return jnp.where(valid, inner_index, -1), jnp.where(valid, end_index, -1)

    def glued(edge, along, on_rows):
        other_edge, reverse = entries[edge]
        position = along * cells + step
        turned = jnp.where(reverse == 1, width - 1 - position, position)
        valid = (position >= 0) & (position < width)
        tile, cell = turned >> cell_shift, turned & cell_bits
        if on_rows:
            end = jnp.where(other_edge == 2, 0, last)
            return held(1 - f, tile, end, 1, cell, valid)
        end = jnp.where(other_edge == 0, 0, last)
        return held(1 - f, end, tile, 0, cell, valid)

    def beside(next_row, far_cell, own_part):
        position = col * cells + step
        valid = (position >= 0) & (position < width)
        tile, cell = position >> cell_shift, position & cell_bits
        level = (next_row >> shift) == y
        part = jnp.where(level & (step >= 0) & (step < cells), own_part, 0)
        cell = jnp.where(level & virtual, far_cell, cell)
        return held(f, next_row, tile, part, cell, valid)

    def either(condition, first, second):
        return tuple(jnp.where(condition, p, q) for p, q in zip(first, second))

    inner = (step >= 0) & (step < cells)
    nothing = (-1, -1)
    top = either(row == 0, glued(0, col, True), beside(row - 1, cells - 1, 1))
    bottom = either(row == last, glued(1, col, True), beside(row + 1, 0, 0))
    west = either(col == 0, glued(2, row, False), held(f, row, col - 1, 0, step, inner))
    east = either(col == last, glued(3, row, False), held(f, row, col + 1, 0, step, inner))
    return [top, bottom, either(x == 0, west, nothing), either(x == cut - 1, east, nothing)]


def two_sides(sources):
    need = [jnp.max(source[1].astype(F32), axis=-1, keepdims=True) >= 0.0 for source in sources]
    near = jnp.where(need[0], 0, jnp.where(need[1], 1, jnp.where(need[2], 2, 3)))
    after_one = jnp.where(need[2], 2, 3)
    far = jnp.where(
        need[0], jnp.where(need[1], 1, after_one), jnp.where(need[1], after_one, jnp.where(need[2], 3, 2))
    )
    return near, far


def plan_arrays(entries, f, r, c, side, cells):
    cut = math.isqrt(side)
    y, x = r // cut, c % cut
    here = c // cut * cut + r % cut
    others = lax.broadcasted_iota(jnp.int32, (side, 128), 0)
    lane = lax.broadcasted_iota(jnp.int32, (side, 128), 1)
    main = lane < 2 * cells
    step = jnp.where(main, lane & (cells - 1), jnp.where((lane & 1) == 0, -1, cells))
    second = jnp.where(main, lane - cells, lane - 2 * cells - 2) >= 0
    used = lane < 2 * cells + 4
    sources = frame_sources(entries, f, y, x, here, others, step, side, cells)
    near, far = two_sides(sources)
    which = jnp.where(second, far, near)
    passed = []
    for form in range(2):
        index = jnp.where(
            which == 0,
            sources[0][form],
            jnp.where(
                which == 1, sources[1][form], jnp.where(which == 2, sources[2][form], sources[3][form])
            ),
        )
        passed.append(jnp.where(used, index, -1))
    sources = frame_sources(entries, f, y, x, others, here, step, side, cells)
    near, far = two_sides(sources)
    which = jnp.where(second, far, near)
    return passed[0], passed[1], jnp.where(used, which * (cells + 2) + step + 1, -1)


def plan_kernel(side, cells, place_ref, adjacency_ref, plan_ref):
    f = place_ref[0]
    entries = [
        (adjacency_ref[f * 12 + 3 * edge + 1], adjacency_ref[f * 12 + 3 * edge + 2])
        for edge in range(4)
    ]
    arrays = plan_arrays(entries, f, place_ref[1], place_ref[2], side, cells)
    for k, array in enumerate(arrays):
        plan_ref[k] = array


def plan_of(place, adjacency, side, cells):
    return pl.pallas_call(
        functools.partial(plan_kernel, side, cells),
        out_shape=jax.ShapeDtypeStruct((3, side, 128), jnp.int32),
        in_specs=[pl.BlockSpec(memory_space=pltpu.SMEM)] * 2,
        out_specs=pl.BlockSpec(memory_space=pltpu.VMEM),
        compiler_params=pltpu.CompilerParams(vmem_limit_bytes=4 * 1024 * 1024),
        name="plan",
    )(place, adjacency.reshape(-1))


def choice(wanted, count):
    chosen = (wanted.reshape(-1, 1) == jnp.arange(count, dtype=jnp.int32)).astype(BF)
    return lax.optimization_barrier(chosen)


def picked(wanted, held):
    chosen = choice(wanted, held.shape[0])
    cells = jnp.dot(chosen, held, preferred_element_type=F32).astype(BF)
    return cells.reshape(wanted.shape + held.shape[1:])


def on_device(
    fields,
    conv_kernel,
    conv_bias,
    norm_gain,
    norm_bias,
    expand_weight,
    expand_bias,
    reduce_weight,
    reduce_bias,
    adjacency,
    out_grad,
):
    tile = fields[0]
    cells = tile.shape[0]
    channels = tile.shape[2]
    hid = expand_weight.shape[1]
    side = lax.axis_size("row")
    width = side * cells
    rim = cells + 2
    cut = math.isqrt(side)
    f = lax.axis_index("face")
    r = lax.axis_index("row")
    c = lax.axis_index("col")
    y, x = r // cut, c % cut
    planes, lines = device_groups(side)
    place = jnp.stack([f, r, c]).astype(jnp.int32)
    few = -(-(13 + hid // channels) // (2 * side))
    extra = 8
    assert 2 * few <= 4 and cells & (cells - 1) == 0 and cut & (cut - 1) == 0

    plan = plan_of(place, adjacency, side, cells)
    inner_wanted = plan[0, :, : 2 * cells + 4]
    end_wanted = plan[1, :, : 2 * cells + extra]
    frame_rows = jnp.arange(4 * rim, dtype=jnp.int32)[:, None]

    def frame_of(strips):
        depth = strips.shape[1]
        arrival = plan[2, :, :depth].reshape(1, -1)
        flat = strips.reshape(-1, channels)
        gather_frame = (frame_rows == arrival).astype(BF)
        return jnp.dot(gather_frame, flat, preferred_element_type=F32).reshape(4, rim, channels)

    def direct(strips, frame):
        base = f * side + y * cut
        west = at(strips, base + jnp.maximum(x - 1, 0)).astype(F32)
        east = at(strips, base + jnp.minimum(x + 1, cut - 1)).astype(F32)
        return jnp.where(x == 0, frame[2], west), jnp.where(x == cut - 1, frame[3], east)

    got = swap(edges_of(place, tile, 2 * side), planes)
    passed = picked(inner_wanted, got.reshape(-1, channels))
    passed = swap(passed.reshape(side, -1, 4, channels), lines)
    frame = frame_of(passed.reshape(side, 2 * cells + 4, channels))
    west, east = direct(got[:, :cells], frame[:, 1:-1])
    ends = frame[2:, ::rim - 1]
    top = jnp.concatenate(
        [frame[0, :1] + ends[0, :1], frame[0, 1:-1], frame[0, -1:] + ends[1, :1]]
    ).astype(BF)
    bottom = jnp.concatenate(
        [frame[1, :1] + ends[0, 1:], frame[1, 1:-1], frame[1, -1:] + ends[1, 1:]]
    ).astype(BF)
    padded = jnp.concatenate(
        [
            top[None],
            jnp.concatenate([west.astype(BF)[:, None], tile, east.astype(BF)[:, None]], axis=1),
            bottom[None],
        ]
    )

    many = 2 * hid // (2 * side)
    grad_cells = out_grad[0].reshape(cells * cells, channels)
    grad_hidden = lax.dot_general(
        grad_cells, reduce_weight, (((1,), (1,)), ((), ())), preferred_element_type=F32
    )
    hidden, sent, base_grad = block_on_tile(
        place,
        padded,
        out_grad[0],
        grad_hidden,
        conv_kernel.reshape(9, channels),
        conv_bias.reshape(1, channels),
        norm_gain.reshape(1, channels),
        norm_bias.reshape(1, channels),
        expand_weight,
        expand_bias.reshape(1, hid),
        2 * side,
        many + 2 * cells + extra,
    )
    block_out = (
        tile.reshape(cells * cells, channels).astype(F32)
        + jnp.dot(hidden, reduce_weight, preferred_element_type=F32)
        + reduce_bias
    ).astype(BF)
    got = swap(sent, planes)

    def pairs(small):
        high = small.astype(BF)
        low = (small - high.astype(F32)).astype(BF)
        return jnp.stack([high, low], axis=-2).reshape(2 * few, channels)

    def small_total(rest):
        sums = jnp.sum(rest.astype(F32), axis=0).reshape(few, 2, channels)
        return sums[:, 0] + sums[:, 1]

    spare = many + 2 * cells + 4
    weights = jnp.sum(got[:, :many].astype(F32), axis=0)
    small = small_total(got[:, spare : spare + 2 * few])
    strips = got[:, many:]
    passed = picked(end_wanted, strips.reshape(-1, channels))
    tail = jnp.pad(pairs(small), ((0, 4 - 2 * few), (0, 0)))
    sent = jnp.concatenate(
        [
            jnp.broadcast_to(weights.astype(BF), (side, many, channels)),
            passed[:, : 2 * cells],
            jnp.concatenate(
                [passed[:, 2 * cells : 2 * cells + 4], jnp.broadcast_to(tail, (side, 4, channels))],
                axis=1,
            ),
        ],
        axis=1,
    )
    got = swap(sent, lines)
    share = share_of(got, 2 * side, many, few, 1.0 / width)
    spread = swap(share.reshape(2 * side, -1, 2, channels), planes).reshape(share.shape)

    frame = frame_of(got[:, many:])
    folded = frame[:, 1:-1]
    folded = folded.at[:, 0].add(frame[:, 0]).at[:, -1].add(frame[:, -1])
    west, east = direct(strips[:, :cells], folded)
    in_grad = base_grad
    in_grad = in_grad + jnp.pad(folded[:1], ((0, cells - 1), (0, 0), (0, 0)))
    in_grad = in_grad + jnp.pad(folded[1:2], ((cells - 1, 0), (0, 0), (0, 0)))
    in_grad = in_grad + jnp.pad(west[:, None], ((0, 0), (0, cells - 1), (0, 0)))
    in_grad = in_grad + jnp.pad(east[:, None], ((0, 0), (cells - 1, 0), (0, 0)))

    taps, bias, gain, shift, expand, expand_vector, reduce, reduce_vector = finish(spread, hid, many, few)
    return (
        block_out.reshape(1, cells, cells, channels),
        in_grad.astype(BF)[None],
        taps,
        bias.reshape(channels),
        gain.reshape(channels),
        shift.reshape(channels),
        expand,
        expand_vector.reshape(hid),
        reduce,
        reduce_vector.reshape(channels),
    )


def solution(mesh):
    tiles = P("face", "row", "col", None)
    in_specs = (tiles,) + (P(),) * 9 + (tiles,)
    out_specs = (tiles, tiles) + (P(),) * 8
    return jax.shard_map(
        on_device, mesh=mesh, in_specs=in_specs, out_specs=out_specs, check_vma=False
    )
```

```python
import functools
import math

import jax
import jax.numpy as jnp
from jax import lax
from jax.experimental import pallas as pl
from jax.experimental.pallas import tpu as pltpu
from jax.sharding import PartitionSpec as P

GELU_SCALE = math.sqrt(2.0 / math.pi)
NORM_EPS = 1e-06
BF = jnp.bfloat16
F32 = jnp.float32


def gelu_pair(preact):
    cubic_term = preact + 0.044715 * preact * preact * preact
    tangent = jnp.tanh(GELU_SCALE * cubic_term)
    gelu_value = 0.5 * preact * (1.0 + tangent)
    gelu_slope = 0.5 * (1.0 + tangent) + 0.5 * preact * (1.0 - tangent * tangent) * GELU_SCALE * (
        1.0 + 3.0 * 0.044715 * preact * preact
    )
    return (gelu_value, gelu_slope)


def slot_strips(face, row, col, slot, side, north, south, west, east):
    cut = math.isqrt(side)
    here_y, here_x = row // cut, col % cut
    same = face == slot // side
    y, x = slot % side // cut, slot % cut
    level = jnp.where(
        x == (here_x + cut - 1) % cut, west, jnp.where(x == (here_x + 1) % cut, east, north)
    )
    inner = jnp.where(y < here_y, north, jnp.where(y > here_y, south, level))
    near = jnp.where(same, inner, jnp.where(row == 0, north, south))
    far = jnp.where(same, south, jnp.where(col == 0, west, east))
    return near, far


def edges_kernel(place_ref, tile_ref, sent_ref):
    slots, depth, _ = sent_ref.shape
    rows = depth // 2
    tile = tile_ref[...].astype(F32)
    north, south = tile[0], tile[rows - 1]
    west = jnp.concatenate([tile[k, 0:1] for k in range(rows)])
    east = jnp.concatenate([tile[k, rows - 1 : rows] for k in range(rows)])
    for slot in range(slots):
        near, far = slot_strips(
            place_ref[0], place_ref[1], place_ref[2], slot, slots // 2, north, south, west, east
        )
        sent_ref[slot, 0:rows] = near.astype(BF)
        sent_ref[slot, rows:depth] = far.astype(BF)


def edges_of(place, tile, slots):
    rows, _, channels = tile.shape
    return pl.pallas_call(
        edges_kernel,
        out_shape=jax.ShapeDtypeStruct((slots, 2 * rows, channels), BF),
        in_specs=[
            pl.BlockSpec(memory_space=pltpu.SMEM),
            pl.BlockSpec(memory_space=pltpu.VMEM),
        ],
        out_specs=pl.BlockSpec(memory_space=pltpu.VMEM),
        compiler_params=pltpu.CompilerParams(vmem_limit_bytes=8 * 1024 * 1024),
        name="edges",
    )(place, tile)


def block_kernel(
    plan_ref,
    padded_ref,
    grad_ref,
    grad_hidden_ref,
    tap_ref,
    conv_bias_ref,
    gain_ref,
    shift_ref,
    expand_ref,
    expand_bias_ref,
    hidden_ref,
    sent_ref,
    base_ref,
    wide_ref,
):
    rows, columns, channels = grad_ref.shape
    count = rows * columns
    rim = rows + 2
    hid = expand_ref.shape[1]
    slots, _, _ = sent_ref.shape
    side = slots // 2
    padded = padded_ref[...].astype(F32)
    shifted = [padded[:, b : b + columns] for b in range(3)]

    mixed = jnp.zeros((rows, columns, channels), F32) + conv_bias_ref[...].reshape(1, 1, channels)
    for a in range(3):
        for b in range(3):
            mixed = mixed + tap_ref[3 * a + b].reshape(1, 1, channels) * shifted[b][a : a + rows]
    mixed = mixed.reshape(count, channels)
    center = mixed - jnp.mean(mixed, axis=-1, keepdims=True)
    inv_std = lax.rsqrt(jnp.mean(center * center, axis=-1, keepdims=True) + NORM_EPS)
    normalized = center * inv_std
    normed = (normalized * gain_ref[...] + shift_ref[...]).astype(BF)
    preact = jnp.dot(normed, expand_ref[...], preferred_element_type=F32) + expand_bias_ref[...]
    gelu_value, gelu_slope = gelu_pair(preact)
    hidden = gelu_value.astype(BF)
    hidden_ref[...] = hidden
    grad_cells = grad_ref[...].reshape(count, channels)
    grad_preact = (grad_hidden_ref[...] * gelu_slope).astype(BF)
    grad_normed = lax.dot_general(
        grad_preact, expand_ref[...], (((1,), (1,)), ((), ())), preferred_element_type=F32
    )
    scaled = grad_normed * gain_ref[...]
    grad_mixed = inv_std * (
        scaled
        - jnp.mean(scaled, axis=-1, keepdims=True)
        - normalized * jnp.mean(scaled * normalized, axis=-1, keepdims=True)
    )

    def total(cells):
        return jnp.sum(cells, axis=0, keepdims=True)

    square = grad_mixed.reshape(rows, columns, channels)
    small = [
        total((square * shifted[b][a : a + rows]).reshape(count, channels))
        for a in range(3)
        for b in range(3)
    ]
    small += [total(grad_mixed), total(grad_normed * normalized), total(grad_normed)]
    preact_total = total(grad_preact.astype(F32))
    small += [preact_total[:, k : k + channels] for k in range(0, hid, channels)]
    small += [total(grad_cells.astype(F32))]

    across = (((0,), (0,)), ((), ()))
    expand_sum = lax.dot_general(normed, grad_preact, across, preferred_element_type=F32).astype(BF)
    reduce_sum = lax.dot_general(hidden, grad_cells, across, preferred_element_type=F32).astype(BF)
    many = 2 * hid // slots
    for k in range(0, hid, channels):
        for j in range(0, channels, many):
            sent_ref[(k + j) // many, 0:many] = expand_sum[j : j + many, k : k + channels]
    for k in range(0, hid, many):
        sent_ref[(hid + k) // many, 0:many] = reduce_sum[k : k + many]

    wide_ref[...] = jnp.zeros(wide_ref.shape, F32)
    for b in range(3):
        parts = [tap_ref[3 * a + b].reshape(1, 1, channels) * square for a in range(3)]
        wide_ref[0, b : b + columns] += parts[0][0]
        wide_ref[1, b : b + columns] += parts[0][1] + parts[1][0]
        wide_ref[2:rows, b : b + columns] += (
            parts[0][2:] + parts[1][1 : rows - 1] + parts[2][: rows - 2]
        )
        wide_ref[rows, b : b + columns] += parts[1][rows - 1] + parts[2][rows - 2]
        wide_ref[rows + 1, b : b + columns] += parts[2][rows - 1]
    base_ref[...] = grad_ref[...].astype(F32) + wide_ref[1 : rows + 1, 1 : columns + 1]
    west = jnp.concatenate([wide_ref[k, 0:1] for k in range(rim)])
    east = jnp.concatenate([wide_ref[k, rim - 1 : rim] for k in range(rim)])
    north = wide_ref[0, 0:rim]
    south = wide_ref[rim - 1, 0:rim]

    face, row, col = plan_ref[0], plan_ref[1], plan_ref[2]
    few = -(-len(small) // slots)
    extra = sent_ref.shape[1] - many - 2 * rows
    place = lax.broadcasted_iota(jnp.int32, (extra, channels), 0)
    near = many + rows
    for slot in range(slots):
        strip, side_strip = slot_strips(face, row, col, slot, side, north, south, west, east)
        sent_ref[slot, many:near] = strip[1 : rim - 1].astype(BF)
        sent_ref[slot, near : near + rows] = side_strip[1 : rim - 1].astype(BF)
        ends = [strip[0:1], strip[rim - 1 : rim], side_strip[0:1], side_strip[rim - 1 : rim]]
        values = ends
        for k in range(few * slot, min(few * slot + few, len(small))):
            high = small[k].astype(BF).astype(F32)
            values = values + [high, small[k] - high]
        block = jnp.zeros((extra, channels), F32)
        for k, value in enumerate(values):
            block = jnp.where(place == k, value, block)
        sent_ref[slot, near + rows : near + rows + extra] = block.astype(BF)


def block_on_tile(place, padded, grad, grad_hidden, *params):
    rows, columns, channels = grad.shape
    slots, depth = params[-2:]
    return pl.pallas_call(
        block_kernel,
        out_shape=(
            jax.ShapeDtypeStruct(grad_hidden.shape, BF),
            jax.ShapeDtypeStruct((slots, depth, channels), BF),
            jax.ShapeDtypeStruct(grad.shape, F32),
        ),
        in_specs=[pl.BlockSpec(memory_space=pltpu.SMEM)]
        + [pl.BlockSpec(memory_space=pltpu.VMEM)] * 9,
        out_specs=(pl.BlockSpec(memory_space=pltpu.VMEM),) * 3,
        scratch_shapes=[pltpu.VMEM((rows + 2, columns + 8, channels), F32)],
        compiler_params=pltpu.CompilerParams(vmem_limit_bytes=24 * 1024 * 1024),
        name="block",
    )(place, padded, grad, grad_hidden, *params[:-2])


def share_kernel(scale, few, many, got_ref, share_ref):
    total, channels = share_ref.shape
    spare = got_ref.shape[1] - 4
    weights = jnp.zeros((many, channels), F32)
    rest = jnp.zeros((4, channels), F32)
    for k in range(got_ref.shape[0]):
        weights = weights + got_ref[k, 0:many].astype(F32)
        rest = rest + got_ref[k, spare - 4 : spare + 4].astype(F32)[4:8]
    parts = [weights * scale]
    for k in range(few):
        small = (rest[2 * k : 2 * k + 1] + rest[2 * k + 1 : 2 * k + 2]) * scale
        high = small.astype(BF).astype(F32)
        parts += [high, small - high]
    block = jnp.concatenate(parts * 8).astype(BF)
    depth = block.shape[0]
    for k in range(0, total, depth):
        share_ref[k : k + depth] = block


def share_of(got, slots, many, few, scale):
    channels = got.shape[2]
    return pl.pallas_call(
        functools.partial(share_kernel, scale, few, many),
        out_shape=jax.ShapeDtypeStruct((slots * (many + 2 * few), channels), BF),
        in_specs=[pl.BlockSpec(memory_space=pltpu.VMEM)],
        out_specs=pl.BlockSpec(memory_space=pltpu.VMEM),
        compiler_params=pltpu.CompilerParams(vmem_limit_bytes=8 * 1024 * 1024),
        name="share",
    )(got)


def finish_kernel(many, few, got_ref, *out_refs):
    tap_ref, bias_ref, gain_ref, shift_ref, expand_ref, expand_bias_ref, reduce_ref, reduce_bias_ref = (
        out_refs
    )
    total, channels = got_ref.shape
    hid = reduce_ref.shape[0]
    depth = many + 2 * few
    small = []
    for start in range(0, total, 8 * depth):
        block = got_ref[start : start + 8 * depth].astype(F32)
        for k in range(8):
            slot = start // depth + k
            part = block[k * depth : (k + 1) * depth]
            row = slot * many
            if row < hid:
                lane, row = row // channels * channels, row % channels
                expand_ref[row : row + many, lane : lane + channels] = part[:many]
            else:
                reduce_ref[row - hid : row - hid + many] = part[:many]
            rest = part[many:]
            small += [rest[2 * k : 2 * k + 1] + rest[2 * k + 1 : 2 * k + 2] for k in range(few)]
    blocks = hid // channels
    for k in range(9):
        tap_ref[k // 3, k % 3 : k % 3 + 1] = small[k]
    bias_ref[...] = small[9]
    gain_ref[...] = small[10]
    shift_ref[...] = small[11]
    for k in range(blocks):
        expand_bias_ref[:, k * channels : (k + 1) * channels] = small[12 + k]
    reduce_bias_ref[...] = small[12 + blocks]


def finish(got, hid, many, few):
    channels = got.shape[1]
    shapes = [(3, 3, channels)] + [(1, channels)] * 3
    shapes += [(channels, hid), (1, hid), (hid, channels), (1, channels)]
    return pl.pallas_call(
        functools.partial(finish_kernel, many, few),
        out_shape=tuple(jax.ShapeDtypeStruct(shape, F32) for shape in shapes),
        in_specs=[pl.BlockSpec(memory_space=pltpu.VMEM)],
        out_specs=(pl.BlockSpec(memory_space=pltpu.VMEM),) * len(shapes),
        compiler_params=pltpu.CompilerParams(vmem_limit_bytes=16 * 1024 * 1024),
        name="finish",
    )(got)


def swap(slots, groups):
    return lax.all_to_all(slots, ("face", "row", "col"), 0, 0, axis_index_groups=groups)


def at(slots, index):
    return lax.dynamic_index_in_dim(slots, index, 0, keepdims=False)


def device_groups(side):
    cut = math.isqrt(side)
    steps = range(cut)

    def device(f, y, x, high, low):
        return (f * side + y * cut + low) * side + high * cut + x

    planes = [
        [device(f, y, x, high, low) for f in range(2) for y in steps for x in steps]
        for high in steps
        for low in steps
    ]
    lines = [
        [device(f, y, x, high, low) for high in steps for low in steps]
        for f in range(2)
        for y in steps
        for x in steps
    ]
    return planes, lines


def frame_sources(entries, f, y, x, sender, target, step, side, cells):
    cut = math.isqrt(side)
    last, width, low_bits, cell_bits = side - 1, side * cells, cut - 1, cells - 1
    shift, cell_shift = low_bits.bit_length(), cell_bits.bit_length()
    high, low = sender >> shift, sender & low_bits
    row, col = y * cut + (target & low_bits), (target >> shift) * cut + x
    virtual = (step < 0) | (step >= cells)

    def held(face, tile_row, tile_col, part, cell, valid):
        valid = valid & ((tile_row & low_bits) == low) & ((tile_col >> shift) == high)
        slot = face * side + ((tile_row >> shift) << shift) + (tile_col & low_bits)
        inner = part * cells + cell
        end = 2 * cells + 2 * part + jnp.where(cell == 0, 0, 1)
        inner_index = slot * (2 * cells) + inner
        end_index = slot * (2 * cells + 8) + jnp.where(virtual, end, inner)
        return jnp.where(valid, inner_index, -1), jnp.where(valid, end_index, -1)

    def glued(edge, along, on_rows):
        other_edge, reverse = entries[edge]
        position = along * cells + step
        turned = jnp.where(reverse == 1, width - 1 - position, position)
        valid = (position >= 0) & (position < width)
        tile, cell = turned >> cell_shift, turned & cell_bits
        if on_rows:
            end = jnp.where(other_edge == 2, 0, last)
            return held(1 - f, tile, end, 1, cell, valid)
        end = jnp.where(other_edge == 0, 0, last)
        return held(1 - f, end, tile, 0, cell, valid)

    def beside(next_row, far_cell, own_part):
        position = col * cells + step
        valid = (position >= 0) & (position < width)
        tile, cell = position >> cell_shift, position & cell_bits
        level = (next_row >> shift) == y
        part = jnp.where(level & (step >= 0) & (step < cells), own_part, 0)
        cell = jnp.where(level & virtual, far_cell, cell)
        return held(f, next_row, tile, part, cell, valid)

    def either(condition, first, second):
        return tuple(jnp.where(condition, p, q) for p, q in zip(first, second))

    inner = (step >= 0) & (step < cells)
    nothing = (-1, -1)
    top = either(row == 0, glued(0, col, True), beside(row - 1, cells - 1, 1))
    bottom = either(row == last, glued(1, col, True), beside(row + 1, 0, 0))
    west = either(col == 0, glued(2, row, False), held(f, row, col - 1, 0, step, inner))
    east = either(col == last, glued(3, row, False), held(f, row, col + 1, 0, step, inner))
    return [top, bottom, either(x == 0, west, nothing), either(x == cut - 1, east, nothing)]


def two_sides(sources):
    need = [jnp.max(source[1].astype(F32), axis=-1, keepdims=True) >= 0.0 for source in sources]
    near = jnp.where(need[0], 0, jnp.where(need[1], 1, jnp.where(need[2], 2, 3)))
    after_one = jnp.where(need[2], 2, 3)
    far = jnp.where(
        need[0], jnp.where(need[1], 1, after_one), jnp.where(need[1], after_one, jnp.where(need[2], 3, 2))
    )
    return near, far


def plan_arrays(entries, f, r, c, side, cells):
    cut = math.isqrt(side)
    y, x = r // cut, c % cut
    here = c // cut * cut + r % cut
    others = lax.broadcasted_iota(jnp.int32, (side, 128), 0)
    lane = lax.broadcasted_iota(jnp.int32, (side, 128), 1)
    main = lane < 2 * cells
    step = jnp.where(main, lane & (cells - 1), jnp.where((lane & 1) == 0, -1, cells))
    second = jnp.where(main, lane - cells, lane - 2 * cells - 2) >= 0
    used = lane < 2 * cells + 4
    sources = frame_sources(entries, f, y, x, here, others, step, side, cells)
    near, far = two_sides(sources)
    which = jnp.where(second, far, near)
    passed = []
    for form in range(2):
        index = jnp.where(
            which == 0,
            sources[0][form],
            jnp.where(
                which == 1, sources[1][form], jnp.where(which == 2, sources[2][form], sources[3][form])
            ),
        )
        passed.append(jnp.where(used, index, -1))
    sources = frame_sources(entries, f, y, x, others, here, step, side, cells)
    near, far = two_sides(sources)
    which = jnp.where(second, far, near)
    return passed[0], passed[1], jnp.where(used, which * (cells + 2) + step + 1, -1)


def plan_kernel(side, cells, place_ref, adjacency_ref, plan_ref):
    f = place_ref[0]
    entries = [
        (adjacency_ref[f * 12 + 3 * edge + 1], adjacency_ref[f * 12 + 3 * edge + 2])
        for edge in range(4)
    ]
    arrays = plan_arrays(entries, f, place_ref[1], place_ref[2], side, cells)
    for k, array in enumerate(arrays):
        plan_ref[k] = array


def plan_of(place, adjacency, side, cells):
    return pl.pallas_call(
        functools.partial(plan_kernel, side, cells),
        out_shape=jax.ShapeDtypeStruct((3, side, 128), jnp.int32),
        in_specs=[pl.BlockSpec(memory_space=pltpu.SMEM)] * 2,
        out_specs=pl.BlockSpec(memory_space=pltpu.VMEM),
        compiler_params=pltpu.CompilerParams(vmem_limit_bytes=4 * 1024 * 1024),
        name="plan",
    )(place, adjacency.reshape(-1))


def picked(wanted, held):
    chosen = (wanted.reshape(-1, 1) == jnp.arange(held.shape[0], dtype=jnp.int32)).astype(BF)
    cells = jnp.dot(chosen, held, preferred_element_type=F32).astype(BF)
    return cells.reshape(wanted.shape + held.shape[1:])


def on_device(
    fields,
    conv_kernel,
    conv_bias,
    norm_gain,
    norm_bias,
    expand_weight,
    expand_bias,
    reduce_weight,
    reduce_bias,
    adjacency,
    out_grad,
):
    tile = fields[0]
    cells = tile.shape[0]
    channels = tile.shape[2]
    hid = expand_weight.shape[1]
    side = lax.axis_size("row")
    width = side * cells
    rim = cells + 2
    cut = math.isqrt(side)
    f = lax.axis_index("face")
    r = lax.axis_index("row")
    c = lax.axis_index("col")
    y, x = r // cut, c % cut
    planes, lines = device_groups(side)
    place = jnp.stack([f, r, c]).astype(jnp.int32)
    few = -(-(13 + hid // channels) // (2 * side))
    extra = 8
    assert 2 * few <= 4 and cells & (cells - 1) == 0 and cut & (cut - 1) == 0

    plan = plan_of(place, adjacency, side, cells)
    inner_wanted = plan[0, :, : 2 * cells + 4]
    end_wanted = plan[1, :, : 2 * cells + extra]
    frame_rows = jnp.arange(4 * rim, dtype=jnp.int32)[:, None]

    def frame_of(strips):
        depth = strips.shape[1]
        arrival = plan[2, :, :depth].reshape(1, -1)
        flat = strips.reshape(-1, channels)
        gather_frame = (frame_rows == arrival).astype(BF)
        return jnp.dot(gather_frame, flat, preferred_element_type=F32).reshape(4, rim, channels)

    def direct(strips, frame):
        base = f * side + y * cut
        west = at(strips, base + jnp.maximum(x - 1, 0)).astype(F32)
        east = at(strips, base + jnp.minimum(x + 1, cut - 1)).astype(F32)
        return jnp.where(x == 0, frame[2], west), jnp.where(x == cut - 1, frame[3], east)

    got = swap(edges_of(place, tile, 2 * side), planes)
    passed = picked(inner_wanted, got.reshape(-1, channels))
    passed = swap(passed.reshape(side, -1, 4, channels), lines)
    frame = frame_of(passed.reshape(side, 2 * cells + 4, channels))
    west, east = direct(got[:, :cells], frame[:, 1:-1])
    ends = frame[2:, ::rim - 1]
    top = jnp.concatenate(
        [frame[0, :1] + ends[0, :1], frame[0, 1:-1], frame[0, -1:] + ends[1, :1]]
    ).astype(BF)
    bottom = jnp.concatenate(
        [frame[1, :1] + ends[0, 1:], frame[1, 1:-1], frame[1, -1:] + ends[1, 1:]]
    ).astype(BF)
    padded = jnp.concatenate(
        [
            top[None],
            jnp.concatenate([west.astype(BF)[:, None], tile, east.astype(BF)[:, None]], axis=1),
            bottom[None],
        ]
    )

    many = 2 * hid // (2 * side)
    grad_cells = out_grad[0].reshape(cells * cells, channels)
    grad_hidden = lax.dot_general(
        grad_cells, reduce_weight, (((1,), (1,)), ((), ())), preferred_element_type=F32
    )
    hidden, sent, base_grad = block_on_tile(
        place,
        padded,
        out_grad[0],
        grad_hidden,
        conv_kernel.reshape(9, channels),
        conv_bias.reshape(1, channels),
        norm_gain.reshape(1, channels),
        norm_bias.reshape(1, channels),
        expand_weight,
        expand_bias.reshape(1, hid),
        2 * side,
        many + 2 * cells + extra,
    )
    block_out = (
        tile.reshape(cells * cells, channels).astype(F32)
        + jnp.dot(hidden, reduce_weight, preferred_element_type=F32)
        + reduce_bias
    ).astype(BF)
    got = swap(sent, planes)

    def pairs(small):
        high = small.astype(BF)
        low = (small - high.astype(F32)).astype(BF)
        return jnp.stack([high, low], axis=-2).reshape(2 * few, channels)

    def small_total(rest):
        sums = jnp.sum(rest.astype(F32), axis=0).reshape(few, 2, channels)
        return sums[:, 0] + sums[:, 1]

    spare = many + 2 * cells + 4
    weights = jnp.sum(got[:, :many].astype(F32), axis=0)
    small = small_total(got[:, spare : spare + 2 * few])
    strips = got[:, many:]
    passed = picked(end_wanted, strips.reshape(-1, channels))
    tail = jnp.pad(pairs(small), ((0, 4 - 2 * few), (0, 0)))
    sent = jnp.concatenate(
        [
            jnp.broadcast_to(weights.astype(BF), (side, many, channels)),
            passed[:, : 2 * cells],
            jnp.concatenate(
                [passed[:, 2 * cells : 2 * cells + 4], jnp.broadcast_to(tail, (side, 4, channels))],
                axis=1,
            ),
        ],
        axis=1,
    )
    got = swap(sent, lines)
    share = share_of(got, 2 * side, many, few, 1.0 / width)
    spread = swap(share.reshape(2 * side, -1, 2, channels), planes).reshape(share.shape)

    frame = frame_of(got[:, many:])
    folded = frame[:, 1:-1]
    folded = folded.at[:, 0].add(frame[:, 0]).at[:, -1].add(frame[:, -1])
    west, east = direct(strips[:, :cells], folded)
    in_grad = base_grad
    in_grad = in_grad + jnp.pad(folded[:1], ((0, cells - 1), (0, 0), (0, 0)))
    in_grad = in_grad + jnp.pad(folded[1:2], ((cells - 1, 0), (0, 0), (0, 0)))
    in_grad = in_grad + jnp.pad(west[:, None], ((0, 0), (0, cells - 1), (0, 0)))
    in_grad = in_grad + jnp.pad(east[:, None], ((0, 0), (cells - 1, 0), (0, 0)))

    taps, bias, gain, shift, expand, expand_vector, reduce, reduce_vector = finish(spread, hid, many, few)
    return (
        block_out.reshape(1, cells, cells, channels),
        in_grad.astype(BF)[None],
        taps,
        bias.reshape(channels),
        gain.reshape(channels),
        shift.reshape(channels),
        expand,
        expand_vector.reshape(hid),
        reduce,
        reduce_vector.reshape(channels),
    )


def solution(mesh):
    tiles = P("face", "row", "col", None)
    in_specs = (tiles,) + (P(),) * 9 + (tiles,)
    out_specs = (tiles, tiles) + (P(),) * 8
    return jax.shard_map(
        on_device, mesh=mesh, in_specs=in_specs, out_specs=out_specs, check_vma=False
    )
```

```python
import functools
import math

import jax
import jax.numpy as jnp
from jax import lax
from jax.experimental import pallas as pl
from jax.experimental.pallas import tpu as pltpu
from jax.sharding import PartitionSpec as P

GELU_SCALE = math.sqrt(2.0 / math.pi)
NORM_EPS = 1e-06
BF = jnp.bfloat16
F32 = jnp.float32


def gelu_pair(preact):
    cubic_term = preact + 0.044715 * preact * preact * preact
    tangent = jnp.tanh(GELU_SCALE * cubic_term)
    gelu_value = 0.5 * preact * (1.0 + tangent)
    gelu_slope = 0.5 * (1.0 + tangent) + 0.5 * preact * (1.0 - tangent * tangent) * GELU_SCALE * (
        1.0 + 3.0 * 0.044715 * preact * preact
    )
    return (gelu_value, gelu_slope)


def slot_strips(face, row, col, slot, side, north, south, west, east):
    cut = math.isqrt(side)
    here_y, here_x = row // cut, col % cut
    same = face == slot // side
    y, x = slot % side // cut, slot % cut
    level = jnp.where(
        x == (here_x + cut - 1) % cut, west, jnp.where(x == (here_x + 1) % cut, east, north)
    )
    inner = jnp.where(y < here_y, north, jnp.where(y > here_y, south, level))
    near = jnp.where(same, inner, jnp.where(row == 0, north, south))
    far = jnp.where(same, south, jnp.where(col == 0, west, east))
    return near, far


def edges_kernel(place_ref, tile_ref, sent_ref):
    slots, depth, _ = sent_ref.shape
    rows = depth // 2
    tile = tile_ref[...].astype(F32)
    north, south = tile[0], tile[rows - 1]
    west = jnp.concatenate([tile[k, 0:1] for k in range(rows)])
    east = jnp.concatenate([tile[k, rows - 1 : rows] for k in range(rows)])
    for slot in range(slots):
        near, far = slot_strips(
            place_ref[0], place_ref[1], place_ref[2], slot, slots // 2, north, south, west, east
        )
        sent_ref[slot, 0:rows] = near.astype(BF)
        sent_ref[slot, rows:depth] = far.astype(BF)


def edges_of(place, tile, slots):
    rows, _, channels = tile.shape
    return pl.pallas_call(
        edges_kernel,
        out_shape=jax.ShapeDtypeStruct((slots, 2 * rows, channels), BF),
        in_specs=[
            pl.BlockSpec(memory_space=pltpu.SMEM),
            pl.BlockSpec(memory_space=pltpu.VMEM),
        ],
        out_specs=pl.BlockSpec(memory_space=pltpu.VMEM),
        compiler_params=pltpu.CompilerParams(vmem_limit_bytes=8 * 1024 * 1024),
        name="edges",
    )(place, tile)


def block_kernel(
    plan_ref,
    padded_ref,
    grad_ref,
    grad_hidden_ref,
    tap_ref,
    conv_bias_ref,
    gain_ref,
    shift_ref,
    expand_ref,
    expand_bias_ref,
    hidden_ref,
    sent_ref,
    base_ref,
    wide_ref,
):
    rows, columns, channels = grad_ref.shape
    count = rows * columns
    rim = rows + 2
    hid = expand_ref.shape[1]
    slots, _, _ = sent_ref.shape
    side = slots // 2
    padded = padded_ref[...].astype(F32)
    shifted = [padded[:, b : b + columns] for b in range(3)]

    mixed = jnp.zeros((rows, columns, channels), F32) + conv_bias_ref[...].reshape(1, 1, channels)
    for a in range(3):
        for b in range(3):
            mixed = mixed + tap_ref[3 * a + b].reshape(1, 1, channels) * shifted[b][a : a + rows]
    mixed = mixed.reshape(count, channels)
    center = mixed - jnp.mean(mixed, axis=-1, keepdims=True)
    inv_std = lax.rsqrt(jnp.mean(center * center, axis=-1, keepdims=True) + NORM_EPS)
    normalized = center * inv_std
    normed = (normalized * gain_ref[...] + shift_ref[...]).astype(BF)
    preact = jnp.dot(normed, expand_ref[...], preferred_element_type=F32) + expand_bias_ref[...]
    gelu_value, gelu_slope = gelu_pair(preact)
    hidden = gelu_value.astype(BF)
    hidden_ref[...] = hidden
    grad_cells = grad_ref[...].reshape(count, channels)
    grad_preact = (grad_hidden_ref[...] * gelu_slope).astype(BF)
    grad_normed = lax.dot_general(
        grad_preact, expand_ref[...], (((1,), (1,)), ((), ())), preferred_element_type=F32
    )
    scaled = grad_normed * gain_ref[...]
    grad_mixed = inv_std * (
        scaled
        - jnp.mean(scaled, axis=-1, keepdims=True)
        - normalized * jnp.mean(scaled * normalized, axis=-1, keepdims=True)
    )

    def total(cells):
        return jnp.sum(cells, axis=0, keepdims=True)

    square = grad_mixed.reshape(rows, columns, channels)
    small = [
        total((square * shifted[b][a : a + rows]).reshape(count, channels))
        for a in range(3)
        for b in range(3)
    ]
    small += [total(grad_mixed), total(grad_normed * normalized), total(grad_normed)]
    preact_total = total(grad_preact.astype(F32))
    small += [preact_total[:, k : k + channels] for k in range(0, hid, channels)]
    small += [total(grad_cells.astype(F32))]

    across = (((0,), (0,)), ((), ()))
    expand_sum = lax.dot_general(normed, grad_preact, across, preferred_element_type=F32).astype(BF)
    reduce_sum = lax.dot_general(hidden, grad_cells, across, preferred_element_type=F32).astype(BF)
    many = 2 * hid // slots
    for k in range(0, hid, channels):
        for j in range(0, channels, many):
            sent_ref[(k + j) // many, 0:many] = expand_sum[j : j + many, k : k + channels]
    for k in range(0, hid, many):
        sent_ref[(hid + k) // many, 0:many] = reduce_sum[k : k + many]

    wide_ref[...] = jnp.zeros(wide_ref.shape, F32)
    for b in range(3):
        parts = [tap_ref[3 * a + b].reshape(1, 1, channels) * square for a in range(3)]
        wide_ref[0, b : b + columns] += parts[0][0]
        wide_ref[1, b : b + columns] += parts[0][1] + parts[1][0]
        wide_ref[2:rows, b : b + columns] += (
            parts[0][2:] + parts[1][1 : rows - 1] + parts[2][: rows - 2]
        )
        wide_ref[rows, b : b + columns] += parts[1][rows - 1] + parts[2][rows - 2]
        wide_ref[rows + 1, b : b + columns] += parts[2][rows - 1]
    base_ref[...] = grad_ref[...].astype(F32) + wide_ref[1 : rows + 1, 1 : columns + 1]
    west = jnp.concatenate([wide_ref[k, 0:1] for k in range(rim)])
    east = jnp.concatenate([wide_ref[k, rim - 1 : rim] for k in range(rim)])
    north = wide_ref[0, 0:rim]
    south = wide_ref[rim - 1, 0:rim]

    face, row, col = plan_ref[0], plan_ref[1], plan_ref[2]
    few = -(-len(small) // slots)
    extra = sent_ref.shape[1] - many - 2 * rows
    place = lax.broadcasted_iota(jnp.int32, (extra, channels), 0)
    near = many + rows
    for slot in range(slots):
        strip, side_strip = slot_strips(face, row, col, slot, side, north, south, west, east)
        sent_ref[slot, many:near] = strip[1 : rim - 1].astype(BF)
        sent_ref[slot, near : near + rows] = side_strip[1 : rim - 1].astype(BF)
        ends = [strip[0:1], strip[rim - 1 : rim], side_strip[0:1], side_strip[rim - 1 : rim]]
        values = ends
        for k in range(few * slot, min(few * slot + few, len(small))):
            high = small[k].astype(BF).astype(F32)
            values = values + [high, small[k] - high]
        block = jnp.zeros((extra, channels), F32)
        for k, value in enumerate(values):
            block = jnp.where(place == k, value, block)
        sent_ref[slot, near + rows : near + rows + extra] = block.astype(BF)


def block_on_tile(place, padded, grad, grad_hidden, *params):
    rows, columns, channels = grad.shape
    slots, depth = params[-2:]
    return pl.pallas_call(
        block_kernel,
        out_shape=(
            jax.ShapeDtypeStruct(grad_hidden.shape, BF),
            jax.ShapeDtypeStruct((slots, depth, channels), BF),
            jax.ShapeDtypeStruct(grad.shape, F32),
        ),
        in_specs=[pl.BlockSpec(memory_space=pltpu.SMEM)]
        + [pl.BlockSpec(memory_space=pltpu.VMEM)] * 9,
        out_specs=(pl.BlockSpec(memory_space=pltpu.VMEM),) * 3,
        scratch_shapes=[pltpu.VMEM((rows + 2, columns + 8, channels), F32)],
        compiler_params=pltpu.CompilerParams(vmem_limit_bytes=24 * 1024 * 1024),
        name="block",
    )(place, padded, grad, grad_hidden, *params[:-2])


def share_kernel(scale, few, many, got_ref, share_ref):
    total, channels = share_ref.shape
    spare = got_ref.shape[1] - 4
    weights = jnp.zeros((many, channels), F32)
    rest = jnp.zeros((4, channels), F32)
    for k in range(got_ref.shape[0]):
        weights = weights + got_ref[k, 0:many].astype(F32)
        rest = rest + got_ref[k, spare - 4 : spare + 4].astype(F32)[4:8]
    parts = [weights * scale]
    for k in range(few):
        small = (rest[2 * k : 2 * k + 1] + rest[2 * k + 1 : 2 * k + 2]) * scale
        high = small.astype(BF).astype(F32)
        parts += [high, small - high]
    block = jnp.concatenate(parts * 8).astype(BF)
    depth = block.shape[0]
    for k in range(0, total, depth):
        share_ref[k : k + depth] = block


def share_of(got, slots, many, few, scale):
    channels = got.shape[2]
    return pl.pallas_call(
        functools.partial(share_kernel, scale, few, many),
        out_shape=jax.ShapeDtypeStruct((slots * (many + 2 * few), channels), BF),
        in_specs=[pl.BlockSpec(memory_space=pltpu.VMEM)],
        out_specs=pl.BlockSpec(memory_space=pltpu.VMEM),
        compiler_params=pltpu.CompilerParams(vmem_limit_bytes=8 * 1024 * 1024),
        name="share",
    )(got)


def finish_kernel(many, few, got_ref, *out_refs):
    tap_ref, bias_ref, gain_ref, shift_ref, expand_ref, expand_bias_ref, reduce_ref, reduce_bias_ref = (
        out_refs
    )
    total, channels = got_ref.shape
    hid = reduce_ref.shape[0]
    depth = many + 2 * few
    small = []
    for start in range(0, total, 8 * depth):
        block = got_ref[start : start + 8 * depth].astype(F32)
        for k in range(8):
            slot = start // depth + k
            part = block[k * depth : (k + 1) * depth]
            row = slot * many
            if row < hid:
                lane, row = row // channels * channels, row % channels
                expand_ref[row : row + many, lane : lane + channels] = part[:many]
            else:
                reduce_ref[row - hid : row - hid + many] = part[:many]
            rest = part[many:]
            small += [rest[2 * k : 2 * k + 1] + rest[2 * k + 1 : 2 * k + 2] for k in range(few)]
    blocks = hid // channels
    for k in range(9):
        tap_ref[k // 3, k % 3 : k % 3 + 1] = small[k]
    bias_ref[...] = small[9]
    gain_ref[...] = small[10]
    shift_ref[...] = small[11]
    for k in range(blocks):
        expand_bias_ref[:, k * channels : (k + 1) * channels] = small[12 + k]
    reduce_bias_ref[...] = small[12 + blocks]


def finish(got, hid, many, few):
    channels = got.shape[1]
    shapes = [(3, 3, channels)] + [(1, channels)] * 3
    shapes += [(channels, hid), (1, hid), (hid, channels), (1, channels)]
    return pl.pallas_call(
        functools.partial(finish_kernel, many, few),
        out_shape=tuple(jax.ShapeDtypeStruct(shape, F32) for shape in shapes),
        in_specs=[pl.BlockSpec(memory_space=pltpu.VMEM)],
        out_specs=(pl.BlockSpec(memory_space=pltpu.VMEM),) * len(shapes),
        compiler_params=pltpu.CompilerParams(vmem_limit_bytes=16 * 1024 * 1024),
        name="finish",
    )(got)


def swap(slots, groups):
    return lax.all_to_all(slots, ("face", "row", "col"), 0, 0, axis_index_groups=groups)


def at(slots, index):
    return lax.dynamic_index_in_dim(slots, index, 0, keepdims=False)


def device_groups(side):
    cut = math.isqrt(side)
    steps = range(cut)

    def device(f, y, x, high, low):
        return (f * side + y * cut + low) * side + high * cut + x

    planes = [
        [device(f, y, x, high, low) for f in range(2) for y in steps for x in steps]
        for high in steps
        for low in steps
    ]
    lines = [
        [device(f, y, x, high, low) for high in steps for low in steps][:: 1 - 2 * f]
        for f in range(2)
        for y in steps
        for x in steps
    ]
    return planes, lines


def frame_sources(entries, f, y, x, sender, target, step, side, cells):
    cut = math.isqrt(side)
    last, width, low_bits, cell_bits = side - 1, side * cells, cut - 1, cells - 1
    shift, cell_shift = low_bits.bit_length(), cell_bits.bit_length()
    high, low = sender >> shift, sender & low_bits
    row, col = y * cut + (target & low_bits), (target >> shift) * cut + x
    virtual = (step < 0) | (step >= cells)

    def held(face, tile_row, tile_col, part, cell, valid):
        valid = valid & ((tile_row & low_bits) == low) & ((tile_col >> shift) == high)
        slot = face * side + ((tile_row >> shift) << shift) + (tile_col & low_bits)
        inner = part * cells + cell
        end = 2 * cells + 2 * part + jnp.where(cell == 0, 0, 1)
        inner_index = slot * (2 * cells) + inner
        end_index = slot * (2 * cells + 8) + jnp.where(virtual, end, inner)
        return jnp.where(valid, inner_index, -1), jnp.where(valid, end_index, -1)

    def glued(edge, along, on_rows):
        other_edge, reverse = entries[edge]
        position = along * cells + step
        turned = jnp.where(reverse == 1, width - 1 - position, position)
        valid = (position >= 0) & (position < width)
        tile, cell = turned >> cell_shift, turned & cell_bits
        if on_rows:
            end = jnp.where(other_edge == 2, 0, last)
            return held(1 - f, tile, end, 1, cell, valid)
        end = jnp.where(other_edge == 0, 0, last)
        return held(1 - f, end, tile, 0, cell, valid)

    def beside(next_row, far_cell, own_part):
        position = col * cells + step
        valid = (position >= 0) & (position < width)
        tile, cell = position >> cell_shift, position & cell_bits
        level = (next_row >> shift) == y
        part = jnp.where(level & (step >= 0) & (step < cells), own_part, 0)
        cell = jnp.where(level & virtual, far_cell, cell)
        return held(f, next_row, tile, part, cell, valid)

    def either(condition, first, second):
        return tuple(jnp.where(condition, p, q) for p, q in zip(first, second))

    inner = (step >= 0) & (step < cells)
    nothing = (-1, -1)
    top = either(row == 0, glued(0, col, True), beside(row - 1, cells - 1, 1))
    bottom = either(row == last, glued(1, col, True), beside(row + 1, 0, 0))
    west = either(col == 0, glued(2, row, False), held(f, row, col - 1, 0, step, inner))
    east = either(col == last, glued(3, row, False), held(f, row, col + 1, 0, step, inner))
    return [top, bottom, either(x == 0, west, nothing), either(x == cut - 1, east, nothing)]


def two_sides(sources):
    need = [jnp.max(source[1].astype(F32), axis=-1, keepdims=True) >= 0.0 for source in sources]
    near = jnp.where(need[0], 0, jnp.where(need[1], 1, jnp.where(need[2], 2, 3)))
    after_one = jnp.where(need[2], 2, 3)
    far = jnp.where(
        need[0], jnp.where(need[1], 1, after_one), jnp.where(need[1], after_one, jnp.where(need[2], 3, 2))
    )
    return near, far


def plan_arrays(entries, f, r, c, side, cells):
    cut = math.isqrt(side)
    y, x = r // cut, c % cut
    here = c // cut * cut + r % cut
    others = lax.broadcasted_iota(jnp.int32, (side, 128), 0)
    others = jnp.where(f == 1, side - 1 - others, others)
    lane = lax.broadcasted_iota(jnp.int32, (side, 128), 1)
    main = lane < 2 * cells
    step = jnp.where(main, lane & (cells - 1), jnp.where((lane & 1) == 0, -1, cells))
    second = jnp.where(main, lane - cells, lane - 2 * cells - 2) >= 0
    used = lane < 2 * cells + 4
    sources = frame_sources(entries, f, y, x, here, others, step, side, cells)
    near, far = two_sides(sources)
    which = jnp.where(second, far, near)
    passed = []
    for form in range(2):
        index = jnp.where(
            which == 0,
            sources[0][form],
            jnp.where(
                which == 1, sources[1][form], jnp.where(which == 2, sources[2][form], sources[3][form])
            ),
        )
        passed.append(jnp.where(used, index, -1))
    sources = frame_sources(entries, f, y, x, others, here, step, side, cells)
    near, far = two_sides(sources)
    which = jnp.where(second, far, near)
    return passed[0], passed[1], jnp.where(used, which * (cells + 2) + step + 1, -1)


def plan_kernel(side, cells, place_ref, adjacency_ref, plan_ref):
    f = place_ref[0]
    entries = [
        (adjacency_ref[f * 12 + 3 * edge + 1], adjacency_ref[f * 12 + 3 * edge + 2])
        for edge in range(4)
    ]
    arrays = plan_arrays(entries, f, place_ref[1], place_ref[2], side, cells)
    for k, array in enumerate(arrays):
        plan_ref[k] = array


def plan_of(place, adjacency, side, cells):
    return pl.pallas_call(
        functools.partial(plan_kernel, side, cells),
        out_shape=jax.ShapeDtypeStruct((3, side, 128), jnp.int32),
        in_specs=[pl.BlockSpec(memory_space=pltpu.SMEM)] * 2,
        out_specs=pl.BlockSpec(memory_space=pltpu.VMEM),
        compiler_params=pltpu.CompilerParams(vmem_limit_bytes=4 * 1024 * 1024),
        name="plan",
    )(place, adjacency.reshape(-1))


def picked(wanted, held):
    chosen = (wanted.reshape(-1, 1) == jnp.arange(held.shape[0], dtype=jnp.int32)).astype(BF)
    cells = jnp.dot(chosen, held, preferred_element_type=F32).astype(BF)
    return cells.reshape(wanted.shape + held.shape[1:])


def on_device(
    fields,
    conv_kernel,
    conv_bias,
    norm_gain,
    norm_bias,
    expand_weight,
    expand_bias,
    reduce_weight,
    reduce_bias,
    adjacency,
    out_grad,
):
    tile = fields[0]
    cells = tile.shape[0]
    channels = tile.shape[2]
    hid = expand_weight.shape[1]
    side = lax.axis_size("row")
    width = side * cells
    rim = cells + 2
    cut = math.isqrt(side)
    f = lax.axis_index("face")
    r = lax.axis_index("row")
    c = lax.axis_index("col")
    y, x = r // cut, c % cut
    planes, lines = device_groups(side)
    place = jnp.stack([f, r, c]).astype(jnp.int32)
    few = -(-(13 + hid // channels) // (2 * side))
    extra = 8
    assert 2 * few <= 4 and cells & (cells - 1) == 0 and cut & (cut - 1) == 0

    plan = plan_of(place, adjacency, side, cells)
    inner_wanted = plan[0, :, : 2 * cells + 4]
    end_wanted = plan[1, :, : 2 * cells + extra]
    frame_rows = jnp.arange(4 * rim, dtype=jnp.int32)[:, None]

    def frame_of(strips):
        depth = strips.shape[1]
        arrival = plan[2, :, :depth].reshape(1, -1)
        flat = strips.reshape(-1, channels)
        gather_frame = (frame_rows == arrival).astype(BF)
        return jnp.dot(gather_frame, flat, preferred_element_type=F32).reshape(4, rim, channels)

    def direct(strips, frame):
        base = f * side + y * cut
        west = at(strips, base + jnp.maximum(x - 1, 0)).astype(F32)
        east = at(strips, base + jnp.minimum(x + 1, cut - 1)).astype(F32)
        return jnp.where(x == 0, frame[2], west), jnp.where(x == cut - 1, frame[3], east)

    got = swap(edges_of(place, tile, 2 * side), planes)
    passed = picked(inner_wanted, got.reshape(-1, channels))
    passed = swap(passed.reshape(side, -1, 4, channels), lines)
    frame = frame_of(passed.reshape(side, 2 * cells + 4, channels))
    west, east = direct(got[:, :cells], frame[:, 1:-1])
    ends = frame[2:, ::rim - 1]
    top = jnp.concatenate(
        [frame[0, :1] + ends[0, :1], frame[0, 1:-1], frame[0, -1:] + ends[1, :1]]
    ).astype(BF)
    bottom = jnp.concatenate(
        [frame[1, :1] + ends[0, 1:], frame[1, 1:-1], frame[1, -1:] + ends[1, 1:]]
    ).astype(BF)
    padded = jnp.concatenate(
        [
            top[None],
            jnp.concatenate([west.astype(BF)[:, None], tile, east.astype(BF)[:, None]], axis=1),
            bottom[None],
        ]
    )

    many = 2 * hid // (2 * side)
    grad_cells = out_grad[0].reshape(cells * cells, channels)
    grad_hidden = lax.dot_general(
        grad_cells, reduce_weight, (((1,), (1,)), ((), ())), preferred_element_type=F32
    )
    hidden, sent, base_grad = block_on_tile(
        place,
        padded,
        out_grad[0],
        grad_hidden,
        conv_kernel.reshape(9, channels),
        conv_bias.reshape(1, channels),
        norm_gain.reshape(1, channels),
        norm_bias.reshape(1, channels),
        expand_weight,
        expand_bias.reshape(1, hid),
        2 * side,
        many + 2 * cells + extra,
    )
    block_out = (
        tile.reshape(cells * cells, channels).astype(F32)
        + jnp.dot(hidden, reduce_weight, preferred_element_type=F32)
        + reduce_bias
    ).astype(BF)
    got = swap(sent, planes)

    def pairs(small):
        high = small.astype(BF)
        low = (small - high.astype(F32)).astype(BF)
        return jnp.stack([high, low], axis=-2).reshape(2 * few, channels)

    def small_total(rest):
        sums = jnp.sum(rest.astype(F32), axis=0).reshape(few, 2, channels)
        return sums[:, 0] + sums[:, 1]

    spare = many + 2 * cells + 4
    weights = jnp.sum(got[:, :many].astype(F32), axis=0)
    small = small_total(got[:, spare : spare + 2 * few])
    strips = got[:, many:]
    passed = picked(end_wanted, strips.reshape(-1, channels))
    tail = jnp.pad(pairs(small), ((0, 4 - 2 * few), (0, 0)))
    sent = jnp.concatenate(
        [
            jnp.broadcast_to(weights.astype(BF), (side, many, channels)),
            passed[:, : 2 * cells],
            jnp.concatenate(
                [passed[:, 2 * cells : 2 * cells + 4], jnp.broadcast_to(tail, (side, 4, channels))],
                axis=1,
            ),
        ],
        axis=1,
    )
    got = swap(sent, lines)
    share = share_of(got, 2 * side, many, few, 1.0 / width)
    spread = swap(share.reshape(2 * side, -1, 2, channels), planes).reshape(share.shape)

    frame = frame_of(got[:, many:])
    folded = frame[:, 1:-1]
    folded = folded.at[:, 0].add(frame[:, 0]).at[:, -1].add(frame[:, -1])
    west, east = direct(strips[:, :cells], folded)
    in_grad = base_grad
    in_grad = in_grad + jnp.pad(folded[:1], ((0, cells - 1), (0, 0), (0, 0)))
    in_grad = in_grad + jnp.pad(folded[1:2], ((cells - 1, 0), (0, 0), (0, 0)))
    in_grad = in_grad + jnp.pad(west[:, None], ((0, 0), (0, cells - 1), (0, 0)))
    in_grad = in_grad + jnp.pad(east[:, None], ((0, 0), (cells - 1, 0), (0, 0)))

    taps, bias, gain, shift, expand, expand_vector, reduce, reduce_vector = finish(spread, hid, many, few)
    return (
        block_out.reshape(1, cells, cells, channels),
        in_grad.astype(BF)[None],
        taps,
        bias.reshape(channels),
        gain.reshape(channels),
        shift.reshape(channels),
        expand,
        expand_vector.reshape(hid),
        reduce,
        reduce_vector.reshape(channels),
    )


def solution(mesh):
    tiles = P("face", "row", "col", None)
    in_specs = (tiles,) + (P(),) * 9 + (tiles,)
    out_specs = (tiles, tiles) + (P(),) * 8
    return jax.shard_map(
        on_device, mesh=mesh, in_specs=in_specs, out_specs=out_specs, check_vma=False
    )
```

```python
import functools
import math

import jax
import jax.numpy as jnp
from jax import lax
from jax.experimental import pallas as pl
from jax.experimental.pallas import tpu as pltpu
from jax.sharding import PartitionSpec as P

GELU_SCALE = math.sqrt(2.0 / math.pi)
NORM_EPS = 1e-06
BF = jnp.bfloat16
F32 = jnp.float32


def gelu_pair(preact):
    cubic_term = preact + 0.044715 * preact * preact * preact
    tangent = jnp.tanh(GELU_SCALE * cubic_term)
    gelu_value = 0.5 * preact * (1.0 + tangent)
    gelu_slope = 0.5 * (1.0 + tangent) + 0.5 * preact * (1.0 - tangent * tangent) * GELU_SCALE * (
        1.0 + 3.0 * 0.044715 * preact * preact
    )
    return (gelu_value, gelu_slope)


def slot_strips(face, row, col, slot, side, north, south, west, east):
    cut = math.isqrt(side)
    here_y, here_x = row // cut, col % cut
    same = face == slot // side
    y, x = slot % side // cut, slot % cut
    level = jnp.where(
        x == (here_x + cut - 1) % cut, west, jnp.where(x == (here_x + 1) % cut, east, north)
    )
    inner = jnp.where(y < here_y, north, jnp.where(y > here_y, south, level))
    near = jnp.where(same, inner, jnp.where(row == 0, north, south))
    far = jnp.where(same, south, jnp.where(col == 0, west, east))
    return near, far


def edges_kernel(place_ref, tile_ref, sent_ref):
    slots, depth, _ = sent_ref.shape
    rows = depth // 2
    tile = tile_ref[...].astype(F32)
    north, south = tile_ref[0], tile_ref[rows - 1]
    west = jnp.concatenate([tile[k, 0:1] for k in range(rows)]).astype(BF)
    east = jnp.concatenate([tile[k, rows - 1 : rows] for k in range(rows)]).astype(BF)
    for slot in range(slots):
        near, far = slot_strips(
            place_ref[0], place_ref[1], place_ref[2], slot, slots // 2, north, south, west, east
        )
        sent_ref[slot, 0:rows] = near
        sent_ref[slot, rows:depth] = far


def edges_of(place, tile, slots):
    rows, _, channels = tile.shape
    return pl.pallas_call(
        edges_kernel,
        out_shape=jax.ShapeDtypeStruct((slots, 2 * rows, channels), BF),
        in_specs=[
            pl.BlockSpec(memory_space=pltpu.SMEM),
            pl.BlockSpec(memory_space=pltpu.VMEM),
        ],
        out_specs=pl.BlockSpec(memory_space=pltpu.VMEM),
        compiler_params=pltpu.CompilerParams(vmem_limit_bytes=8 * 1024 * 1024),
        name="edges",
    )(place, tile)


def block_kernel(
    plan_ref,
    padded_ref,
    grad_ref,
    grad_hidden_ref,
    tap_ref,
    conv_bias_ref,
    gain_ref,
    shift_ref,
    expand_ref,
    expand_bias_ref,
    hidden_ref,
    sent_ref,
    base_ref,
    wide_ref,
):
    rows, columns, channels = grad_ref.shape
    count = rows * columns
    rim = rows + 2
    hid = expand_ref.shape[1]
    slots, _, _ = sent_ref.shape
    side = slots // 2
    padded = padded_ref[...].astype(F32)
    shifted = [padded[:, b : b + columns] for b in range(3)]

    mixed = jnp.zeros((rows, columns, channels), F32) + conv_bias_ref[...].reshape(1, 1, channels)
    for a in range(3):
        for b in range(3):
            mixed = mixed + tap_ref[3 * a + b].reshape(1, 1, channels) * shifted[b][a : a + rows]
    mixed = mixed.reshape(count, channels)
    center = mixed - jnp.mean(mixed, axis=-1, keepdims=True)
    inv_std = lax.rsqrt(jnp.mean(center * center, axis=-1, keepdims=True) + NORM_EPS)
    normalized = center * inv_std
    normed = (normalized * gain_ref[...] + shift_ref[...]).astype(BF)
    preact = jnp.dot(normed, expand_ref[...], preferred_element_type=F32) + expand_bias_ref[...]
    gelu_value, gelu_slope = gelu_pair(preact)
    hidden = gelu_value.astype(BF)
    hidden_ref[...] = hidden
    grad_cells = grad_ref[...].reshape(count, channels)
    grad_preact = (grad_hidden_ref[...] * gelu_slope).astype(BF)
    grad_normed = lax.dot_general(
        grad_preact, expand_ref[...], (((1,), (1,)), ((), ())), preferred_element_type=F32
    )
    scaled = grad_normed * gain_ref[...]
    grad_mixed = inv_std * (
        scaled
        - jnp.mean(scaled, axis=-1, keepdims=True)
        - normalized * jnp.mean(scaled * normalized, axis=-1, keepdims=True)
    )

    def total(cells):
        return jnp.sum(cells, axis=0, keepdims=True)

    square = grad_mixed.reshape(rows, columns, channels)
    small = [
        total((square * shifted[b][a : a + rows]).reshape(count, channels))
        for a in range(3)
        for b in range(3)
    ]
    small += [total(grad_mixed), total(grad_normed * normalized), total(grad_normed)]
    preact_total = total(grad_preact.astype(F32))
    small += [preact_total[:, k : k + channels] for k in range(0, hid, channels)]
    small += [total(grad_cells.astype(F32))]

    across = (((0,), (0,)), ((), ()))
    expand_sum = lax.dot_general(normed, grad_preact, across, preferred_element_type=F32).astype(BF)
    reduce_sum = lax.dot_general(hidden, grad_cells, across, preferred_element_type=F32).astype(BF)
    many = 2 * hid // slots
    for k in range(0, hid, channels):
        for j in range(0, channels, many):
            sent_ref[(k + j) // many, 0:many] = expand_sum[j : j + many, k : k + channels]
    for k in range(0, hid, many):
        sent_ref[(hid + k) // many, 0:many] = reduce_sum[k : k + many]

    wide_ref[...] = jnp.zeros(wide_ref.shape, F32)
    for b in range(3):
        parts = [tap_ref[3 * a + b].reshape(1, 1, channels) * square for a in range(3)]
        wide_ref[0, b : b + columns] += parts[0][0]
        wide_ref[1, b : b + columns] += parts[0][1] + parts[1][0]
        wide_ref[2:rows, b : b + columns] += (
            parts[0][2:] + parts[1][1 : rows - 1] + parts[2][: rows - 2]
        )
        wide_ref[rows, b : b + columns] += parts[1][rows - 1] + parts[2][rows - 2]
        wide_ref[rows + 1, b : b + columns] += parts[2][rows - 1]
    base_ref[...] = grad_ref[...].astype(F32) + wide_ref[1 : rows + 1, 1 : columns + 1]
    west = jnp.concatenate([wide_ref[k, 0:1] for k in range(rim)])
    east = jnp.concatenate([wide_ref[k, rim - 1 : rim] for k in range(rim)])
    north = wide_ref[0, 0:rim]
    south = wide_ref[rim - 1, 0:rim]

    face, row, col = plan_ref[0], plan_ref[1], plan_ref[2]
    few = -(-len(small) // slots)
    extra = sent_ref.shape[1] - many - 2 * rows
    place = lax.broadcasted_iota(jnp.int32, (extra, channels), 0)
    near = many + rows
    rims = (north, south, west, east)
    inner = [strip[1 : rim - 1].astype(BF) for strip in rims]

    def ends_at(start):
        return [
            jnp.where(
                place == start, strip[0:1], jnp.where(place == start + 1, strip[rim - 1 : rim], 0.0)
            )
            for strip in rims
        ]

    near_ends, far_ends = ends_at(0), ends_at(2)
    for slot in range(slots):
        strip, side_strip = slot_strips(face, row, col, slot, side, *inner)
        sent_ref[slot, many:near] = strip
        sent_ref[slot, near : near + rows] = side_strip
        block, _ = slot_strips(face, row, col, slot, side, *near_ends)
        _, side_block = slot_strips(face, row, col, slot, side, *far_ends)
        block = block + side_block
        for j, k in enumerate(range(few * slot, min(few * slot + few, len(small)))):
            high = small[k].astype(BF).astype(F32)
            block = jnp.where(place == 4 + 2 * j, high, block)
            block = jnp.where(place == 5 + 2 * j, small[k] - high, block)
        sent_ref[slot, near + rows : near + rows + extra] = block.astype(BF)


def block_on_tile(place, padded, grad, grad_hidden, *params):
    rows, columns, channels = grad.shape
    slots, depth = params[-2:]
    return pl.pallas_call(
        block_kernel,
        out_shape=(
            jax.ShapeDtypeStruct(grad_hidden.shape, BF),
            jax.ShapeDtypeStruct((slots, depth, channels), BF),
            jax.ShapeDtypeStruct(grad.shape, F32),
        ),
        in_specs=[pl.BlockSpec(memory_space=pltpu.SMEM)]
        + [pl.BlockSpec(memory_space=pltpu.VMEM)] * 9,
        out_specs=(pl.BlockSpec(memory_space=pltpu.VMEM),) * 3,
        scratch_shapes=[pltpu.VMEM((rows + 2, columns + 8, channels), F32)],
        compiler_params=pltpu.CompilerParams(vmem_limit_bytes=24 * 1024 * 1024),
        name="block",
    )(place, padded, grad, grad_hidden, *params[:-2])


def share_kernel(scale, few, many, got_ref, share_ref):
    total, channels = share_ref.shape
    spare = got_ref.shape[1] - 4
    weights = jnp.zeros((many, channels), F32)
    rest = jnp.zeros((4, channels), F32)
    for k in range(got_ref.shape[0]):
        weights = weights + got_ref[k, 0:many].astype(F32)
        rest = rest + got_ref[k, spare - 4 : spare + 4].astype(F32)[4:8]
    parts = [weights * scale]
    for k in range(few):
        small = (rest[2 * k : 2 * k + 1] + rest[2 * k + 1 : 2 * k + 2]) * scale
        high = small.astype(BF).astype(F32)
        parts += [high, small - high]
    block = jnp.concatenate(parts * 8).astype(BF)
    depth = block.shape[0]
    for k in range(0, total, depth):
        share_ref[k : k + depth] = block


def share_of(got, slots, many, few, scale):
    channels = got.shape[2]
    return pl.pallas_call(
        functools.partial(share_kernel, scale, few, many),
        out_shape=jax.ShapeDtypeStruct((slots * (many + 2 * few), channels), BF),
        in_specs=[pl.BlockSpec(memory_space=pltpu.VMEM)],
        out_specs=pl.BlockSpec(memory_space=pltpu.VMEM),
        compiler_params=pltpu.CompilerParams(vmem_limit_bytes=8 * 1024 * 1024),
        name="share",
    )(got)


def finish_kernel(many, few, got_ref, *out_refs):
    tap_ref, bias_ref, gain_ref, shift_ref, expand_ref, expand_bias_ref, reduce_ref, reduce_bias_ref = (
        out_refs
    )
    total, channels = got_ref.shape
    hid = reduce_ref.shape[0]
    depth = many + 2 * few
    small = []
    for start in range(0, total, 8 * depth):
        block = got_ref[start : start + 8 * depth].astype(F32)
        for k in range(8):
            slot = start // depth + k
            part = block[k * depth : (k + 1) * depth]
            row = slot * many
            if row < hid:
                lane, row = row // channels * channels, row % channels
                expand_ref[row : row + many, lane : lane + channels] = part[:many]
            else:
                reduce_ref[row - hid : row - hid + many] = part[:many]
            rest = part[many:]
            small += [rest[2 * k : 2 * k + 1] + rest[2 * k + 1 : 2 * k + 2] for k in range(few)]
    blocks = hid // channels
    for k in range(9):
        tap_ref[k // 3, k % 3 : k % 3 + 1] = small[k]
    bias_ref[...] = small[9]
    gain_ref[...] = small[10]
    shift_ref[...] = small[11]
    for k in range(blocks):
        expand_bias_ref[:, k * channels : (k + 1) * channels] = small[12 + k]
    reduce_bias_ref[...] = small[12 + blocks]


def finish(got, hid, many, few):
    channels = got.shape[1]
    shapes = [(3, 3, channels)] + [(1, channels)] * 3
    shapes += [(channels, hid), (1, hid), (hid, channels), (1, channels)]
    return pl.pallas_call(
        functools.partial(finish_kernel, many, few),
        out_shape=tuple(jax.ShapeDtypeStruct(shape, F32) for shape in shapes),
        in_specs=[pl.BlockSpec(memory_space=pltpu.VMEM)],
        out_specs=(pl.BlockSpec(memory_space=pltpu.VMEM),) * len(shapes),
        compiler_params=pltpu.CompilerParams(vmem_limit_bytes=16 * 1024 * 1024),
        name="finish",
    )(got)


def swap(slots, groups):
    return lax.all_to_all(slots, ("face", "row", "col"), 0, 0, axis_index_groups=groups)


def at(slots, index):
    return lax.dynamic_index_in_dim(slots, index, 0, keepdims=False)


def device_groups(side):
    cut = math.isqrt(side)
    steps = range(cut)

    def device(f, y, x, high, low):
        return (f * side + y * cut + low) * side + high * cut + x

    planes = [
        [device(f, y, x, high, low) for f in range(2) for y in steps for x in steps]
        for high in steps
        for low in steps
    ]
    lines = [
        [device(f, y, x, high, low) for high in steps for low in steps][:: 1 - 2 * f]
        for f in range(2)
        for y in steps
        for x in steps
    ]
    return planes, lines


def frame_sources(entries, f, y, x, sender, target, step, side, cells):
    cut = math.isqrt(side)
    last, width, low_bits, cell_bits = side - 1, side * cells, cut - 1, cells - 1
    shift, cell_shift = low_bits.bit_length(), cell_bits.bit_length()
    high, low = sender >> shift, sender & low_bits
    row, col = y * cut + (target & low_bits), (target >> shift) * cut + x
    virtual = (step < 0) | (step >= cells)

    def held(face, tile_row, tile_col, part, cell, valid):
        valid = valid & ((tile_row & low_bits) == low) & ((tile_col >> shift) == high)
        slot = face * side + ((tile_row >> shift) << shift) + (tile_col & low_bits)
        inner = part * cells + cell
        end = 2 * cells + 2 * part + jnp.where(cell == 0, 0, 1)
        inner_index = slot * (2 * cells) + inner
        end_index = slot * (2 * cells + 8) + jnp.where(virtual, end, inner)
        return jnp.where(valid, inner_index, -1), jnp.where(valid, end_index, -1)

    def glued(edge, along, on_rows):
        other_edge, reverse = entries[edge]
        position = along * cells + step
        turned = jnp.where(reverse == 1, width - 1 - position, position)
        valid = (position >= 0) & (position < width)
        tile, cell = turned >> cell_shift, turned & cell_bits
        if on_rows:
            end = jnp.where(other_edge == 2, 0, last)
            return held(1 - f, tile, end, 1, cell, valid)
        end = jnp.where(other_edge == 0, 0, last)
        return held(1 - f, end, tile, 0, cell, valid)

    def beside(next_row, far_cell, own_part):
        position = col * cells + step
        valid = (position >= 0) & (position < width)
        tile, cell = position >> cell_shift, position & cell_bits
        level = (next_row >> shift) == y
        part = jnp.where(level & (step >= 0) & (step < cells), own_part, 0)
        cell = jnp.where(level & virtual, far_cell, cell)
        return held(f, next_row, tile, part, cell, valid)

    def either(condition, first, second):
        return tuple(jnp.where(condition, p, q) for p, q in zip(first, second))

    inner = (step >= 0) & (step < cells)
    nothing = (-1, -1)
    top = either(row == 0, glued(0, col, True), beside(row - 1, cells - 1, 1))
    bottom = either(row == last, glued(1, col, True), beside(row + 1, 0, 0))
    west = either(col == 0, glued(2, row, False), held(f, row, col - 1, 0, step, inner))
    east = either(col == last, glued(3, row, False), held(f, row, col + 1, 0, step, inner))
    return [top, bottom, either(x == 0, west, nothing), either(x == cut - 1, east, nothing)]


def two_sides(sources):
    need = [jnp.max(source[1].astype(F32), axis=-1, keepdims=True) >= 0.0 for source in sources]
    near = jnp.where(need[0], 0, jnp.where(need[1], 1, jnp.where(need[2], 2, 3)))
    after_one = jnp.where(need[2], 2, 3)
    far = jnp.where(
        need[0], jnp.where(need[1], 1, after_one), jnp.where(need[1], after_one, jnp.where(need[2], 3, 2))
    )
    return near, far


def plan_arrays(entries, f, r, c, side, cells):
    cut = math.isqrt(side)
    y, x = r // cut, c % cut
    here = c // cut * cut + r % cut
    others = lax.broadcasted_iota(jnp.int32, (side, 128), 0)
    others = jnp.where(f == 1, side - 1 - others, others)
    lane = lax.broadcasted_iota(jnp.int32, (side, 128), 1)
    main = lane < 2 * cells
    step = jnp.where(main, lane & (cells - 1), jnp.where((lane & 1) == 0, -1, cells))
    second = jnp.where(main, lane - cells, lane - 2 * cells - 2) >= 0
    used = lane < 2 * cells + 4
    sources = frame_sources(entries, f, y, x, here, others, step, side, cells)
    near, far = two_sides(sources)
    which = jnp.where(second, far, near)
    passed = []
    for form in range(2):
        index = jnp.where(
            which == 0,
            sources[0][form],
            jnp.where(
                which == 1, sources[1][form], jnp.where(which == 2, sources[2][form], sources[3][form])
            ),
        )
        passed.append(jnp.where(used, index, -1))
    sources = frame_sources(entries, f, y, x, others, here, step, side, cells)
    near, far = two_sides(sources)
    which = jnp.where(second, far, near)
    return passed[0], passed[1], jnp.where(used, which * (cells + 2) + step + 1, -1)


def plan_kernel(side, cells, place_ref, adjacency_ref, plan_ref):
    f = place_ref[0]
    entries = [
        (adjacency_ref[f * 12 + 3 * edge + 1], adjacency_ref[f * 12 + 3 * edge + 2])
        for edge in range(4)
    ]
    arrays = plan_arrays(entries, f, place_ref[1], place_ref[2], side, cells)
    for k, array in enumerate(arrays):
        plan_ref[k] = array


def plan_of(place, adjacency, side, cells):
    return pl.pallas_call(
        functools.partial(plan_kernel, side, cells),
        out_shape=jax.ShapeDtypeStruct((3, side, 128), jnp.int32),
        in_specs=[pl.BlockSpec(memory_space=pltpu.SMEM)] * 2,
        out_specs=pl.BlockSpec(memory_space=pltpu.VMEM),
        compiler_params=pltpu.CompilerParams(vmem_limit_bytes=4 * 1024 * 1024),
        name="plan",
    )(place, adjacency.reshape(-1))


def picked(wanted, held):
    chosen = (wanted.reshape(-1, 1) == jnp.arange(held.shape[0], dtype=jnp.int32)).astype(BF)
    cells = jnp.dot(chosen, held, preferred_element_type=F32).astype(BF)
    return cells.reshape(wanted.shape + held.shape[1:])


def on_device(
    fields,
    conv_kernel,
    conv_bias,
    norm_gain,
    norm_bias,
    expand_weight,
    expand_bias,
    reduce_weight,
    reduce_bias,
    adjacency,
    out_grad,
):
    tile = fields[0]
    cells = tile.shape[0]
    channels = tile.shape[2]
    hid = expand_weight.shape[1]
    side = lax.axis_size("row")
    width = side * cells
    rim = cells + 2
    cut = math.isqrt(side)
    f = lax.axis_index("face")
    r = lax.axis_index("row")
    c = lax.axis_index("col")
    y, x = r // cut, c % cut
    planes, lines = device_groups(side)
    place = jnp.stack([f, r, c]).astype(jnp.int32)
    few = -(-(13 + hid // channels) // (2 * side))
    extra = 8
    assert 2 * few <= 4 and cells & (cells - 1) == 0 and cut & (cut - 1) == 0

    plan = plan_of(place, adjacency, side, cells)
    inner_wanted = plan[0, :, : 2 * cells + 4]
    end_wanted = plan[1, :, : 2 * cells + extra]
    frame_rows = jnp.arange(4 * rim, dtype=jnp.int32)[:, None]

    def frame_of(strips):
        depth = strips.shape[1]
        arrival = plan[2, :, :depth].reshape(1, -1)
        flat = strips.reshape(-1, channels)
        gather_frame = (frame_rows == arrival).astype(BF)
        return jnp.dot(gather_frame, flat, preferred_element_type=F32).reshape(4, rim, channels)

    def direct(strips, frame):
        base = f * side + y * cut
        west = at(strips, base + jnp.maximum(x - 1, 0)).astype(F32)
        east = at(strips, base + jnp.minimum(x + 1, cut - 1)).astype(F32)
        return jnp.where(x == 0, frame[2], west), jnp.where(x == cut - 1, frame[3], east)

    got = swap(edges_of(place, tile, 2 * side), planes)
    passed = picked(inner_wanted, got.reshape(-1, channels))
    passed = swap(passed.reshape(side, -1, 4, channels), lines)
    frame = frame_of(passed.reshape(side, 2 * cells + 4, channels))
    west, east = direct(got[:, :cells], frame[:, 1:-1])
    ends = frame[2:, ::rim - 1]
    top = jnp.concatenate(
        [frame[0, :1] + ends[0, :1], frame[0, 1:-1], frame[0, -1:] + ends[1, :1]]
    ).astype(BF)
    bottom = jnp.concatenate(
        [frame[1, :1] + ends[0, 1:], frame[1, 1:-1], frame[1, -1:] + ends[1, 1:]]
    ).astype(BF)
    padded = jnp.concatenate(
        [
            top[None],
            jnp.concatenate([west.astype(BF)[:, None], tile, east.astype(BF)[:, None]], axis=1),
            bottom[None],
        ]
    )

    many = 2 * hid // (2 * side)
    grad_cells = out_grad[0].reshape(cells * cells, channels)
    grad_hidden = lax.dot_general(
        grad_cells, reduce_weight, (((1,), (1,)), ((), ())), preferred_element_type=F32
    )
    hidden, sent, base_grad = block_on_tile(
        place,
        padded,
        out_grad[0],
        grad_hidden,
        conv_kernel.reshape(9, channels),
        conv_bias.reshape(1, channels),
        norm_gain.reshape(1, channels),
        norm_bias.reshape(1, channels),
        expand_weight,
        expand_bias.reshape(1, hid),
        2 * side,
        many + 2 * cells + extra,
    )
    block_out = (
        tile.reshape(cells * cells, channels).astype(F32)
        + jnp.dot(hidden, reduce_weight, preferred_element_type=F32)
        + reduce_bias
    ).astype(BF)
    got = swap(sent, planes)

    def pairs(small):
        high = small.astype(BF)
        low = (small - high.astype(F32)).astype(BF)
        return jnp.stack([high, low], axis=-2).reshape(2 * few, channels)

    def small_total(rest):
        sums = jnp.sum(rest.astype(F32), axis=0).reshape(few, 2, channels)
        return sums[:, 0] + sums[:, 1]

    spare = many + 2 * cells + 4
    weights = jnp.sum(got[:, :many].astype(F32), axis=0)
    small = small_total(got[:, spare : spare + 2 * few])
    strips = got[:, many:]
    passed = picked(end_wanted, strips.reshape(-1, channels))
    tail = jnp.pad(pairs(small), ((0, 4 - 2 * few), (0, 0)))
    sent = jnp.concatenate(
        [
            jnp.broadcast_to(weights.astype(BF), (side, many, channels)),
            passed[:, : 2 * cells],
            jnp.concatenate(
                [passed[:, 2 * cells : 2 * cells + 4], jnp.broadcast_to(tail, (side, 4, channels))],
                axis=1,
            ),
        ],
        axis=1,
    )
    got = swap(sent, lines)
    share = share_of(got, 2 * side, many, few, 1.0 / width)
    spread = swap(share.reshape(2 * side, -1, 2, channels), planes).reshape(share.shape)

    frame = frame_of(got[:, many:])
    folded = frame[:, 1:-1]
    folded = folded.at[:, 0].add(frame[:, 0]).at[:, -1].add(frame[:, -1])
    west, east = direct(strips[:, :cells], folded)
    in_grad = base_grad
    in_grad = in_grad + jnp.pad(folded[:1], ((0, cells - 1), (0, 0), (0, 0)))
    in_grad = in_grad + jnp.pad(folded[1:2], ((cells - 1, 0), (0, 0), (0, 0)))
    in_grad = in_grad + jnp.pad(west[:, None], ((0, 0), (0, cells - 1), (0, 0)))
    in_grad = in_grad + jnp.pad(east[:, None], ((0, 0), (cells - 1, 0), (0, 0)))

    taps, bias, gain, shift, expand, expand_vector, reduce, reduce_vector = finish(spread, hid, many, few)
    return (
        block_out.reshape(1, cells, cells, channels),
        in_grad.astype(BF)[None],
        taps,
        bias.reshape(channels),
        gain.reshape(channels),
        shift.reshape(channels),
        expand,
        expand_vector.reshape(hid),
        reduce,
        reduce_vector.reshape(channels),
    )


def solution(mesh):
    tiles = P("face", "row", "col", None)
    in_specs = (tiles,) + (P(),) * 9 + (tiles,)
    out_specs = (tiles, tiles) + (P(),) * 8
    return jax.shard_map(
        on_device, mesh=mesh, in_specs=in_specs, out_specs=out_specs, check_vma=False
    )
```

```python
import functools
import math

import jax
import jax.numpy as jnp
from jax import lax
from jax.experimental import pallas as pl
from jax.experimental.pallas import tpu as pltpu
from jax.sharding import PartitionSpec as P

GELU_SCALE = math.sqrt(2.0 / math.pi)
NORM_EPS = 1e-06
BF = jnp.bfloat16
F32 = jnp.float32


def gelu_pair(preact):
    cubic_term = preact + 0.044715 * preact * preact * preact
    tangent = jnp.tanh(GELU_SCALE * cubic_term)
    gelu_value = 0.5 * preact * (1.0 + tangent)
    gelu_slope = 0.5 * (1.0 + tangent) + 0.5 * preact * (1.0 - tangent * tangent) * GELU_SCALE * (
        1.0 + 3.0 * 0.044715 * preact * preact
    )
    return (gelu_value, gelu_slope)


def slot_strips(face, row, col, slot, side, north, south, west, east):
    cut = math.isqrt(side)
    here_y, here_x = row // cut, col % cut
    same = face == slot // side
    y, x = slot % side // cut, slot % cut
    level = jnp.where(
        x == (here_x + cut - 1) % cut, west, jnp.where(x == (here_x + 1) % cut, east, north)
    )
    inner = jnp.where(y < here_y, north, jnp.where(y > here_y, south, level))
    near = jnp.where(same, inner, jnp.where(row == 0, north, south))
    far = jnp.where(same, south, jnp.where(col == 0, west, east))
    return near, far


def edges_kernel(place_ref, tile_ref, sent_ref):
    slots, depth, _ = sent_ref.shape
    rows = depth // 2
    tile = tile_ref[...].astype(F32)
    north, south = tile[0], tile[rows - 1]
    west = jnp.concatenate([tile[k, 0:1] for k in range(rows)])
    east = jnp.concatenate([tile[k, rows - 1 : rows] for k in range(rows)])
    for slot in range(slots):
        near, far = slot_strips(
            place_ref[0], place_ref[1], place_ref[2], slot, slots // 2, north, south, west, east
        )
        sent_ref[slot, 0:rows] = near.astype(BF)
        sent_ref[slot, rows:depth] = far.astype(BF)


def edges_of(place, tile, slots):
    rows, _, channels = tile.shape
    return pl.pallas_call(
        edges_kernel,
        out_shape=jax.ShapeDtypeStruct((slots, 2 * rows, channels), BF),
        in_specs=[
            pl.BlockSpec(memory_space=pltpu.SMEM),
            pl.BlockSpec(memory_space=pltpu.VMEM),
        ],
        out_specs=pl.BlockSpec(memory_space=pltpu.VMEM),
        compiler_params=pltpu.CompilerParams(vmem_limit_bytes=8 * 1024 * 1024),
        name="edges",
    )(place, tile)


def block_kernel(
    plan_ref,
    padded_ref,
    grad_ref,
    grad_hidden_ref,
    tap_ref,
    conv_bias_ref,
    gain_ref,
    shift_ref,
    expand_ref,
    expand_bias_ref,
    hidden_ref,
    sent_ref,
    base_ref,
    wide_ref,
):
    rows, columns, channels = grad_ref.shape
    count = rows * columns
    rim = rows + 2
    hid = expand_ref.shape[1]
    slots, _, _ = sent_ref.shape
    side = slots // 2
    padded = padded_ref[...].astype(F32)
    shifted = [padded[:, b : b + columns] for b in range(3)]

    mixed = jnp.zeros((rows, columns, channels), F32) + conv_bias_ref[...].reshape(1, 1, channels)
    for a in range(3):
        for b in range(3):
            mixed = mixed + tap_ref[3 * a + b].reshape(1, 1, channels) * shifted[b][a : a + rows]
    mixed = mixed.reshape(count, channels)
    center = mixed - jnp.mean(mixed, axis=-1, keepdims=True)
    inv_std = lax.rsqrt(jnp.mean(center * center, axis=-1, keepdims=True) + NORM_EPS)
    normalized = center * inv_std
    normed = (normalized * gain_ref[...] + shift_ref[...]).astype(BF)
    preact = jnp.dot(normed, expand_ref[...], preferred_element_type=F32) + expand_bias_ref[...]
    gelu_value, gelu_slope = gelu_pair(preact)
    hidden = gelu_value.astype(BF)
    hidden_ref[...] = hidden
    grad_cells = grad_ref[...].reshape(count, channels)
    grad_preact = (grad_hidden_ref[...] * gelu_slope).astype(BF)
    grad_normed = lax.dot_general(
        grad_preact, expand_ref[...], (((1,), (1,)), ((), ())), preferred_element_type=F32
    )
    scaled = grad_normed * gain_ref[...]
    grad_mixed = inv_std * (
        scaled
        - jnp.mean(scaled, axis=-1, keepdims=True)
        - normalized * jnp.mean(scaled * normalized, axis=-1, keepdims=True)
    )

    def total(cells):
        return jnp.sum(cells, axis=0, keepdims=True)

    square = grad_mixed.reshape(rows, columns, channels)
    small = [
        total((square * shifted[b][a : a + rows]).reshape(count, channels))
        for a in range(3)
        for b in range(3)
    ]
    small += [total(grad_mixed), total(grad_normed * normalized), total(grad_normed)]
    preact_total = total(grad_preact.astype(F32))
    small += [preact_total[:, k : k + channels] for k in range(0, hid, channels)]
    small += [total(grad_cells.astype(F32))]

    across = (((0,), (0,)), ((), ()))
    expand_sum = lax.dot_general(normed, grad_preact, across, preferred_element_type=F32).astype(BF)
    reduce_sum = lax.dot_general(hidden, grad_cells, across, preferred_element_type=F32).astype(BF)
    many = 2 * hid // slots
    for k in range(0, hid, channels):
        for j in range(0, channels, many):
            sent_ref[(k + j) // many, 0:many] = expand_sum[j : j + many, k : k + channels]
    for k in range(0, hid, many):
        sent_ref[(hid + k) // many, 0:many] = reduce_sum[k : k + many]

    wide_ref[...] = jnp.zeros(wide_ref.shape, F32)
    for b in range(3):
        parts = [tap_ref[3 * a + b].reshape(1, 1, channels) * square for a in range(3)]
        wide_ref[0, b : b + columns] += parts[0][0]
        wide_ref[1, b : b + columns] += parts[0][1] + parts[1][0]
        wide_ref[2:rows, b : b + columns] += (
            parts[0][2:] + parts[1][1 : rows - 1] + parts[2][: rows - 2]
        )
        wide_ref[rows, b : b + columns] += parts[1][rows - 1] + parts[2][rows - 2]
        wide_ref[rows + 1, b : b + columns] += parts[2][rows - 1]
    base_ref[...] = grad_ref[...].astype(F32) + wide_ref[1 : rows + 1, 1 : columns + 1]
    west = jnp.concatenate([wide_ref[k, 0:1] for k in range(rim)])
    east = jnp.concatenate([wide_ref[k, rim - 1 : rim] for k in range(rim)])
    north = wide_ref[0, 0:rim]
    south = wide_ref[rim - 1, 0:rim]

    face, row, col = plan_ref[0], plan_ref[1], plan_ref[2]
    few = -(-len(small) // slots)
    extra = sent_ref.shape[1] - many - 2 * rows
    place = lax.broadcasted_iota(jnp.int32, (extra, channels), 0)
    near = many + rows
    for slot in range(slots):
        strip, side_strip = slot_strips(face, row, col, slot, side, north, south, west, east)
        sent_ref[slot, many:near] = strip[1 : rim - 1].astype(BF)
        sent_ref[slot, near : near + rows] = side_strip[1 : rim - 1].astype(BF)
        ends = [strip[0:1], strip[rim - 1 : rim], side_strip[0:1], side_strip[rim - 1 : rim]]
        values = ends
        for k in range(few * slot, min(few * slot + few, len(small))):
            high = small[k].astype(BF).astype(F32)
            values = values + [high, small[k] - high]
        block = jnp.zeros((extra, channels), F32)
        for k, value in enumerate(values):
            block = jnp.where(place == k, value, block)
        sent_ref[slot, near + rows : near + rows + extra] = block.astype(BF)


def block_on_tile(place, padded, grad, grad_hidden, *params):
    rows, columns, channels = grad.shape
    slots, depth = params[-2:]
    return pl.pallas_call(
        block_kernel,
        out_shape=(
            jax.ShapeDtypeStruct(grad_hidden.shape, BF),
            jax.ShapeDtypeStruct((slots, depth, channels), BF),
            jax.ShapeDtypeStruct(grad.shape, F32),
        ),
        in_specs=[pl.BlockSpec(memory_space=pltpu.SMEM)]
        + [pl.BlockSpec(memory_space=pltpu.VMEM)] * 9,
        out_specs=(pl.BlockSpec(memory_space=pltpu.VMEM),) * 3,
        scratch_shapes=[pltpu.VMEM((rows + 2, columns + 8, channels), F32)],
        compiler_params=pltpu.CompilerParams(vmem_limit_bytes=24 * 1024 * 1024),
        name="block",
    )(place, padded, grad, grad_hidden, *params[:-2])


def share_kernel(scale, few, many, got_ref, share_ref):
    total, channels = share_ref.shape
    spare = got_ref.shape[1] - 4
    weights = jnp.zeros((many, channels), F32)
    rest = jnp.zeros((4, channels), F32)
    for k in range(got_ref.shape[0]):
        weights = weights + got_ref[k, 0:many].astype(F32)
        rest = rest + got_ref[k, spare - 4 : spare + 4].astype(F32)[4:8]
    parts = [weights * scale]
    for k in range(few):
        small = (rest[2 * k : 2 * k + 1] + rest[2 * k + 1 : 2 * k + 2]) * scale
        high = small.astype(BF).astype(F32)
        parts += [high, small - high]
    block = jnp.concatenate(parts * 8).astype(BF)
    depth = block.shape[0]
    for k in range(0, total, depth):
        share_ref[k : k + depth] = block


def share_of(got, slots, many, few, scale):
    channels = got.shape[2]
    return pl.pallas_call(
        functools.partial(share_kernel, scale, few, many),
        out_shape=jax.ShapeDtypeStruct((slots * (many + 2 * few), channels), BF),
        in_specs=[pl.BlockSpec(memory_space=pltpu.VMEM)],
        out_specs=pl.BlockSpec(memory_space=pltpu.VMEM),
        compiler_params=pltpu.CompilerParams(vmem_limit_bytes=8 * 1024 * 1024),
        name="share",
    )(got)


def finish_kernel(many, few, got_ref, *out_refs):
    tap_ref, bias_ref, gain_ref, shift_ref, expand_ref, expand_bias_ref, reduce_ref, reduce_bias_ref = (
        out_refs
    )
    total, channels = got_ref.shape
    hid = reduce_ref.shape[0]
    depth = many + 2 * few
    small = []
    for start in range(0, total, 8 * depth):
        block = got_ref[start : start + 8 * depth].astype(F32)
        for k in range(8):
            slot = start // depth + k
            part = block[k * depth : (k + 1) * depth]
            row = slot * many
            if row < hid:
                lane, row = row // channels * channels, row % channels
                expand_ref[row : row + many, lane : lane + channels] = part[:many]
            else:
                reduce_ref[row - hid : row - hid + many] = part[:many]
            rest = part[many:]
            small += [rest[2 * k : 2 * k + 1] + rest[2 * k + 1 : 2 * k + 2] for k in range(few)]
    blocks = hid // channels
    for k in range(9):
        tap_ref[k // 3, k % 3 : k % 3 + 1] = small[k]
    bias_ref[...] = small[9]
    gain_ref[...] = small[10]
    shift_ref[...] = small[11]
    for k in range(blocks):
        expand_bias_ref[:, k * channels : (k + 1) * channels] = small[12 + k]
    reduce_bias_ref[...] = small[12 + blocks]


def finish(got, hid, many, few):
    channels = got.shape[1]
    shapes = [(3, 3, channels)] + [(1, channels)] * 3
    shapes += [(channels, hid), (1, hid), (hid, channels), (1, channels)]
    return pl.pallas_call(
        functools.partial(finish_kernel, many, few),
        out_shape=tuple(jax.ShapeDtypeStruct(shape, F32) for shape in shapes),
        in_specs=[pl.BlockSpec(memory_space=pltpu.VMEM)],
        out_specs=(pl.BlockSpec(memory_space=pltpu.VMEM),) * len(shapes),
        compiler_params=pltpu.CompilerParams(vmem_limit_bytes=16 * 1024 * 1024),
        name="finish",
    )(got)


def swap(slots, groups):
    return lax.all_to_all(slots, ("face", "row", "col"), 0, 0, axis_index_groups=groups)


def at(slots, index):
    return lax.dynamic_index_in_dim(slots, index, 0, keepdims=False)


def device_groups(side):
    cut = math.isqrt(side)
    steps = range(cut)

    def device(f, y, x, high, low):
        return (f * side + y * cut + low) * side + high * cut + x

    planes = [
        [device(f, y, x, high, low) for f in range(2) for y in steps for x in steps]
        for high in steps
        for low in steps
    ]
    lines = [
        [device(f, y, x, (high + f * cut // 2) % cut, low) for high in steps for low in steps]
        for f in range(2)
        for y in steps
        for x in steps
    ]
    return planes, lines


def frame_sources(entries, f, y, x, sender, target, step, side, cells):
    cut = math.isqrt(side)
    last, width, low_bits, cell_bits = side - 1, side * cells, cut - 1, cells - 1
    shift, cell_shift = low_bits.bit_length(), cell_bits.bit_length()
    high, low = sender >> shift, sender & low_bits
    row, col = y * cut + (target & low_bits), (target >> shift) * cut + x
    virtual = (step < 0) | (step >= cells)

    def held(face, tile_row, tile_col, part, cell, valid):
        valid = valid & ((tile_row & low_bits) == low) & ((tile_col >> shift) == high)
        slot = face * side + ((tile_row >> shift) << shift) + (tile_col & low_bits)
        inner = part * cells + cell
        end = 2 * cells + 2 * part + jnp.where(cell == 0, 0, 1)
        inner_index = slot * (2 * cells) + inner
        end_index = slot * (2 * cells + 8) + jnp.where(virtual, end, inner)
        return jnp.where(valid, inner_index, -1), jnp.where(valid, end_index, -1)

    def glued(edge, along, on_rows):
        other_edge, reverse = entries[edge]
        position = along * cells + step
        turned = jnp.where(reverse == 1, width - 1 - position, position)
        valid = (position >= 0) & (position < width)
        tile, cell = turned >> cell_shift, turned & cell_bits
        if on_rows:
            end = jnp.where(other_edge == 2, 0, last)
            return held(1 - f, tile, end, 1, cell, valid)
        end = jnp.where(other_edge == 0, 0, last)
        return held(1 - f, end, tile, 0, cell, valid)

    def beside(next_row, far_cell, own_part):
        position = col * cells + step
        valid = (position >= 0) & (position < width)
        tile, cell = position >> cell_shift, position & cell_bits
        level = (next_row >> shift) == y
        part = jnp.where(level & (step >= 0) & (step < cells), own_part, 0)
        cell = jnp.where(level & virtual, far_cell, cell)
        return held(f, next_row, tile, part, cell, valid)

    def either(condition, first, second):
        return tuple(jnp.where(condition, p, q) for p, q in zip(first, second))

    inner = (step >= 0) & (step < cells)
    nothing = (-1, -1)
    top = either(row == 0, glued(0, col, True), beside(row - 1, cells - 1, 1))
    bottom = either(row == last, glued(1, col, True), beside(row + 1, 0, 0))
    west = either(col == 0, glued(2, row, False), held(f, row, col - 1, 0, step, inner))
    east = either(col == last, glued(3, row, False), held(f, row, col + 1, 0, step, inner))
    return [top, bottom, either(x == 0, west, nothing), either(x == cut - 1, east, nothing)]


def two_sides(sources):
    need = [jnp.max(source[1].astype(F32), axis=-1, keepdims=True) >= 0.0 for source in sources]
    near = jnp.where(need[0], 0, jnp.where(need[1], 1, jnp.where(need[2], 2, 3)))
    after_one = jnp.where(need[2], 2, 3)
    far = jnp.where(
        need[0], jnp.where(need[1], 1, after_one), jnp.where(need[1], after_one, jnp.where(need[2], 3, 2))
    )
    return near, far


def plan_arrays(entries, f, r, c, side, cells):
    cut = math.isqrt(side)
    y, x = r // cut, c % cut
    here = c // cut * cut + r % cut
    others = lax.broadcasted_iota(jnp.int32, (side, 128), 0)
    others = (others + f * (side // 2)) & (side - 1)
    lane = lax.broadcasted_iota(jnp.int32, (side, 128), 1)
    main = lane < 2 * cells
    step = jnp.where(main, lane & (cells - 1), jnp.where((lane & 1) == 0, -1, cells))
    second = jnp.where(main, lane - cells, lane - 2 * cells - 2) >= 0
    used = lane < 2 * cells + 4
    sources = frame_sources(entries, f, y, x, here, others, step, side, cells)
    near, far = two_sides(sources)
    which = jnp.where(second, far, near)
    passed = []
    for form in range(2):
        index = jnp.where(
            which == 0,
            sources[0][form],
            jnp.where(
                which == 1, sources[1][form], jnp.where(which == 2, sources[2][form], sources[3][form])
            ),
        )
        passed.append(jnp.where(used, index, -1))
    sources = frame_sources(entries, f, y, x, others, here, step, side, cells)
    near, far = two_sides(sources)
    which = jnp.where(second, far, near)
    return passed[0], passed[1], jnp.where(used, which * (cells + 2) + step + 1, -1)


def plan_kernel(side, cells, place_ref, adjacency_ref, plan_ref):
    f = place_ref[0]
    entries = [
        (adjacency_ref[f * 12 + 3 * edge + 1], adjacency_ref[f * 12 + 3 * edge + 2])
        for edge in range(4)
    ]
    arrays = plan_arrays(entries, f, place_ref[1], place_ref[2], side, cells)
    for k, array in enumerate(arrays):
        plan_ref[k] = array


def plan_of(place, adjacency, side, cells):
    return pl.pallas_call(
        functools.partial(plan_kernel, side, cells),
        out_shape=jax.ShapeDtypeStruct((3, side, 128), jnp.int32),
        in_specs=[pl.BlockSpec(memory_space=pltpu.SMEM)] * 2,
        out_specs=pl.BlockSpec(memory_space=pltpu.VMEM),
        compiler_params=pltpu.CompilerParams(vmem_limit_bytes=4 * 1024 * 1024),
        name="plan",
    )(place, adjacency.reshape(-1))


def picked(wanted, held):
    chosen = (wanted.reshape(-1, 1) == jnp.arange(held.shape[0], dtype=jnp.int32)).astype(BF)
    cells = jnp.dot(chosen, held, preferred_element_type=F32).astype(BF)
    return cells.reshape(wanted.shape + held.shape[1:])


def on_device(
    fields,
    conv_kernel,
    conv_bias,
    norm_gain,
    norm_bias,
    expand_weight,
    expand_bias,
    reduce_weight,
    reduce_bias,
    adjacency,
    out_grad,
):
    tile = fields[0]
    cells = tile.shape[0]
    channels = tile.shape[2]
    hid = expand_weight.shape[1]
    side = lax.axis_size("row")
    width = side * cells
    rim = cells + 2
    cut = math.isqrt(side)
    f = lax.axis_index("face")
    r = lax.axis_index("row")
    c = lax.axis_index("col")
    y, x = r // cut, c % cut
    planes, lines = device_groups(side)
    place = jnp.stack([f, r, c]).astype(jnp.int32)
    few = -(-(13 + hid // channels) // (2 * side))
    extra = 8
    assert 2 * few <= 4 and cells & (cells - 1) == 0 and cut & (cut - 1) == 0

    plan = plan_of(place, adjacency, side, cells)
    inner_wanted = plan[0, :, : 2 * cells + 4]
    end_wanted = plan[1, :, : 2 * cells + extra]
    frame_rows = jnp.arange(4 * rim, dtype=jnp.int32)[:, None]

    def frame_of(strips):
        depth = strips.shape[1]
        arrival = plan[2, :, :depth].reshape(1, -1)
        flat = strips.reshape(-1, channels)
        gather_frame = (frame_rows == arrival).astype(BF)
        return jnp.dot(gather_frame, flat, preferred_element_type=F32).reshape(4, rim, channels)

    def direct(strips, frame):
        base = f * side + y * cut
        west = at(strips, base + jnp.maximum(x - 1, 0)).astype(F32)
        east = at(strips, base + jnp.minimum(x + 1, cut - 1)).astype(F32)
        return jnp.where(x == 0, frame[2], west), jnp.where(x == cut - 1, frame[3], east)

    got = swap(edges_of(place, tile, 2 * side), planes)
    passed = picked(inner_wanted, got.reshape(-1, channels))
    passed = swap(passed.reshape(side, -1, 4, channels), lines)
    frame = frame_of(passed.reshape(side, 2 * cells + 4, channels))
    west, east = direct(got[:, :cells], frame[:, 1:-1])
    ends = frame[2:, ::rim - 1]
    top = jnp.concatenate(
        [frame[0, :1] + ends[0, :1], frame[0, 1:-1], frame[0, -1:] + ends[1, :1]]
    ).astype(BF)
    bottom = jnp.concatenate(
        [frame[1, :1] + ends[0, 1:], frame[1, 1:-1], frame[1, -1:] + ends[1, 1:]]
    ).astype(BF)
    padded = jnp.concatenate(
        [
            top[None],
            jnp.concatenate([west.astype(BF)[:, None], tile, east.astype(BF)[:, None]], axis=1),
            bottom[None],
        ]
    )

    many = 2 * hid // (2 * side)
    grad_cells = out_grad[0].reshape(cells * cells, channels)
    grad_hidden = lax.dot_general(
        grad_cells, reduce_weight, (((1,), (1,)), ((), ())), preferred_element_type=F32
    )
    hidden, sent, base_grad = block_on_tile(
        place,
        padded,
        out_grad[0],
        grad_hidden,
        conv_kernel.reshape(9, channels),
        conv_bias.reshape(1, channels),
        norm_gain.reshape(1, channels),
        norm_bias.reshape(1, channels),
        expand_weight,
        expand_bias.reshape(1, hid),
        2 * side,
        many + 2 * cells + extra,
    )
    block_out = (
        tile.reshape(cells * cells, channels).astype(F32)
        + jnp.dot(hidden, reduce_weight, preferred_element_type=F32)
        + reduce_bias
    ).astype(BF)
    got = swap(sent, planes)

    def pairs(small):
        high = small.astype(BF)
        low = (small - high.astype(F32)).astype(BF)
        return jnp.stack([high, low], axis=-2).reshape(2 * few, channels)

    def small_total(rest):
        sums = jnp.sum(rest.astype(F32), axis=0).reshape(few, 2, channels)
        return sums[:, 0] + sums[:, 1]

    spare = many + 2 * cells + 4
    weights = jnp.sum(got[:, :many].astype(F32), axis=0)
    small = small_total(got[:, spare : spare + 2 * few])
    strips = got[:, many:]
    passed = picked(end_wanted, strips.reshape(-1, channels))
    tail = jnp.pad(pairs(small), ((0, 4 - 2 * few), (0, 0)))
    sent = jnp.concatenate(
        [
            jnp.broadcast_to(weights.astype(BF), (side, many, channels)),
            passed[:, : 2 * cells],
            jnp.concatenate(
                [passed[:, 2 * cells : 2 * cells + 4], jnp.broadcast_to(tail, (side, 4, channels))],
                axis=1,
            ),
        ],
        axis=1,
    )
    got = swap(sent, lines)
    share = share_of(got, 2 * side, many, few, 1.0 / width)
    spread = swap(share.reshape(2 * side, -1, 2, channels), planes).reshape(share.shape)

    frame = frame_of(got[:, many:])
    folded = frame[:, 1:-1]
    folded = folded.at[:, 0].add(frame[:, 0]).at[:, -1].add(frame[:, -1])
    west, east = direct(strips[:, :cells], folded)
    in_grad = base_grad
    in_grad = in_grad + jnp.pad(folded[:1], ((0, cells - 1), (0, 0), (0, 0)))
    in_grad = in_grad + jnp.pad(folded[1:2], ((cells - 1, 0), (0, 0), (0, 0)))
    in_grad = in_grad + jnp.pad(west[:, None], ((0, 0), (0, cells - 1), (0, 0)))
    in_grad = in_grad + jnp.pad(east[:, None], ((0, 0), (cells - 1, 0), (0, 0)))

    taps, bias, gain, shift, expand, expand_vector, reduce, reduce_vector = finish(spread, hid, many, few)
    return (
        block_out.reshape(1, cells, cells, channels),
        in_grad.astype(BF)[None],
        taps,
        bias.reshape(channels),
        gain.reshape(channels),
        shift.reshape(channels),
        expand,
        expand_vector.reshape(hid),
        reduce,
        reduce_vector.reshape(channels),
    )


def solution(mesh):
    tiles = P("face", "row", "col", None)
    in_specs = (tiles,) + (P(),) * 9 + (tiles,)
    out_specs = (tiles, tiles) + (P(),) * 8
    return jax.shard_map(
        on_device, mesh=mesh, in_specs=in_specs, out_specs=out_specs, check_vma=False
    )
```
